256 devices in a mesh: leaf: 64 (over z, x, core), cols: 4 (over y).
Axes of the slice: x: 4, y: 4, z: 8, core: 2. Of those that a mesh axis runs over, the one named last changes fastest.
Arguments:
- points: bfloat16 [131072, 256], P('leaf')
- weights: bfloat16 [131072, 512], P('leaf', 'cols'), may hold values from -0.1796875 to 0.1796875
- leaf_basis: bfloat16 [512, 256, 128], P('leaf'), may hold values from -0.375 to 0.375
- leaf_transfer: bfloat16 [512, 128, 128], P('leaf'), may hold values from -0.25 to 0.25
- node_transfer: bfloat16 [128, 128, 128], P('leaf'), may hold values from -0.25 to 0.25
- leaf_skeleton: int32 [512, 128], P('leaf'), may hold values from 0 to 255, as said below
- node_skeleton: int32 [128, 128], P('leaf'), may hold values from 0 to 511, as said below
- upper_skeleton: int32 [32, 128], replicated, may hold values from 0 to 511, as said below
- leaf_far: int32 [512, 12], P('leaf'), may hold values from 0 to 511, as said below
- leaf_count: int32 [512], P('leaf'), may hold values from 1 to 12
- node_far: int32 [128, 12], P('leaf'), may hold values from 0 to 127, as said below
- node_count: int32 [128], P('leaf'), may hold values from 1 to 8
- upper_far: int32 [32, 12], replicated, may hold values from 0 to 31, as said below
- upper_count: int32 [32], replicated, may hold values from 1 to 2
Outputs:
- potentials: bfloat16 [131072, 512], P('leaf', 'cols')
The draws below stay inside these ranges and needn't reach their ends.
Inputs may be any that keep to these rules, and one draw needn't show every extreme that they name: `leaf_skeleton`: each row holds 128 different positions. `node_skeleton`: each row holds 128 different positions. `upper_skeleton`: each row holds 128 different positions. `leaf_far`: entries of row t are (t + e) mod 512 with 1 <= |e| <= 8; the used entries of a row are different. `node_far`: entries of row t are (t + e) mod 128 with 1 <= |e| <= 4; the used entries of a row are different. `upper_far`: entries of row t are (t + 1) or (t - 1) mod 32; the used entries of a row are different.
All inputs are finite; a program needn't handle non-finite values.
Results may differ from the reference program's by a relative error of at most 0.009.
Values may be sent and summed in bfloat16 or wider, within the bound.
No kernel may reach another device: no remote copies, remote signals or barrier semaphores. Data moves between devices by JAX's collectives and lax.ppermute only.
A program may use at most 128 MiB of HBM per device.

```python
import math
import jax
import jax.numpy as jnp
from jax import lax

F = 256
C = 512
R = 128
LEAF = 256
K_FAR = 12
LEAVES_DEV = 8
NODES = 128
LEAVES = 512
UPPER_NODES = 32
NPTS = 131072


def draw_points(key, part):
    key = jax.random.fold_in(key, 11)
    values = jnp.clip(jax.random.normal(key, (NPTS, F), jnp.float32), -4.0, 4.0)
    return values.astype(jnp.bfloat16)


def skeleton_sets(key, rows, choices_count):
    scores = jax.random.randint(key, (rows, choices_count), 0, 1 << 16) * choices_count
    scores = scores + jnp.arange(choices_count, dtype=jnp.int32)[None, :]
    return jnp.argsort(scores, axis=1)[:, :R].astype(jnp.int32)


def far_lists(key, rows, reach):
    span_count = 2 * reach
    position = jnp.arange(span_count, dtype=jnp.int32)
    offset_table = jnp.where(position < reach, position - reach, position - reach + 1)
    scores = jax.random.randint(key, (rows, span_count), 0, 1 << 16) * span_count
    scores = scores + position[None, :]
    order = jnp.argsort(scores, axis=1).astype(jnp.int32)
    offsets = offset_table[order]
    column_ids = jnp.arange(K_FAR, dtype=jnp.int32) % span_count
    offsets = offsets[:, column_ids]
    targets = jnp.arange(rows, dtype=jnp.int32)[:, None] + offsets
    return jnp.mod(targets, rows).astype(jnp.int32)


def slot_counts(key, rows, most):
    first_key, second_key = jax.random.split(key)
    counts = jax.random.randint(first_key, (rows,), 1, most + 1)
    position = jax.random.randint(second_key, (), 0, rows)
    return counts.at[position].set(most).astype(jnp.int32)


def draw_leaf_skeleton(key, part):
    key = jax.random.fold_in(key, 21)
    return skeleton_sets(key, LEAVES, LEAF)


def draw_node_skeleton(key, part):
    key = jax.random.fold_in(key, 22)
    return skeleton_sets(key, NODES, 4 * R)


def draw_upper_skeleton(key, part):
    key = jax.random.fold_in(key, 23)
    return skeleton_sets(key, UPPER_NODES, 4 * R)


def draw_leaf_far(key, part):
    key = jax.random.fold_in(key, 31)
    return far_lists(key, LEAVES, LEAVES_DEV)


def draw_node_far(key, part):
    key = jax.random.fold_in(key, 32)
    return far_lists(key, NODES, 4)


def draw_upper_far(key, part):
    key = jax.random.fold_in(key, 33)
    return far_lists(key, UPPER_NODES, 1)


def draw_leaf_count(key, part):
    key = jax.random.fold_in(key, 41)
    return slot_counts(key, LEAVES, min(K_FAR, 2 * LEAVES_DEV))


def draw_node_count(key, part):
    key = jax.random.fold_in(key, 42)
    return slot_counts(key, NODES, min(K_FAR, 8))


def draw_upper_count(key, part):
    key = jax.random.fold_in(key, 43)
    return slot_counts(key, UPPER_NODES, 2)


def level_of(stream_key, extent, shards, smallest, high):
    factor_of, own = 1.0, jax.random.fold_in(stream_key, 6)
    for axis_at, parts in shards:
        heights = jnp.exp(jax.random.uniform(jax.random.fold_in(own, axis_at), (parts,), jnp.float32, smallest / len(shards), high / len(shards)))
        factor_of = factor_of * jnp.repeat(heights, extent[axis_at] // parts).reshape([-1 if axis == axis_at else 1 for axis in range(len(extent))])
    return factor_of


def normal_values(rng, shape, scale, most, pieces=(), kind=jnp.bfloat16):
    entries = scale * jax.random.normal(rng, shape, jnp.float32)
    if pieces:
        entries = entries * level_of(rng, shape, pieces, -0.22, 0.18)
    return jnp.clip(entries, -most, most).astype(kind)


def setup_inputs(seed: int = 0) -> dict:
    keys = jax.random.split(jax.random.key(seed), 15)
    points = draw_points(jax.random.fold_in(keys[14], 71), 0)
    weights = normal_values(keys[1], (NPTS, C), 0.03, 0.1796875, ((0, 64), (1, 4)))
    leaf_basis = normal_values(keys[2], (LEAVES, LEAF, R), LEAF ** -0.5, 0.375, ((0, 64),))
    leaf_transfer = normal_values(keys[3], (LEAVES, R, R), (4 * R) ** -0.5, 0.25, ((0, 64),))
    node_transfer = normal_values(keys[4], (NODES, R, R), (4 * R) ** -0.5, 0.25, ((0, 64),))
    leaf_skeleton = draw_leaf_skeleton(jax.random.fold_in(keys[14], 71), 0)
    node_skeleton = draw_node_skeleton(jax.random.fold_in(keys[14], 71), 0)
    upper_skeleton = draw_upper_skeleton(jax.random.fold_in(keys[14], 71), 0)
    leaf_far = draw_leaf_far(jax.random.fold_in(keys[14], 71), 0)
    leaf_count = draw_leaf_count(jax.random.fold_in(keys[14], 71), 0)
    node_far = draw_node_far(jax.random.fold_in(keys[14], 71), 0)
    node_count = draw_node_count(jax.random.fold_in(keys[14], 71), 0)
    upper_far = draw_upper_far(jax.random.fold_in(keys[14], 71), 0)
    upper_count = draw_upper_count(jax.random.fold_in(keys[14], 71), 0)
    return {"points": points, "weights": weights, "leaf_basis": leaf_basis, "leaf_transfer": leaf_transfer, "node_transfer": node_transfer, "leaf_skeleton": leaf_skeleton, "node_skeleton": node_skeleton, "upper_skeleton": upper_skeleton, "leaf_far": leaf_far, "leaf_count": leaf_count, "node_far": node_far, "node_count": node_count, "upper_far": upper_far, "upper_count": upper_count}


def kernel_block(left_pts, right_pts):
    inner_prod = jnp.einsum('...af,...bf->...ab', left_pts.astype(jnp.float32), right_pts.astype(jnp.float32))
    left_sq = lax.optimization_barrier(jnp.sum(jnp.square(left_pts.astype(jnp.float32)), -1))
    right_sq = lax.optimization_barrier(jnp.sum(jnp.square(right_pts.astype(jnp.float32)), -1))
    distance = left_sq[..., :, None] + right_sq[..., None, :] - 2.0 * inner_prod
    features = left_pts.shape[-1]
    gamma_scale = 1.0 / math.sqrt(8.0 * features)
    return jnp.exp(gamma_scale * (2.0 * features - distance))

def far_level(all_pts, all_charges, far_list, live_counts):
    kslots = jnp.arange(K_FAR, dtype=jnp.int32)

    def one_node(operand):
        own_pts, far_row, far_count = operand
        blocks = kernel_block(own_pts[None], all_pts[far_row])
        live_mask = (kslots < far_count).astype(jnp.float32)
        blocks = (blocks * live_mask[:, None, None]).astype(jnp.bfloat16)
        return jnp.einsum('krs,ksc->rc', blocks.astype(jnp.float32), all_charges[far_row].astype(jnp.float32))
    return lax.map(one_node, (all_pts, far_list, live_counts))

def reference(points, weights, leaf_basis, leaf_transfer, node_transfer, leaf_skeleton, node_skeleton, upper_skeleton, leaf_far, leaf_count, node_far, node_count, upper_far, upper_count):
    leaf_points = points.reshape(LEAVES, LEAF, F)
    leaf_weights = weights.reshape(LEAVES, LEAF, C)
    no_self = 1.0 - jnp.eye(LEAF, dtype=jnp.float32)

    def near_one(operand):
        leaf_block, leaf_weight = operand
        tile_vals = (kernel_block(leaf_block, leaf_block) * no_self).astype(jnp.bfloat16)
        return jnp.dot(tile_vals, leaf_weight, preferred_element_type=jnp.float32)
    near_field = lax.map(near_one, (leaf_points, leaf_weights))
    charges = jnp.einsum('lpr,lpc->lrc', leaf_basis.astype(jnp.float32), leaf_weights.astype(jnp.float32)).astype(jnp.bfloat16)
    skel_pts = jnp.take_along_axis(leaf_points, leaf_skeleton[:, :, None], axis=1)
    leaf_pot = far_level(skel_pts, charges, leaf_far, leaf_count)
    node_q = jnp.einsum('nkrs,nkrc->nsc', leaf_transfer.reshape(NODES, 4, R, R).astype(jnp.float32), charges.reshape(NODES, 4, R, C).astype(jnp.float32)).astype(jnp.bfloat16)
    node_pts = jnp.take_along_axis(skel_pts.reshape(NODES, 4 * R, F), node_skeleton[:, :, None], axis=1)
    node_pot = far_level(node_pts, node_q, node_far, node_count)
    upper_q = jnp.einsum('nkrs,nkrc->nsc', node_transfer.reshape(UPPER_NODES, 4, R, R).astype(jnp.float32), node_q.reshape(UPPER_NODES, 4, R, C).astype(jnp.float32)).astype(jnp.bfloat16)
    upper_pts = jnp.take_along_axis(node_pts.reshape(UPPER_NODES, 4 * R, F), upper_skeleton[:, :, None], axis=1)
    upper_pot = far_level(upper_pts, upper_q, upper_far, upper_count)
    upper_down = upper_pot.astype(jnp.bfloat16)
    node_down = (node_pot + jnp.einsum('nrs,nsc->nrc', node_transfer.astype(jnp.float32), jnp.repeat(upper_down, 4, axis=0).astype(jnp.float32))).astype(jnp.bfloat16)
    leaf_down = (leaf_pot + jnp.einsum('lrs,lsc->lrc', leaf_transfer.astype(jnp.float32), jnp.repeat(node_down, 4, axis=0).astype(jnp.float32))).astype(jnp.bfloat16)
    result = near_field + jnp.einsum('lpr,lrc->lpc', leaf_basis.astype(jnp.float32), leaf_down.astype(jnp.float32))
    return result.reshape(NPTS, C).astype(jnp.bfloat16)
```

```python
import functools
import math

import jax
import jax.numpy as jnp
from jax import lax
from jax.experimental import pallas as pl
from jax.experimental.pallas import tpu as pltpu
from jax.sharding import PartitionSpec as P

NEG = -1e38
VMEM = pltpu.VMEM
SMEM = pltpu.SMEM
LIMIT = 48 * 1024 * 1024


def mm(a, b):
    return jnp.dot(a, b, preferred_element_type=jnp.float32)


def mm_nt(a, b):
    return lax.dot_general(a, b, (((1,), (1,)), ((), ())), preferred_element_type=jnp.float32)


def mm_tn(a, b):
    return lax.dot_general(a, b, (((0,), (0,)), ((), ())), preferred_element_type=jnp.float32)


def scale_of(features):
    return math.log2(math.e) / math.sqrt(8.0 * features)


def split_squares(pts):
    wide = pts.astype(jnp.float32)
    square = wide * wide
    high = square.astype(jnp.bfloat16)
    low = (square - high.astype(jnp.float32)).astype(jnp.bfloat16)
    return high, low


def col_term(high, low):
    features = high.shape[1]
    ones = jnp.ones((features, 128), jnp.bfloat16)
    return scale_of(features) * (features - (mm(high, ones) + mm(low, ones)))


def row_term(high, low):
    features = high.shape[1]
    ones = jnp.ones((8, features), jnp.bfloat16)
    return scale_of(features) * (features - (mm_nt(ones, high) + mm_nt(ones, low)))


def wide(col, lanes):
    return jnp.concatenate([col] * (lanes // 128), axis=1)


def hits(far, counts, first):
    rows, slots = far.shape
    ids = lax.broadcasted_iota(jnp.int32, (rows, 128), 1) + first
    found = jnp.zeros((rows, 128), jnp.float32)
    for k in range(slots):
        same = (far[:, k : k + 1] == ids) & (counts > k)
        found = jnp.where(same, 1.0, found)
    return found


def count_column(count_ref, rows):
    spot = lax.broadcasted_iota(jnp.int32, (rows, 128), 0)
    column = jnp.zeros((rows, 128), jnp.int32)
    for t in range(rows):
        column = jnp.where(spot == t, count_ref[t], column)
    return column


def one_hot_rows(index_columns, at, choices):
    spots = lax.broadcasted_iota(jnp.int32, (index_columns.shape[0], choices), 1)
    same = index_columns[:, at : at + 1] == spots
    return jnp.where(same, 1.0, 0.0).astype(jnp.bfloat16)


def neighbours(cores_axis_size):
    me = lax.axis_index("leaf")
    core = lax.rem(me, 2)
    chips = cores_axis_size // 2
    chip = me // 2
    step = 2 * core - 1
    side_b = lax.rem(chip + step + chips, chips)
    side_a = lax.rem(chip - step + chips, chips)
    return me, core, chip, side_a, side_b


def front_kernel(
    points_ref, weights_ref, basis_ref, lt_ref, t_ref, ls_ref, ns_ref, leaf_ref, node_ref
):
    leaves, rows, rank = basis_ref.shape
    nodes = t_ref.shape[0]
    features = points_ref.shape[1]
    cols = weights_ref.shape[1]
    leaf_columns = jnp.transpose(ls_ref[...])
    node_columns = jnp.transpose(jnp.concatenate([ns_ref[...]] * 4, axis=0))
    for leaf in range(leaves):
        own = slice(leaf * rank, (leaf + 1) * rank)
        pts = points_ref[leaf * rows : (leaf + 1) * rows, :]
        picked = mm(one_hot_rows(leaf_columns, leaf, rows), pts)
        leaf_ref[own, 0:features] = picked.astype(jnp.bfloat16)
        charge = mm_tn(basis_ref[leaf], weights_ref[leaf * rows : (leaf + 1) * rows, :])
        leaf_ref[own, features : features + cols] = charge.astype(jnp.bfloat16)
    for node in range(nodes):
        own = slice(node * rank, (node + 1) * rank)
        kids = slice(node * 4 * rank, (node + 1) * 4 * rank)
        picked = mm(one_hot_rows(node_columns, node, 4 * rank), leaf_ref[kids, 0:features])
        node_ref[own, 0:features] = picked.astype(jnp.bfloat16)
        transfer = lt_ref[node * 4 : node * 4 + 4].reshape(4 * rank, rank)
        charge = mm_tn(transfer, leaf_ref[kids, features : features + cols])
        node_ref[own, features : features + cols] = charge.astype(jnp.bfloat16)
        node_ref[own, features + cols :] = t_ref[node]


def upper_kernel(own_ref, other_ref, us_ref, out_ref, stacked, *, total):
    _, core, chip, _, _ = neighbours(total)
    half, width = own_ref.shape
    kept = out_ref.shape[1]
    rank = width - kept
    features = kept - rank
    mine = pl.multiple_of(core * half, half)
    theirs = pl.multiple_of((1 - core) * half, half)
    stacked[pl.ds(mine, half), :] = own_ref[...]
    stacked[pl.ds(theirs, half), :] = other_ref[...]
    out_ref[0 : 2 * half, :] = stacked[:, 0:kept]
    index = us_ref[pl.ds(chip, 1), :]
    columns = jnp.transpose(jnp.broadcast_to(index, (8, index.shape[1])))
    picked = mm(one_hot_rows(columns, 0, 2 * half), stacked[:, 0:features])
    out_ref[2 * half :, 0:features] = picked.astype(jnp.bfloat16)
    charge = mm_tn(stacked[:, kept:], stacked[:, features:kept])
    out_ref[2 * half :, features:] = charge.astype(jnp.bfloat16)


def near_kernel(points_ref, weights_ref, out_ref, *, rows):
    features = points_ref.shape[1]
    same = lax.broadcasted_iota(jnp.int32, (rows, rows), 0) == lax.broadcasted_iota(
        jnp.int32, (rows, rows), 1
    )
    for leaf in range(points_ref.shape[0] // rows):
        own = slice(leaf * rows, (leaf + 1) * rows)
        pts = points_ref[own, :]
        high, low = split_squares(pts)
        inner = mm_nt(pts, pts)
        power = (
            inner * (2.0 * scale_of(features))
            + wide(col_term(high, low), rows)
            + row_term(high, low)[0:1]
        )
        tile = jnp.exp2(jnp.where(same, NEG, power)).astype(jnp.bfloat16)
        out_ref[own, :] = mm(tile, weights_ref[own, :])


def unit(left, col, right, row_top, row_bottom, charge):
    features = left.shape[1]
    power = mm_nt(left, right) * (2.0 * scale_of(features)) + wide(col, right.shape[0])
    half = left.shape[0] // 2
    block = jnp.concatenate(
        [jnp.exp2(power[:half] + row_top), jnp.exp2(power[half:] + row_bottom)], axis=0
    )
    return mm(block.astype(jnp.bfloat16), charge)


def fill_rows(source_ref, rows_ref, found, features):
    for group in range(rows_ref.shape[0]):
        high, low = split_squares(source_ref[group * 256 : (group + 1) * 256, 0:features])
        term = row_term(high, low)[0 : found.shape[0]]
        for half in range(2):
            j = group * 2 + half
            lanes = slice(half * 128, half * 128 + 128)
            rows_ref[group, :, lanes] = jnp.where(found[:, j : j + 1] > 0.0, term[:, lanes], NEG)


def own_far_kernel(
    leaf_ref, side_ref, far_ref, nodes_ref, nfar_ref, count_ref, ncount_ref,
    pot_ref, npot_ref, own_rows, side_rows, node_rows, *, total,
):
    me, core, chip, _, _ = neighbours(total)
    features = leaf_ref.shape[1] - pot_ref.shape[1]
    targets = far_ref.shape[0]
    counts = count_column(count_ref, targets)
    fill_rows(leaf_ref, own_rows, hits(far_ref[...], counts, me * targets), features)
    other = me + 1 - 2 * core
    fill_rows(side_ref, side_rows, hits(far_ref[...], counts, other * targets), features)
    groups = targets // 2
    for group in range(groups):
        at = group + core * (groups - 1 - 2 * group)
        own = pl.ds(pl.multiple_of(at * 256, 256), 256)
        left = leaf_ref[own, 0:features]
        col = col_term(*split_squares(left))
        total_here = jnp.zeros((256, pot_ref.shape[1]), jnp.float32)
        for source in range(groups):
            here = slice(source * 256, source * 256 + 256)
            total_here += unit(
                left, col, leaf_ref[here, 0:features],
                own_rows[source, pl.ds(2 * at, 1), :],
                own_rows[source, pl.ds(2 * at + 1, 1), :],
                leaf_ref[here, features:],
            )
        for source in range(group + 1):
            src = source + core * (groups - 1 - 2 * source)
            here = pl.ds(pl.multiple_of(src * 256, 256), 256)
            total_here += unit(
                left, col, side_ref[here, 0:features],
                side_rows[src, pl.ds(2 * at, 1), :],
                side_rows[src, pl.ds(2 * at + 1, 1), :],
                side_ref[here, features:],
            )
        pot_ref[own, :] = total_here
    ncounts = count_column(ncount_ref, 2)
    fill_rows(nodes_ref, node_rows, hits(nfar_ref[...], ncounts, chip * 4), features)
    left = nodes_ref[pl.ds(pl.multiple_of(core * 256, 256), 256), 0:features]
    col = col_term(*split_squares(left))
    total_here = jnp.zeros((256, pot_ref.shape[1]), jnp.float32)
    for source in range(2):
        here = slice(source * 256, source * 256 + 256)
        total_here += unit(
            left, col, nodes_ref[here, 0:features],
            node_rows[source, 0:1, :], node_rows[source, 1:2, :], nodes_ref[here, features:],
        )
    npot_ref[...] = total_here


def rim_far_kernel(
    leaf_ref, rim_ref, far_ref, start_ref, count_ref, pot_ref, rim_rows, *, total
):
    me, core, _, _, _ = neighbours(total)
    features = leaf_ref.shape[1] - pot_ref.shape[1]
    targets = far_ref.shape[0]
    counts = count_column(count_ref, targets)
    partner = lax.rem(me + 2 * core - 1 + total, total)
    fill_rows(rim_ref, rim_rows, hits(far_ref[...], counts, partner * targets), features)
    groups = targets // 2
    for group in range(groups):
        at = group + core * (groups - 1 - 2 * group)
        own = pl.ds(pl.multiple_of(at * 256, 256), 256)
        left = leaf_ref[own, 0:features]
        col = col_term(*split_squares(left))
        total_here = start_ref[own, :]
        for source in range(group, groups):
            src = source + core * (groups - 1 - 2 * source)
            here = pl.ds(pl.multiple_of(src * 256, 256), 256)
            total_here += unit(
                left, col, rim_ref[here, 0:features],
                rim_rows[src, pl.ds(2 * at, 1), :],
                rim_rows[src, pl.ds(2 * at + 1, 1), :],
                rim_ref[here, features:],
            )
        pot_ref[own, :] = total_here


def last_kernel(
    near_ref, pot_ref, npot_ref, nodes_ref, side_b_ref, side_a_ref, nfar_ref,
    t_ref, lt_ref, basis_ref, ncount_ref, ufar_ref, ucount_ref,
    out_ref, rows_b, rows_a, *, total,
):
    _, core, chip, side_a, side_b = neighbours(total)
    cols = pot_ref.shape[1]
    features = nodes_ref.shape[1] - cols
    own_upper = nodes_ref[512:640, 0:features]
    upper_col = col_term(*split_squares(own_upper))
    live = ucount_ref[chip]
    far2 = jnp.zeros((128, cols), jnp.float32)
    for ref, ident in ((side_b_ref, side_b), (side_a_ref, side_a)):
        source = ref[512:640, 0:features]
        used = jnp.int32(0)
        for k in range(ufar_ref.shape[1]):
            used = jnp.where((ufar_ref[chip, k] == ident) & (k < live), 1, used)
        row = jnp.where(used > 0, row_term(*split_squares(source))[0:1], NEG)
        power = mm_nt(own_upper, source) * (2.0 * scale_of(features)) + upper_col + row
        far2 += mm(jnp.exp2(power).astype(jnp.bfloat16), ref[512:640, features:])
    down2 = far2.astype(jnp.bfloat16)
    ncounts = count_column(ncount_ref, 2)
    left = nodes_ref[pl.ds(pl.multiple_of(core * 256, 256), 256), 0:features]
    col = col_term(*split_squares(left))
    far1 = npot_ref[...]
    for ref, ident, rows_ref in ((side_b_ref, side_b, rows_b), (side_a_ref, side_a, rows_a)):
        fill_rows(ref, rows_ref, hits(nfar_ref[...], ncounts, ident * 4), features)
        for source in range(2):
            here = slice(source * 256, source * 256 + 256)
            far1 += unit(
                left, col, ref[here, 0:features],
                rows_ref[source, 0:1, :], rows_ref[source, 1:2, :], ref[here, features:],
            )
    leaves, rows, rank = basis_ref.shape
    for node in range(2):
        down1 = (far1[node * 128 : node * 128 + 128] + mm(t_ref[node], down2)).astype(jnp.bfloat16)
        for leaf in range(node * 4, node * 4 + 4):
            down0 = pot_ref[leaf * rank : (leaf + 1) * rank, :] + mm(lt_ref[leaf], down1)
            own = slice(leaf * rows, (leaf + 1) * rows)
            result = near_ref[own, :] + mm(basis_ref[leaf], down0.astype(jnp.bfloat16))
            out_ref[own, :] = result.astype(jnp.bfloat16)


def call(kernel, outs, args, smem=0, scratch=(), mmacs=0, name=None):
    n = len(args) - smem
    bytes_moved = sum(a.size * a.dtype.itemsize for a in list(args) + list(outs))
    return pl.pallas_call(
        kernel,
        out_shape=outs,
        in_specs=[pl.BlockSpec(memory_space=VMEM)] * n + [pl.BlockSpec(memory_space=SMEM)] * smem,
        out_specs=[pl.BlockSpec(memory_space=VMEM)] * len(outs),
        scratch_shapes=list(scratch),
        compiler_params=pltpu.CompilerParams(vmem_limit_bytes=LIMIT),
        cost_estimate=pl.CostEstimate(
            flops=int(2e6 * mmacs), bytes_accessed=int(bytes_moved), transcendentals=0
        ),
        name=name,
    )(*args)


def per_device(
    points, weights, leaf_basis, leaf_transfer, node_transfer, leaf_skeleton, node_skeleton,
    upper_skeleton, leaf_far, leaf_count, node_far, node_count, upper_far, upper_count,
):
    leaves, rows, rank = leaf_basis.shape
    features = points.shape[1]
    cols = weights.shape[1]
    total = lax.axis_size("leaf")
    pack = features + cols
    bf16, f32 = jnp.bfloat16, jnp.float32
    across = [(d, d ^ 1) for d in range(total)]
    outward = [(d, (d + 1) % total if d % 2 else (d - 1) % total) for d in range(total)]
    shape = jax.ShapeDtypeStruct

    leaf_pack, node_pack = call(
        front_kernel,
        [shape((leaves * rank, pack), bf16), shape((2 * rank, pack + rank), bf16)],
        [points, weights, leaf_basis, leaf_transfer, node_transfer, leaf_skeleton, node_skeleton],
        mmacs=250, name="front",
    )
    other_nodes = lax.ppermute(node_pack, "leaf", across)
    rim = lax.ppermute(leaf_pack, "leaf", outward)
    side = lax.ppermute(leaf_pack, "leaf", across)
    (nodes,) = call(
        functools.partial(upper_kernel, total=total),
        [shape((5 * rank, pack), bf16)],
        [node_pack, other_nodes, upper_skeleton],
        scratch=[pltpu.VMEM((4 * rank, pack + rank), bf16)],
        mmacs=30, name="upper",
    )
    nodes_b = lax.ppermute(nodes, "leaf", outward)
    nodes_a = lax.ppermute(nodes_b, "leaf", across)
    (near,) = call(
        functools.partial(near_kernel, rows=rows),
        [shape((leaves * rows, cols), f32)],
        [points, weights],
        mmacs=1500, name="near",
    )
    pot_start, node_pot = call(
        functools.partial(own_far_kernel, total=total),
        [shape((leaves * rank, cols), f32), shape((2 * rank, cols), f32)],
        [leaf_pack, side, leaf_far, nodes, node_far, leaf_count, node_count],
        smem=2,
        scratch=[
            pltpu.VMEM((leaves // 2, leaves, 256), f32),
            pltpu.VMEM((leaves // 2, leaves, 256), f32),
            pltpu.VMEM((2, 2, 256), f32),
        ],
        mmacs=2000, name="own_far",
    )
    (pot,) = call(
        functools.partial(rim_far_kernel, total=total),
        [shape((leaves * rank, cols), f32)],
        [leaf_pack, rim, leaf_far, pot_start, leaf_count],
        smem=1,
        scratch=[pltpu.VMEM((leaves // 2, leaves, 256), f32)],
        mmacs=1000, name="rim_far",
    )
    (out,) = call(
        functools.partial(last_kernel, total=total),
        [shape((leaves * rows, cols), bf16)],
        [near, pot, node_pot, nodes, nodes_b, nodes_a, node_far, node_transfer, leaf_transfer,
         leaf_basis, node_count, upper_far, upper_count],
        smem=3,
        scratch=[pltpu.VMEM((2, 2, 256), f32), pltpu.VMEM((2, 2, 256), f32)],
        mmacs=500, name="last",
    )
    return out


def solution(mesh):
    placed = (
        P("leaf", None),
        P("leaf", "cols"),
        P("leaf", None, None),
        P("leaf", None, None),
        P("leaf", None, None),
        P("leaf", None),
        P("leaf", None),
        P(),
        P("leaf", None),
        P("leaf"),
        P("leaf", None),
        P("leaf"),
        P(),
        P(),
    )
    return jax.shard_map(
        per_device, mesh=mesh, in_specs=placed, out_specs=P("leaf", "cols"), check_vma=False
    )
```

```python
import functools
import math

import jax
import jax.numpy as jnp
from jax import lax
from jax.experimental import pallas as pl
from jax.experimental.pallas import tpu as pltpu
from jax.sharding import PartitionSpec as P

NEG = -1e38
VMEM = pltpu.VMEM
SMEM = pltpu.SMEM
HBM = pltpu.HBM
LIMIT = 48 * 1024 * 1024


def mm(a, b):
    return jnp.dot(a, b, preferred_element_type=jnp.float32)


def mm_nt(a, b):
    return lax.dot_general(a, b, (((1,), (1,)), ((), ())), preferred_element_type=jnp.float32)


def mm_tn(a, b):
    return lax.dot_general(a, b, (((0,), (0,)), ((), ())), preferred_element_type=jnp.float32)


def scale_of(features):
    return math.log2(math.e) / math.sqrt(8.0 * features)


def split_squares(pts):
    wide = pts.astype(jnp.float32)
    square = wide * wide
    high = square.astype(jnp.bfloat16)
    low = (square - high.astype(jnp.float32)).astype(jnp.bfloat16)
    return high, low


def col_term(high, low):
    features = high.shape[1]
    ones = jnp.ones((features, 128), jnp.bfloat16)
    return scale_of(features) * (features - (mm(high, ones) + mm(low, ones)))


def row_term(high, low):
    features = high.shape[1]
    ones = jnp.ones((8, features), jnp.bfloat16)
    return scale_of(features) * (features - (mm_nt(ones, high) + mm_nt(ones, low)))


def wide(col, lanes):
    return jnp.concatenate([col] * (lanes // 128), axis=1)


def hits(far, counts, first):
    rows, slots = far.shape
    ids = lax.broadcasted_iota(jnp.int32, (rows, 128), 1) + first
    found = jnp.zeros((rows, 128), jnp.float32)
    for k in range(slots):
        same = (far[:, k : k + 1] == ids) & (counts > k)
        found = jnp.where(same, 1.0, found)
    return found


def count_column(count_ref, rows):
    spot = lax.broadcasted_iota(jnp.int32, (rows, 128), 0)
    column = jnp.zeros((rows, 128), jnp.int32)
    for t in range(rows):
        column = jnp.where(spot == t, count_ref[t], column)
    return column


def one_hot_rows(index_columns, at, choices):
    spots = lax.broadcasted_iota(jnp.int32, (index_columns.shape[0], choices), 1)
    same = index_columns[:, at : at + 1] == spots
    return jnp.where(same, 1.0, 0.0).astype(jnp.bfloat16)


def place(total):
    me = lax.axis_index("leaf")
    core = lax.rem(me, 2)
    chips = total // 2
    chip = me // 2
    step = 2 * core - 1
    side_b = lax.rem(chip + step + chips, chips)
    side_a = lax.rem(chip - step + chips, chips)
    return me, core, chip, side_a, side_b


def outer_first(core, group, groups):
    return group + core * (groups - 1 - 2 * group)


def fetch(pairs, sems):
    copies = [pltpu.make_async_copy(s, d, sems.at[i]) for i, (s, d) in enumerate(pairs)]
    for copy in copies:
        copy.start()
    return copies


def group_rows(at):
    return pl.ds(pl.multiple_of(at * 256, 256), 256)


def fill_rows(source_ref, rows_ref, found, features, place_of):
    for group in range(rows_ref.shape[0]):
        high, low = split_squares(source_ref[place_of(group), 0:features])
        term = row_term(high, low)[0 : found.shape[0]]
        for half in range(2):
            j = group * 2 + half
            lanes = slice(half * 128, half * 128 + 128)
            rows_ref[group, :, lanes] = jnp.where(found[:, j : j + 1] > 0.0, term[:, lanes], NEG)


def unit(left, col, right, row_top, row_bottom, charge):
    features = left.shape[1]
    power = mm_nt(left, right) * (2.0 * scale_of(features)) + wide(col, right.shape[0])
    half = left.shape[0] // 2
    block = jnp.concatenate(
        [jnp.exp2(power[:half] + row_top), jnp.exp2(power[half:] + row_bottom)], axis=0
    )
    return mm(block.astype(jnp.bfloat16), charge)


def front_kernel(
    points_hbm, weights_hbm, basis_hbm, lt_hbm, t_hbm, ls_hbm, ns_hbm, far_hbm, count_hbm,
    pack_ref, rim_ref, mask_ref,
    points, weights, basis, lt, t, ls, ns, far, count, sems, *, total,
):
    me, core, _, _, _ = place(total)
    leaves, rows, rank = basis.shape
    nodes = t.shape[0]
    features = points.shape[1]
    cols = weights.shape[1]
    pairs = [(ls_hbm, ls), (ns_hbm, ns), (far_hbm, far), (count_hbm, count)]
    small = len(pairs)
    for leaf in range(leaves):
        own = pl.ds(leaf * rows, rows)
        pairs += [
            (points_hbm.at[own], points.at[own]),
            (weights_hbm.at[own], weights.at[own]),
            (basis_hbm.at[leaf], basis.at[leaf]),
        ]
    pairs += [(lt_hbm, lt), (t_hbm, t)]
    copies = fetch(pairs, sems)
    for copy in copies[:small]:
        copy.wait()
    counts = count_column(count, leaves)
    for at, first in enumerate((me, me + 1 - 2 * core, lax.rem(me + 2 * core - 1 + total, total))):
        found = hits(far[...], counts, first * leaves)
        mask_ref[at * 8 : at * 8 + 8, :] = found
    rim_ref[512:528, :] = jnp.zeros((16, rim_ref.shape[1]), jnp.bfloat16)
    rim_ref[512:528, 0:128] = jnp.concatenate(
        [found, jnp.zeros((8, 128), jnp.float32)], axis=0
    ).astype(jnp.bfloat16)
    leaf_columns = jnp.transpose(ls[...])
    node_columns = jnp.transpose(jnp.concatenate([ns[...]] * 4, axis=0))
    groups = leaves // 2
    picked, charges = [], []
    for leaf in range(leaves):
        for copy in copies[small + 3 * leaf : small + 3 * leaf + 3]:
            copy.wait()
        own = slice(leaf * rows, (leaf + 1) * rows)
        skel = mm(one_hot_rows(leaf_columns, leaf, rows), points[own, :]).astype(jnp.bfloat16)
        charge = mm_tn(basis[leaf], weights[own, :]).astype(jnp.bfloat16)
        start = outer_first(core, leaf // 2, groups) * 256 + (leaf % 2) * rank
        here = pl.ds(pl.multiple_of(start, 128), rank)
        pack_ref[here, 0:features] = skel
        pack_ref[here, features:] = charge
        picked.append(skel)
        charges.append(charge)
    rim_ref[0:512, :] = pack_ref[0:512, :]
    for copy in copies[small + 3 * leaves :]:
        copy.wait()
    base = leaves * rank
    for node in range(nodes):
        own = slice(base + node * rank, base + (node + 1) * rank)
        kids = jnp.concatenate(picked[node * 4 : node * 4 + 4], axis=0)
        rows_hot = one_hot_rows(node_columns, node, 4 * rank)
        pack_ref[own, 0:features] = mm(rows_hot, kids).astype(jnp.bfloat16)
        transfer = lt[node * 4 : node * 4 + 4].reshape(4 * rank, rank)
        charge = mm_tn(transfer, jnp.concatenate(charges[node * 4 : node * 4 + 4], axis=0))
        pack_ref[own, features:] = charge.astype(jnp.bfloat16)
        last = slice(base + 2 * rank, base + 3 * rank)
        pack_ref[last, node * rank : (node + 1) * rank] = t[node]
    pack_ref[base + 2 * rank :, 2 * rank :] = jnp.zeros((rank, rank), jnp.bfloat16)


def upper_kernel(own_ref, other_ref, us_hbm, out_ref, us, transfers, sems, *, total):
    _, core, chip, _, _ = place(total)
    (copy,) = fetch([(us_hbm, us)], sems)
    cols = 128
    features = own_ref.shape[1] - cols
    base = own_ref.shape[0] - 384
    mine = pl.multiple_of(core * 256, 256)
    theirs = pl.multiple_of((1 - core) * 256, 256)
    for start, ref in ((mine, own_ref), (theirs, other_ref)):
        out_ref[pl.ds(start, 256), :] = ref[base : base + 256, :]
        transfers[pl.ds(start, 128), :] = ref[base + 256 : base + 384, 0:128]
        transfers[pl.ds(start + 128, 128), :] = ref[base + 256 : base + 384, 128:256]
    charge = mm_tn(transfers[...], out_ref[0:512, features:])
    out_ref[512:640, features:] = charge.astype(jnp.bfloat16)
    copy.wait()
    index = us[pl.ds(chip, 1), :]
    columns = jnp.transpose(jnp.broadcast_to(index, (8, index.shape[1])))
    picked = mm(one_hot_rows(columns, 0, 512), out_ref[0:512, 0:features])
    out_ref[512:640, 0:features] = picked.astype(jnp.bfloat16)


def near_kernel(points_hbm, weights_hbm, out_ref, points, weights, sems, *, rows):
    features = points.shape[1]
    leaves = points.shape[0] // rows
    pairs = []
    for leaf in range(leaves):
        own = pl.ds(leaf * rows, rows)
        pairs += [
            (points_hbm.at[own], points.at[own]), (weights_hbm.at[own], weights.at[own])
        ]
    copies = fetch(pairs, sems)
    same = lax.broadcasted_iota(jnp.int32, (rows, rows), 0) == lax.broadcasted_iota(
        jnp.int32, (rows, rows), 1
    )
    for leaf in range(leaves):
        copies[2 * leaf].wait()
        copies[2 * leaf + 1].wait()
        own = slice(leaf * rows, (leaf + 1) * rows)
        pts = points[own, :]
        high, low = split_squares(pts)
        power = (
            mm_nt(pts, pts) * (2.0 * scale_of(features))
            + wide(col_term(high, low), rows)
            + row_term(high, low)[0:1]
        )
        tile = jnp.exp2(jnp.where(same, NEG, power)).astype(jnp.bfloat16)
        out_ref[own, :] = mm(tile, weights[own, :])


def far_groups(targets_ref, source_ref, rows_ref, start, pot_ref, core, pairs, features):
    groups = 4
    for group, sources in pairs:
        own = group_rows(group)
        at = outer_first(core[0], group, groups)
        left = targets_ref[own, 0:features]
        col = col_term(*split_squares(left))
        total_here = None if start is None else start[own, :]
        for source in sources:
            here = group_rows(source)
            src = outer_first(core[1], source, groups)
            part = unit(
                left, col, source_ref[here, 0:features],
                rows_ref[src, pl.ds(2 * at, 1), :], rows_ref[src, pl.ds(2 * at + 1, 1), :],
                source_ref[here, features:],
            )
            total_here = part if total_here is None else total_here + part
        pot_ref[own, :] = total_here.astype(pot_ref.dtype)


def own_kernel(pack_ref, mask_ref, pot_ref, rows_ref, *, total):
    _, core, _, _, _ = place(total)
    features = pack_ref.shape[1] - pot_ref.shape[1]
    fill_rows(
        pack_ref, rows_ref, mask_ref[0:8, :], features,
        lambda g: group_rows(outer_first(core, g, 4)),
    )
    pairs = [(g, range(4)) for g in range(4)]
    far_groups(pack_ref, pack_ref, rows_ref, None, pot_ref, (core, core), pairs, features)


def side_kernel(pack_ref, side_ref, mask_ref, start_ref, pot_ref, rows_ref, *, total):
    _, core, _, _, _ = place(total)
    features = pack_ref.shape[1] - pot_ref.shape[1]
    fill_rows(
        side_ref, rows_ref, mask_ref[8:16, :], features,
        lambda g: group_rows(outer_first(1 - core, g, 4)),
    )
    pairs = [(g, range(3 - g, 4)) for g in range(4)]
    far_groups(pack_ref, side_ref, rows_ref, start_ref, pot_ref, (core, 1 - core), pairs, features)


def back_kernel(pack_ref, rim_ref, ret_ref, rows_ref, *, total):
    _, core, _, _, _ = place(total)
    features = pack_ref.shape[1] - ret_ref.shape[1]
    found = rim_ref[512:528, 0:128].astype(jnp.float32)[0:8, :]
    fill_rows(
        pack_ref, rows_ref, found, features, lambda g: group_rows(outer_first(core, g, 4))
    )
    pairs = [(0, (2, 3)), (1, (2,))]
    far_groups(rim_ref, pack_ref, rows_ref, None, ret_ref, (1 - core, core), pairs, features)


def rim_kernel(pack_ref, rim_ref, mask_ref, start_ref, pot_ref, rows_ref, *, total):
    _, core, _, _, _ = place(total)
    features = pack_ref.shape[1] - pot_ref.shape[1]
    found = mask_ref[16:24, :]
    for source in range(2):
        tree = outer_first(1 - core, source, 4)
        high, low = split_squares(rim_ref[group_rows(source), 0:features])
        term = row_term(high, low)[0:8]
        for half in range(2):
            zero = found[:, 2 * source + half : 2 * source + half + 1]
            one = found[:, 2 * (3 - source) + half : 2 * (3 - source) + half + 1]
            used = jnp.where(core == 0, one, zero)
            lanes = slice(half * 128, half * 128 + 128)
            rows_ref[tree, :, lanes] = jnp.where(used > 0.0, term[:, lanes], NEG)
    pairs = [(0, (0, 1)), (1, (0, 1)), (2, (0, 1)), (3, (0,))]
    far_groups(pack_ref, rim_ref, rows_ref, start_ref, pot_ref, (core, 1 - core), pairs, features)


def node_kernel(
    nodes_ref, side_b_ref, side_a_ref, pot_ref, ufar_ref, t_hbm, lt_hbm, nfar_hbm,
    ncount_hbm, ucount_hbm, out_ref, rows_ref, t, lt, nfar, ncount, ucount, sems, *, total,
):
    _, core, chip, side_a, side_b = place(total)
    copies = fetch(
        [(nfar_hbm, nfar), (ncount_hbm, ncount), (ucount_hbm, ucount), (t_hbm, t), (lt_hbm, lt)],
        sems,
    )
    cols = pot_ref.shape[1]
    features = nodes_ref.shape[1] - cols
    scale = 2.0 * scale_of(features)
    own_upper = nodes_ref[512:640, 0:features]
    upper_col = col_term(*split_squares(own_upper))
    left = nodes_ref[group_rows(core), 0:features]
    col = col_term(*split_squares(left))
    for copy in copies[0:3]:
        copy.wait()
    ufar = ufar_ref[pl.ds(chip, 1), :]
    live = ucount[chip]
    far2 = jnp.zeros((128, cols), jnp.float32)
    for ref, ident in ((side_b_ref, side_b), (side_a_ref, side_a)):
        source = ref[512:640, 0:features]
        used = jnp.zeros((1, 128), jnp.float32)
        for k in range(ufar.shape[1]):
            same = (jnp.broadcast_to(ufar[:, k : k + 1], (1, 128)) == ident) & (k < live)
            used = jnp.where(same, 1.0, used)
        row = jnp.where(used > 0.0, row_term(*split_squares(source))[0:1], NEG)
        power = mm_nt(own_upper, source) * scale + upper_col + row
        far2 += mm(jnp.exp2(power).astype(jnp.bfloat16), ref[512:640, features:])
    down2 = far2.astype(jnp.bfloat16)
    ncounts = count_column(ncount, 2)
    far1 = None
    for ref, first in ((nodes_ref, chip), (side_b_ref, side_b), (side_a_ref, side_a)):
        found = hits(nfar[...], ncounts, first * 4)
        fill_rows(ref, rows_ref, found, features, group_rows)
        for source in range(2):
            here = group_rows(source)
            part = unit(
                left, col, ref[here, 0:features],
                rows_ref[source, 0:1, :], rows_ref[source, 1:2, :], ref[here, features:],
            )
            far1 = part if far1 is None else far1 + part
    for copy in copies[3:]:
        copy.wait()
    rank = t.shape[1]
    for node in range(2):
        down1 = (far1[node * rank : (node + 1) * rank] + mm(t[node], down2)).astype(jnp.bfloat16)
        for leaf in range(node * 4, node * 4 + 4):
            start = outer_first(core, leaf // 2, 4) * 256 + (leaf % 2) * rank
            here = pl.ds(pl.multiple_of(start, 128), rank)
            out_ref[leaf * rank : (leaf + 1) * rank, :] = pot_ref[here, :] + mm(lt[leaf], down1)


def last_kernel(near_ref, pot_ref, ret_ref, basis_hbm, out_ref, basis, sems, *, total):
    _, core, _, _, _ = place(total)
    (copy,) = fetch([(basis_hbm, basis)], sems)
    copy.wait()
    leaves, rows, rank = basis.shape
    for leaf in range(leaves):
        group = outer_first(core, leaf // 2, 4)
        inside = jnp.minimum(group, 1) * 256 + (leaf % 2) * rank
        back = ret_ref[pl.ds(pl.multiple_of(inside, 128), rank), :].astype(jnp.float32)
        down0 = pot_ref[leaf * rank : (leaf + 1) * rank, :] + jnp.where(group < 2, back, 0.0)
        own = slice(leaf * rows, (leaf + 1) * rows)
        result = near_ref[own, :] + mm(basis[leaf], down0.astype(jnp.bfloat16))
        out_ref[own, :] = result.astype(jnp.bfloat16)


def call(kernel, outs, args, spaces, scratch=(), mmacs=0, name=None):
    kinds = {"v": VMEM, "h": HBM, "s": SMEM}
    return pl.pallas_call(
        kernel,
        out_shape=outs,
        in_specs=[pl.BlockSpec(memory_space=kinds[k]) for k in spaces],
        out_specs=[pl.BlockSpec(memory_space=VMEM)] * len(outs),
        scratch_shapes=list(scratch),
        compiler_params=pltpu.CompilerParams(vmem_limit_bytes=LIMIT),
        cost_estimate=pl.CostEstimate(
            flops=int(2e6 * mmacs), bytes_accessed=0, transcendentals=0
        ),
        name=name,
    )(*[pltpu.with_memory_space_constraint(a, pltpu.HBM) if k == 'h' else a for a, k in zip(args, spaces)])


def like(array, space=None):
    return (space or VMEM)(array.shape, array.dtype)


def per_device(
    points, weights, leaf_basis, leaf_transfer, node_transfer, leaf_skeleton, node_skeleton,
    upper_skeleton, leaf_far, leaf_count, node_far, node_count, upper_far, upper_count,
):
    leaves, rows, rank = leaf_basis.shape
    features = points.shape[1]
    cols = weights.shape[1]
    total = lax.axis_size("leaf")
    width = features + cols
    bf16, f32 = jnp.bfloat16, jnp.float32
    across = [(d, d ^ 1) for d in range(total)]
    outward = [(d, (d + 1) % total if d % 2 else (d - 1) % total) for d in range(total)]
    shape = jax.ShapeDtypeStruct
    sems = pltpu.SemaphoreType.DMA
    bind = functools.partial
    rows_scratch = pltpu.VMEM((leaves // 2, leaves, 256), f32)
    pot_shape = shape((leaves * rank, cols), f32)

    pack, rim, mask = call(
        bind(front_kernel, total=total),
        [
            shape((leaves * rank + 3 * rank, width), bf16),
            shape((4 * rank + 16, width), bf16),
            shape((24, 128), f32),
        ],
        [points, weights, leaf_basis, leaf_transfer, node_transfer, leaf_skeleton, node_skeleton,
         leaf_far, leaf_count],
        "hhhhhhhhh",
        [like(points), like(weights), like(leaf_basis), like(leaf_transfer), like(node_transfer),
         like(leaf_skeleton), like(node_skeleton), like(leaf_far), like(leaf_count, SMEM),
         sems((3 * leaves + 6,))],
        mmacs=300, name="front",
    )
    rim_in = lax.ppermute(rim, "leaf", outward)
    side = lax.ppermute(pack, "leaf", across)
    (nodes,) = call(
        bind(upper_kernel, total=total),
        [shape((5 * rank, width), bf16)],
        [pack, side, upper_skeleton], "vvh",
        [like(upper_skeleton), pltpu.VMEM((4 * rank, rank), bf16), sems((1,))],
        mmacs=30, name="upper",
    )
    nodes_b = lax.ppermute(nodes, "leaf", outward)
    nodes_a = lax.ppermute(nodes_b, "leaf", across)
    (near,) = call(
        bind(near_kernel, rows=rows),
        [shape((leaves * rows, cols), f32)],
        [points, weights], "hh",
        [like(points), like(weights), sems((2 * leaves,))],
        mmacs=1000, name="near",
    )
    (pot,) = call(
        bind(own_kernel, total=total), [pot_shape], [pack, mask], "vv", [rows_scratch],
        mmacs=1000, name="own",
    )
    (ret,) = call(
        bind(back_kernel, total=total), [shape((4 * rank, cols), bf16)], [pack, rim_in], "vv",
        [rows_scratch], mmacs=300, name="back",
    )
    ret_in = lax.ppermute(ret, "leaf", outward)
    (pot,) = call(
        bind(side_kernel, total=total), [pot_shape], [pack, side, mask, pot], "vvvv",
        [rows_scratch], mmacs=800, name="side",
    )
    (pot,) = call(
        bind(rim_kernel, total=total), [pot_shape], [pack, rim_in, mask, pot], "vvvv",
        [rows_scratch], mmacs=600, name="rim",
    )
    (pot,) = call(
        bind(node_kernel, total=total), [pot_shape],
        [nodes, nodes_b, nodes_a, pot, upper_far, node_transfer, leaf_transfer, node_far,
         node_count, upper_count],
        "vvvvvhhhhh",
        [pltpu.VMEM((2, 2, 256), f32), like(node_transfer), like(leaf_transfer), like(node_far),
         like(node_count, SMEM), like(upper_count, SMEM), sems((5,))],
        mmacs=500, name="node",
    )
    (out,) = call(
        bind(last_kernel, total=total),
        [shape((leaves * rows, cols), bf16)],
        [near, pot, ret_in, leaf_basis], "vvvh",
        [like(leaf_basis), sems((1,))],
        mmacs=200, name="last",
    )
    return out


def solution(mesh):
    placed = (
        P("leaf", None),
        P("leaf", "cols"),
        P("leaf", None, None),
        P("leaf", None, None),
        P("leaf", None, None),
        P("leaf", None),
        P("leaf", None),
        P(),
        P("leaf", None),
        P("leaf"),
        P("leaf", None),
        P("leaf"),
        P(),
        P(),
    )
    return jax.shard_map(
        per_device, mesh=mesh, in_specs=placed, out_specs=P("leaf", "cols"), check_vma=False
    )
```

```python
import functools
import math

import jax
import jax.numpy as jnp
from jax import lax
from jax.experimental import pallas as pl
from jax.experimental.pallas import tpu as pltpu
from jax.sharding import PartitionSpec as P

NEG = -1e38
VMEM = pltpu.VMEM
SMEM = pltpu.SMEM
HBM = pltpu.HBM
LIMIT = 12 * 1024 * 1024


def mm(a, b):
    return jnp.dot(a, b, preferred_element_type=jnp.float32)


def mm_nt(a, b):
    return lax.dot_general(a, b, (((1,), (1,)), ((), ())), preferred_element_type=jnp.float32)


def mm_tn(a, b):
    return lax.dot_general(a, b, (((0,), (0,)), ((), ())), preferred_element_type=jnp.float32)


def scale_of(features):
    return math.log2(math.e) / math.sqrt(8.0 * features)


def norm_col(pts):
    rows, features = pts.shape
    wide = pts.astype(jnp.float32)
    total = jnp.sum(wide * wide, axis=1, keepdims=True)
    return jnp.broadcast_to(scale_of(features) * (features - total), (rows, 128))


def norm_row(col, targets):
    return jnp.transpose(col)[0:targets]


def twice(col):
    return jnp.concatenate([col, col], axis=1)


def hits(far, counts, first):
    rows, slots = far.shape
    ids = lax.broadcasted_iota(jnp.int32, (rows, 128), 1) + first
    found = jnp.zeros((rows, 128), jnp.float32)
    for k in range(slots):
        same = (far[:, k : k + 1] == ids) & (counts > k)
        found = jnp.where(same, 1.0, found)
    return found


def count_column(count_ref, rows):
    spot = lax.broadcasted_iota(jnp.int32, (rows, 128), 0)
    column = jnp.zeros((rows, 128), jnp.int32)
    for t in range(rows):
        column = jnp.where(spot == t, count_ref[t], column)
    return column


def one_hot_rows(index_columns, at, choices):
    spots = lax.broadcasted_iota(jnp.int32, (index_columns.shape[0], choices), 1)
    same = index_columns[:, at : at + 1] == spots
    return jnp.where(same, 1.0, 0.0).astype(jnp.bfloat16)


def place(total):
    me = lax.axis_index("leaf")
    core = lax.rem(me, 2)
    chips = total // 2
    chip = me // 2
    step = 2 * core - 1
    side_b = lax.rem(chip + step + chips, chips)
    side_a = lax.rem(chip - step + chips, chips)
    return me, core, chip, side_a, side_b


def outer_first(core, group, groups):
    return group + core * (groups - 1 - 2 * group)


def fetch(pairs, sems):
    copies = [pltpu.make_async_copy(s, d, sems.at[i]) for i, (s, d) in enumerate(pairs)]
    for copy in copies:
        copy.start()
    return copies


def group_rows(at):
    return pl.ds(pl.multiple_of(at * 256, 256), 256)


def fill_rows(rows_ref, at, source, used_columns, targets):
    col = norm_col(source) if source.shape[1] != 128 else source
    for half in range(2):
        term = norm_row(col[half * 128 : half * 128 + 128], targets)
        lanes = slice(half * 128, half * 128 + 128)
        rows_ref[at, :, lanes] = jnp.where(used_columns[half] > 0.0, term, NEG)


def blocks(left, col, right, row_of):
    features = left.shape[1]
    inner = mm_nt(left, right)
    parts = []
    for at in range(left.shape[0] // 128):
        own = slice(at * 128, at * 128 + 128)
        power = inner[own] * (2.0 * scale_of(features)) + twice(col[own]) + row_of(at)
        parts.append(jnp.exp2(power).astype(jnp.bfloat16))
    return jnp.concatenate(parts, axis=0) if len(parts) > 1 else parts[0]


def tree_leaf(core, at):
    return outer_first(core, at // 2, 4) * 2 + at % 2


def front_kernel(
    points_hbm, weights_hbm, basis_hbm, lt_hbm, t_hbm, ls_hbm, ns_hbm, far_hbm, count_hbm, us_hbm,
    pack_ref, rim_ref, mask_ref, us,
    points, weights, basis, lt, t, ls, ns, far, count, sems, *, total,
):
    me, core, _, _, _ = place(total)
    leaves, rows, rank = basis.shape
    nodes = t.shape[0]
    features = points.shape[1]
    cols = weights.shape[1]
    small = [(ls_hbm, ls), (ns_hbm, ns), (far_hbm, far), (count_hbm, count), (us_hbm, us)]
    pairs = list(small)
    part = leaves // 2
    for half in range(2):
        own = pl.ds(half * part * rows, part * rows)
        some = pl.ds(half * part, part)
        pairs += [
            (points_hbm.at[own], points.at[own]),
            (weights_hbm.at[own], weights.at[own]),
            (basis_hbm.at[some], basis.at[some]),
        ]
    pairs += [(lt_hbm, lt), (t_hbm, t)]
    copies = fetch(pairs, sems)
    for copy in copies[: len(small)]:
        copy.wait()
    counts = count_column(count, leaves)
    for at, first in enumerate((me, me + 1 - 2 * core, lax.rem(me + 2 * core - 1 + total, total))):
        found = hits(far[...], counts, first * leaves)
        mask_ref[at * 8 : at * 8 + 8, :] = found
    rim_ref[512:528, :] = jnp.zeros((16, rim_ref.shape[1]), jnp.bfloat16)
    rim_ref[512:528, 0:128] = jnp.concatenate(
        [found, jnp.zeros((8, 128), jnp.float32)], axis=0
    ).astype(jnp.bfloat16)
    leaf_columns = jnp.transpose(ls[...])
    node_columns = jnp.transpose(jnp.concatenate([ns[...]] * 4, axis=0))
    groups = leaves // 2
    picked, charges = [], []
    base = leaves * rank
    for leaf in range(leaves):
        if leaf % part == 0:
            first = len(small) + 3 * (leaf // part)
            for copy in copies[first : first + 3]:
                copy.wait()
        own = slice(leaf * rows, (leaf + 1) * rows)
        skel = mm(one_hot_rows(leaf_columns, leaf, rows), points[own, :]).astype(jnp.bfloat16)
        charge = mm_tn(basis[leaf], weights[own, :]).astype(jnp.bfloat16)
        start = outer_first(core, leaf // 2, groups) * 256 + (leaf % 2) * rank
        here = pl.ds(pl.multiple_of(start, 128), rank)
        pack_ref[here, 0:features] = skel
        pack_ref[here, features:] = charge
        picked.append(skel)
        charges.append(charge)
    for copy in copies[len(small) + 6 :]:
        copy.wait()
    for node in range(nodes):
        own = slice(base + node * rank, base + (node + 1) * rank)
        kids = jnp.concatenate(picked[node * 4 : node * 4 + 4], axis=0)
        rows_hot = one_hot_rows(node_columns, node, 4 * rank)
        pack_ref[own, 0:features] = mm(rows_hot, kids).astype(jnp.bfloat16)
        transfer = lt[node * 4 : node * 4 + 4].reshape(4 * rank, rank)
        charge = mm_tn(transfer, jnp.concatenate(charges[node * 4 : node * 4 + 4], axis=0))
        pack_ref[own, features:] = charge.astype(jnp.bfloat16)
        last = slice(base + 2 * rank, base + 3 * rank)
        pack_ref[last, node * rank : (node + 1) * rank] = t[node]
    pack_ref[base + 2 * rank :, 2 * rank :] = jnp.zeros((rank, rank), jnp.bfloat16)
    rim_ref[0:512, :] = pack_ref[0:512, :]


def upper_kernel(own_ref, other_ref, us_ref, out_ref, transfers, *, total):
    _, core, chip, _, _ = place(total)
    cols = 128
    features = own_ref.shape[1] - cols
    base = own_ref.shape[0] - 384
    mine = pl.multiple_of(core * 256, 256)
    theirs = pl.multiple_of((1 - core) * 256, 256)
    for start, ref in ((mine, own_ref), (theirs, other_ref)):
        out_ref[pl.ds(start, 256), :] = ref[base : base + 256, :]
        transfers[pl.ds(start, 128), :] = ref[base + 256 : base + 384, 0:128]
        transfers[pl.ds(start + 128, 128), :] = ref[base + 256 : base + 384, 128:256]
    charge = mm_tn(transfers[...], out_ref[0:512, features:])
    out_ref[512:640, features:] = charge.astype(jnp.bfloat16)
    index = us_ref[pl.ds(chip, 1), :]
    columns = jnp.transpose(jnp.broadcast_to(index, (8, index.shape[1])))
    picked = mm(one_hot_rows(columns, 0, 512), out_ref[0:512, 0:features])
    out_ref[512:640, 0:features] = picked.astype(jnp.bfloat16)


def near_kernel(
    points, weights, ufar_ref, nfar_hbm, ncount_hbm, ucount_hbm, out_ref, mask_ref,
    nfar, ncount, ucount, sems, *, rows, total,
):
    _, _, chip, side_a, side_b = place(total)
    copies = fetch([(nfar_hbm, nfar), (ncount_hbm, ncount), (ucount_hbm, ucount)], sems)
    features = points.shape[1]
    same = lax.broadcasted_iota(jnp.int32, (rows, rows), 0) == lax.broadcasted_iota(
        jnp.int32, (rows, rows), 1
    )
    for leaf in range(points.shape[0] // rows):
        own = slice(leaf * rows, (leaf + 1) * rows)
        pts = points[own, :]
        col = norm_col(pts)
        row = jnp.concatenate([norm_row(col[0:128], 1), norm_row(col[128:256], 1)], axis=1)
        power = mm_nt(pts, pts) * (2.0 * scale_of(features)) + twice(col) + row
        tile = jnp.exp2(jnp.where(same, NEG, power)).astype(jnp.bfloat16)
        out_ref[own, :] = mm(tile, weights[own, :])
    for copy in copies:
        copy.wait()
    ncounts = count_column(ncount, 2)
    for at, ident in enumerate((chip, side_b, side_a)):
        mask_ref[at * 8 : at * 8 + 2, :] = hits(nfar[...], ncounts, ident * 4)
    ufar = ufar_ref[pl.ds(chip, 1), :]
    live = ucount[chip]
    for at, ident in enumerate((side_b, side_a)):
        used = jnp.zeros((1, 128), jnp.float32)
        for k in range(ufar.shape[1]):
            hit = (jnp.broadcast_to(ufar[:, k : k + 1], (1, 128)) == ident) & (k < live)
            used = jnp.where(hit, 1.0, used)
        mask_ref[24 + at : 25 + at, :] = used


def own_kernel(pack_ref, mask_ref, pot_ref, col_ref, rows_ref, block_ref, *, total):
    _, core, _, _, _ = place(total)
    features = pack_ref.shape[1] - pot_ref.shape[1]
    found = mask_ref[0:8, :]
    col_ref[...] = norm_col(pack_ref[0:1024, 0:features])
    for tree in range(4):
        here = group_rows(outer_first(core, tree, 4))
        used = [found[:, 2 * tree + h : 2 * tree + h + 1] for h in range(2)]
        fill_rows(rows_ref, tree, col_ref[here, :], used, 8)
    left = pack_ref[0:1024, 0:features]
    for source in range(4):
        src = outer_first(core, source, 4)
        here = slice(source * 256, source * 256 + 256)
        block_ref[:, here] = blocks(
            left, col_ref[...], pack_ref[here, 0:features],
            lambda at: rows_ref[src, pl.ds(tree_leaf(core, at), 1), :],
        )
    pot_ref[...] = mm(block_ref[...], pack_ref[0:1024, features:])


def side_kernel(
    pack_ref, side_ref, mask_ref, col_ref, start_ref, pot_ref, rows_ref, block_ref, *, total
):
    _, core, _, _, _ = place(total)
    features = pack_ref.shape[1] - pot_ref.shape[1]
    found = mask_ref[8:16, :]
    for tree in range(4):
        here = group_rows(outer_first(1 - core, tree, 4))
        used = [found[:, 2 * tree + h : 2 * tree + h + 1] for h in range(2)]
        fill_rows(rows_ref, tree, side_ref[here, 0:features], used, 8)
    for source in range(4):
        src = outer_first(1 - core, source, 4)
        here = slice(source * 256, source * 256 + 256)
        first = 3 - source
        block_ref[first * 256 :, here] = blocks(
            pack_ref[first * 256 : 1024, 0:features], col_ref[first * 256 :, :],
            side_ref[here, 0:features],
            lambda at: rows_ref[src, pl.ds(tree_leaf(core, at + 2 * first), 1), :],
        )
    for group in range(4):
        own = slice(group * 256, group * 256 + 256)
        span = slice((3 - group) * 256, 1024)
        pot_ref[own, :] = start_ref[own, :] + mm(block_ref[own, span], side_ref[span, features:])


def back_kernel(pack_ref, rim_ref, col_ref, ret_ref, rows_ref, *, total):
    _, core, _, _, _ = place(total)
    features = pack_ref.shape[1] - ret_ref.shape[1]
    found = rim_ref[512:528, 0:128].astype(jnp.float32)[0:8, :]
    left = rim_ref[0:512, 0:features]
    col = norm_col(left)
    parts = []
    for source in (2, 3):
        used = []
        for half in range(2):
            one = found[:, 2 * source + half : 2 * source + half + 1]
            other = found[:, 2 * (3 - source) + half : 2 * (3 - source) + half + 1]
            used.append(jnp.where(core == 0, one, other))
        here = slice(source * 256, source * 256 + 256)
        fill_rows(rows_ref, source, col_ref[here, :], used, 8)
        rows = 512 if source == 2 else 256
        parts.append(
            blocks(
                left[0:rows], col[0:rows], pack_ref[here, 0:features],
                lambda at: rows_ref[source, pl.ds(tree_leaf(1 - core, at), 1), :],
            )
        )
    both = jnp.concatenate([parts[0][0:256], parts[1]], axis=1)
    ret_ref[0:256, :] = mm(both, pack_ref[512:1024, features:]).astype(jnp.bfloat16)
    ret_ref[256:512, :] = mm(parts[0][256:512], pack_ref[512:768, features:]).astype(jnp.bfloat16)


def rim_kernel(
    pack_ref, rim_ref, mask_ref, col_ref, start_ref, pot_ref, rows_ref, block_ref, *, total
):
    _, core, _, _, _ = place(total)
    features = pack_ref.shape[1] - pot_ref.shape[1]
    found = mask_ref[16:24, :]
    for source in range(2):
        used = []
        for half in range(2):
            zero = found[:, 2 * source + half : 2 * source + half + 1]
            one = found[:, 2 * (3 - source) + half : 2 * (3 - source) + half + 1]
            used.append(jnp.where(core == 0, one, zero))
        here = slice(source * 256, source * 256 + 256)
        fill_rows(rows_ref, source, rim_ref[here, 0:features], used, 8)
        stop = 1024 - source * 256
        block_ref[0:stop, here] = blocks(
            pack_ref[0:stop, 0:features], col_ref[0:stop, :], rim_ref[here, 0:features],
            lambda at: rows_ref[source, pl.ds(tree_leaf(core, at), 1), :],
        )
    pot_ref[0:768, :] = start_ref[0:768, :] + mm(block_ref[0:768, :], rim_ref[0:512, features:])
    pot_ref[768:, :] = start_ref[768:, :] + mm(block_ref[768:, 0:256], rim_ref[0:256, features:])


def node_part(nodes_ref, ref, mask, core, rows_ref, features):
    own = nodes_ref[group_rows(core), 0:features]
    col = norm_col(own)
    parts = []
    for source in range(2):
        here = slice(source * 256, source * 256 + 256)
        used = [mask[:, 2 * source + h : 2 * source + h + 1] for h in range(2)]
        fill_rows(rows_ref, source, ref[here, 0:features], used, 2)
        parts.append(
            blocks(
                own, col, ref[here, 0:features], lambda at: rows_ref[source, at : at + 1, :]
            )
        )
    return mm(jnp.concatenate(parts, axis=1), ref[0:512, features:])


def upper_part(nodes_ref, ref, used, features):
    own = nodes_ref[512:640, 0:features]
    source = ref[512:640, 0:features]
    row = jnp.where(used > 0.0, norm_row(norm_col(source), 1), NEG)
    power = mm_nt(own, source) * (2.0 * scale_of(features)) + norm_col(own) + row
    return mm(jnp.exp2(power).astype(jnp.bfloat16), ref[512:640, features:])


def outer_node_kernel(
    nodes_ref, side_b_ref, mask_ref, far1_ref, far2_ref, rows_own, rows_ref, *, total
):
    _, core, _, _, _ = place(total)
    features = nodes_ref.shape[1] - far1_ref.shape[1]
    far2_ref[...] = upper_part(nodes_ref, side_b_ref, mask_ref[24:25, :], features)
    far1_ref[...] = node_part(
        nodes_ref, nodes_ref, mask_ref[0:2, :], core, rows_own, features
    ) + node_part(nodes_ref, side_b_ref, mask_ref[8:10, :], core, rows_ref, features)


def node_kernel(
    nodes_ref, side_a_ref, mask_ref, far1_ref, far2_ref, t, lt, pot_ref, out_ref, rows_ref, *, total
):
    _, core, _, _, _ = place(total)
    features = nodes_ref.shape[1] - pot_ref.shape[1]
    far2 = far2_ref[...] + upper_part(nodes_ref, side_a_ref, mask_ref[25:26, :], features)
    down2 = far2.astype(jnp.bfloat16)
    far1 = far1_ref[...] + node_part(
        nodes_ref, side_a_ref, mask_ref[16:18, :], core, rows_ref, features
    )
    rank = t.shape[1]
    for node in range(2):
        down1 = (far1[node * rank : (node + 1) * rank] + mm(t[node], down2)).astype(jnp.bfloat16)
        for leaf in range(node * 4, node * 4 + 4):
            start = outer_first(core, leaf // 2, 4) * 256 + (leaf % 2) * rank
            here = pl.ds(pl.multiple_of(start, 128), rank)
            out_ref[leaf * rank : (leaf + 1) * rank, :] = pot_ref[here, :] + mm(lt[leaf], down1)


def last_kernel(near_ref, pot_ref, ret_ref, basis, out_hbm, out_ref, sems, *, total):
    _, core, _, _, _ = place(total)
    leaves, rows, rank = basis.shape
    copies = []
    for leaf in range(leaves):
        group = outer_first(core, leaf // 2, 4)
        inside = jnp.minimum(group, 1) * 256 + (leaf % 2) * rank
        back = ret_ref[pl.ds(pl.multiple_of(inside, 128), rank), :].astype(jnp.float32)
        down0 = pot_ref[leaf * rank : (leaf + 1) * rank, :] + jnp.where(group < 2, back, 0.0)
        own = slice(leaf * rows, (leaf + 1) * rows)
        result = near_ref[own, :] + mm(basis[leaf], down0.astype(jnp.bfloat16))
        out_ref[own, :] = result.astype(jnp.bfloat16)
        if leaf % 4 == 3:
            done = pl.ds((leaf - 3) * rows, 4 * rows)
            copy = pltpu.make_async_copy(out_ref.at[done], out_hbm.at[done], sems.at[leaf // 4])
            copy.start()
            copies.append(copy)
    for copy in copies:
        copy.wait()


def call(kernel, outs, args, spaces, scratch=(), us=1.0, name=None, out_space=VMEM, after=()):
    kinds = {"v": VMEM, "h": HBM, "a": pl.ANY}
    n, skip = len(args), len(after)

    def body(*refs):
        kernel(*refs[:n], *refs[n + skip :])

    args = list(args) + list(after)
    spaces = spaces + "a" * skip
    args = [
        pltpu.with_memory_space_constraint(a, HBM) if k == "h" else a for a, k in zip(args, spaces)
    ]
    return pl.pallas_call(
        body,
        out_shape=outs,
        in_specs=[pl.BlockSpec(memory_space=kinds[k]) for k in spaces],
        out_specs=[pl.BlockSpec(memory_space=out_space)] * len(outs),
        scratch_shapes=list(scratch),
        compiler_params=pltpu.CompilerParams(vmem_limit_bytes=LIMIT),
        cost_estimate=pl.CostEstimate(flops=int(us * 1.15e9), bytes_accessed=0, transcendentals=0),
        name=name,
    )(*args)


def like(array, space=None):
    return (space or VMEM)(array.shape, array.dtype)


def per_device(
    points, weights, leaf_basis, leaf_transfer, node_transfer, leaf_skeleton, node_skeleton,
    upper_skeleton, leaf_far, leaf_count, node_far, node_count, upper_far, upper_count,
):
    leaves, rows, rank = leaf_basis.shape
    features = points.shape[1]
    cols = weights.shape[1]
    total = lax.axis_size("leaf")
    width = features + cols
    bf16, f32 = jnp.bfloat16, jnp.float32
    across = [(d, d ^ 1) for d in range(total)]
    outward = [(d, (d + 1) % total if d % 2 else (d - 1) % total) for d in range(total)]
    shape = jax.ShapeDtypeStruct
    sems = pltpu.SemaphoreType.DMA
    bind = functools.partial
    rows_scratch = pltpu.VMEM((leaves // 2, leaves, 256), f32)
    node_rows = pltpu.VMEM((2, 2, 256), f32)
    pot_shape = shape((leaves * rank, cols), f32)

    pack, rim, mask, us_v = call(
        bind(front_kernel, total=total),
        [
            shape((leaves * rank + 3 * rank, width), bf16),
            shape((4 * rank + 16, width), bf16),
            shape((24, 128), f32),
            shape(upper_skeleton.shape, upper_skeleton.dtype),
        ],
        [points, weights, leaf_basis, leaf_transfer, node_transfer, leaf_skeleton, node_skeleton,
         leaf_far, leaf_count, upper_skeleton],
        "hhhhhhhhhh",
        [like(points), like(weights), like(leaf_basis), like(leaf_transfer), like(node_transfer),
         like(leaf_skeleton), like(node_skeleton), like(leaf_far), like(leaf_count, SMEM),
         sems((13,))],
        name="front", us=2.5,
    )
    rim_in = lax.ppermute(rim, "leaf", outward)
    side = lax.ppermute(pack, "leaf", across)
    near, node_mask = call(
        bind(near_kernel, rows=rows, total=total),
        [shape((leaves * rows, cols), f32), shape((32, 128), f32)],
        [points, weights, upper_far, node_far, node_count, upper_count], "vvvhhh",
        [like(node_far), like(node_count, SMEM), like(upper_count, SMEM), sems((3,))],
        name="near", us=1.7,
    )
    (nodes,) = call(
        bind(upper_kernel, total=total),
        [shape((5 * rank, width), bf16)],
        [pack, side, us_v], "vvv",
        [pltpu.VMEM((4 * rank, rank), bf16)],
        name="upper", us=0.3, after=[node_mask],
    )
    nodes_b = lax.ppermute(nodes, "leaf", outward)
    pot, col = call(
        bind(own_kernel, total=total), [pot_shape, shape((leaves * rank, 128), f32)],
        [pack, mask], "vv", [rows_scratch, pltpu.VMEM((1024, 1024), bf16)],
        name="own", us=1.7, after=[nodes],
    )
    (ret,) = call(
        bind(back_kernel, total=total), [shape((4 * rank, cols), bf16)], [pack, rim_in, col],
        "vvv", [rows_scratch], name="back", us=1.3,
    )
    ret_in = lax.ppermute(ret, "leaf", outward)
    (pot,) = call(
        bind(side_kernel, total=total), [pot_shape], [pack, side, mask, col, pot], "vvvvv",
        [rows_scratch, pltpu.VMEM((1024, 1024), bf16)], name="side", us=0.1, after=[ret],
    )
    (pot,) = call(
        bind(rim_kernel, total=total), [pot_shape], [pack, rim_in, mask, col, pot], "vvvvv",
        [rows_scratch, pltpu.VMEM((1024, 512), bf16)], name="rim", us=0.1,
    )
    nodes_b, pot = lax.optimization_barrier((nodes_b, pot))
    nodes_a = lax.ppermute(nodes_b, "leaf", across)
    far1, far2 = call(
        bind(outer_node_kernel, total=total),
        [shape((2 * rank, cols), f32), shape((rank, cols), f32)],
        [nodes, nodes_b, node_mask], "vvv", [node_rows, node_rows],
        name="outer_node", us=0.1, after=[pot],
    )
    (pot,) = call(
        bind(node_kernel, total=total), [pot_shape],
        [nodes, nodes_a, node_mask, far1, far2, node_transfer, leaf_transfer, pot], "vvvvvvvv", [node_rows],
        name="node", us=0.1,
    )
    (out,) = call(
        bind(last_kernel, total=total),
        [shape((leaves * rows, cols), bf16)],
        [near, pot, ret_in, leaf_basis], "vvvv",
        [pltpu.VMEM((leaves * rows, cols), bf16), sems((2,))],
        name="last", us=1.9, out_space=HBM,
    )
    return out


def solution(mesh):
    placed = (
        P("leaf", None),
        P("leaf", "cols"),
        P("leaf", None, None),
        P("leaf", None, None),
        P("leaf", None, None),
        P("leaf", None),
        P("leaf", None),
        P(),
        P("leaf", None),
        P("leaf"),
        P("leaf", None),
        P("leaf"),
        P(),
        P(),
    )
    return jax.shard_map(
        per_device, mesh=mesh, in_specs=placed, out_specs=P("leaf", "cols"), check_vma=False
    )
```

```python
import functools
import math

import jax
import jax.numpy as jnp
from jax import lax
from jax.experimental import pallas as pl
from jax.experimental.pallas import tpu as pltpu
from jax.sharding import PartitionSpec as P

NEG = -1e38
VMEM = pltpu.VMEM
SMEM = pltpu.SMEM
HBM = pltpu.HBM
LIMIT = 12 * 1024 * 1024


def mm(a, b):
    return jnp.dot(a, b, preferred_element_type=jnp.float32)


def mm_nt(a, b):
    return lax.dot_general(a, b, (((1,), (1,)), ((), ())), preferred_element_type=jnp.float32)


def mm_tn(a, b):
    return lax.dot_general(a, b, (((0,), (0,)), ((), ())), preferred_element_type=jnp.float32)


def scale_of(features):
    return math.log2(math.e) / math.sqrt(8.0 * features)


def norm_col(pts):
    rows, features = pts.shape
    wide = pts.astype(jnp.float32)
    total = jnp.sum(wide * wide, axis=1, keepdims=True)
    return jnp.broadcast_to(scale_of(features) * (features - total), (rows, 128))


def norm_row(col, targets):
    return jnp.transpose(col)[0:targets]


def twice(col):
    return jnp.concatenate([col, col], axis=1)


def hits(far, counts, first):
    rows, slots = far.shape
    ids = lax.broadcasted_iota(jnp.int32, (rows, 128), 1) + first
    found = jnp.zeros((rows, 128), jnp.float32)
    for k in range(slots):
        same = (far[:, k : k + 1] == ids) & (counts > k)
        found = jnp.where(same, 1.0, found)
    return found


def count_column(count_ref, rows):
    spot = lax.broadcasted_iota(jnp.int32, (rows, 128), 0)
    column = jnp.zeros((rows, 128), jnp.int32)
    for t in range(rows):
        column = jnp.where(spot == t, count_ref[t], column)
    return column


def one_hot_rows(index_columns, at, choices):
    spots = lax.broadcasted_iota(jnp.int32, (index_columns.shape[0], choices), 1)
    same = index_columns[:, at : at + 1] == spots
    return jnp.where(same, 1.0, 0.0).astype(jnp.bfloat16)


def place(total):
    me = lax.axis_index("leaf")
    core = lax.rem(me, 2)
    chips = total // 2
    chip = me // 2
    step = 2 * core - 1
    side_b = lax.rem(chip + step + chips, chips)
    side_a = lax.rem(chip - step + chips, chips)
    return me, core, chip, side_a, side_b


def outer_first(core, group, groups):
    return group + core * (groups - 1 - 2 * group)


def fetch(pairs, sems):
    copies = [pltpu.make_async_copy(s, d, sems.at[i]) for i, (s, d) in enumerate(pairs)]
    for copy in copies:
        copy.start()
    return copies


def group_rows(at):
    return pl.ds(pl.multiple_of(at * 256, 256), 256)


def fill_rows(rows_ref, at, source, used_columns, targets):
    col = norm_col(source) if source.shape[1] != 128 else source
    for half in range(2):
        term = norm_row(col[half * 128 : half * 128 + 128], targets)
        lanes = slice(half * 128, half * 128 + 128)
        rows_ref[at, :, lanes] = jnp.where(used_columns[half] > 0.0, term, NEG)


def blocks(left, col, right, row_of):
    features = left.shape[1]
    inner = mm_nt(left, right)
    parts = []
    for at in range(left.shape[0] // 128):
        own = slice(at * 128, at * 128 + 128)
        power = inner[own] * (2.0 * scale_of(features)) + twice(col[own]) + row_of(at)
        parts.append(jnp.exp2(power).astype(jnp.bfloat16))
    return jnp.concatenate(parts, axis=0) if len(parts) > 1 else parts[0]


def tree_leaf(core, at):
    return outer_first(core, at // 2, 4) * 2 + at % 2


def front_kernel(
    points_hbm, weights_hbm, basis_hbm, lt_hbm, t_hbm, ls_hbm, ns_hbm, far_hbm, count_hbm, us_hbm,
    pack_ref, rim_ref, mask_ref, us,
    points, weights, basis, lt, t, ls, ns, far, count, sems, *, total,
):
    me, core, _, _, _ = place(total)
    leaves, rows, rank = basis.shape
    nodes = t.shape[0]
    features = points.shape[1]
    cols = weights.shape[1]
    small = [(ls_hbm, ls), (ns_hbm, ns), (far_hbm, far), (count_hbm, count), (us_hbm, us)]
    pairs = list(small)
    part = leaves // 2
    for half in range(2):
        own = pl.ds(half * part * rows, part * rows)
        some = pl.ds(half * part, part)
        pairs += [
            (points_hbm.at[own], points.at[own]),
            (weights_hbm.at[own], weights.at[own]),
            (basis_hbm.at[some], basis.at[some]),
        ]
    pairs += [(lt_hbm, lt), (t_hbm, t)]
    copies = fetch(pairs, sems)
    for copy in copies[: len(small)]:
        copy.wait()
    counts = count_column(count, leaves)
    for at, first in enumerate((me, me + 1 - 2 * core, lax.rem(me + 2 * core - 1 + total, total))):
        found = hits(far[...], counts, first * leaves)
        mask_ref[at * 8 : at * 8 + 8, :] = found
    rim_ref[512:528, :] = jnp.zeros((16, rim_ref.shape[1]), jnp.bfloat16)
    rim_ref[512:528, 0:128] = jnp.concatenate(
        [found, jnp.zeros((8, 128), jnp.float32)], axis=0
    ).astype(jnp.bfloat16)
    leaf_columns = jnp.transpose(ls[...])
    node_columns = jnp.transpose(jnp.concatenate([ns[...]] * 4, axis=0))
    groups = leaves // 2
    picked, charges = [], []
    base = leaves * rank
    for leaf in range(leaves):
        if leaf % part == 0:
            first = len(small) + 3 * (leaf // part)
            for copy in copies[first : first + 3]:
                copy.wait()
        own = slice(leaf * rows, (leaf + 1) * rows)
        skel = mm(one_hot_rows(leaf_columns, leaf, rows), points[own, :]).astype(jnp.bfloat16)
        charge = mm_tn(basis[leaf], weights[own, :]).astype(jnp.bfloat16)
        start = outer_first(core, leaf // 2, groups) * 256 + (leaf % 2) * rank
        here = pl.ds(pl.multiple_of(start, 128), rank)
        pack_ref[here, 0:features] = skel
        pack_ref[here, features:] = charge
        picked.append(skel)
        charges.append(charge)
    for copy in copies[len(small) + 6 :]:
        copy.wait()
    for node in range(nodes):
        own = slice(base + node * rank, base + (node + 1) * rank)
        kids = jnp.concatenate(picked[node * 4 : node * 4 + 4], axis=0)
        rows_hot = one_hot_rows(node_columns, node, 4 * rank)
        pack_ref[own, 0:features] = mm(rows_hot, kids).astype(jnp.bfloat16)
        transfer = lt[node * 4 : node * 4 + 4].reshape(4 * rank, rank)
        charge = mm_tn(transfer, jnp.concatenate(charges[node * 4 : node * 4 + 4], axis=0))
        pack_ref[own, features:] = charge.astype(jnp.bfloat16)
        last = slice(base + 2 * rank, base + 3 * rank)
        pack_ref[last, node * rank : (node + 1) * rank] = t[node]
    pack_ref[base + 2 * rank :, 2 * rank :] = jnp.zeros((rank, rank), jnp.bfloat16)
    rim_ref[0:512, :] = pack_ref[0:512, :]


def upper_kernel(own_ref, other_ref, us_ref, out_ref, transfers, *, total):
    _, core, chip, _, _ = place(total)
    cols = 128
    features = own_ref.shape[1] - cols
    base = own_ref.shape[0] - 384
    mine = pl.multiple_of(core * 256, 256)
    theirs = pl.multiple_of((1 - core) * 256, 256)
    for start, ref in ((mine, own_ref), (theirs, other_ref)):
        out_ref[pl.ds(start, 256), :] = ref[base : base + 256, :]
        transfers[pl.ds(start, 128), :] = ref[base + 256 : base + 384, 0:128]
        transfers[pl.ds(start + 128, 128), :] = ref[base + 256 : base + 384, 128:256]
    charge = mm_tn(transfers[...], out_ref[0:512, features:])
    out_ref[512:640, features:] = charge.astype(jnp.bfloat16)
    index = us_ref[pl.ds(chip, 1), :]
    columns = jnp.transpose(jnp.broadcast_to(index, (8, index.shape[1])))
    picked = mm(one_hot_rows(columns, 0, 512), out_ref[0:512, 0:features])
    out_ref[512:640, 0:features] = picked.astype(jnp.bfloat16)


def near_kernel(
    points, weights, ufar_hbm, nfar_hbm, ncount_hbm, ucount_hbm, out_ref, mask_ref,
    ufar, nfar, ncount, ucount, sems, *, rows, total,
):
    _, _, chip, side_a, side_b = place(total)
    copies = fetch(
        [(ufar_hbm, ufar), (nfar_hbm, nfar), (ncount_hbm, ncount), (ucount_hbm, ucount)], sems
    )
    features = points.shape[1]
    same = lax.broadcasted_iota(jnp.int32, (rows, rows), 0) == lax.broadcasted_iota(
        jnp.int32, (rows, rows), 1
    )
    for leaf in range(points.shape[0] // rows):
        own = slice(leaf * rows, (leaf + 1) * rows)
        pts = points[own, :]
        col = norm_col(pts)
        row = jnp.concatenate([norm_row(col[0:128], 1), norm_row(col[128:256], 1)], axis=1)
        power = mm_nt(pts, pts) * (2.0 * scale_of(features)) + twice(col) + row
        tile = jnp.exp2(jnp.where(same, NEG, power)).astype(jnp.bfloat16)
        out_ref[own, :] = mm(tile, weights[own, :])
    for copy in copies:
        copy.wait()
    ncounts = count_column(ncount, 2)
    for at, ident in enumerate((chip, side_b, side_a)):
        mask_ref[at * 8 : at * 8 + 2, :] = hits(nfar[...], ncounts, ident * 4)
    lists = ufar[...]
    live = ucount[chip]
    mine = lax.broadcasted_iota(jnp.int32, lists.shape, 1) == chip
    mine = mine & (lax.broadcasted_iota(jnp.int32, lists.shape, 0) < live)
    for at, ident in enumerate((side_b, side_a)):
        hit = jnp.where(mine & (lists == ident), 1.0, 0.0)
        used = jnp.max(jnp.max(hit, axis=0, keepdims=True), axis=1, keepdims=True)
        mask_ref[24 + at : 25 + at, :] = jnp.broadcast_to(used, (1, 128))


def own_kernel(pack_ref, mask_ref, pot_ref, col_ref, rows_ref, block_ref, *, total):
    _, core, _, _, _ = place(total)
    features = pack_ref.shape[1] - pot_ref.shape[1]
    found = mask_ref[0:8, :]
    col_ref[...] = norm_col(pack_ref[0:1024, 0:features])
    for tree in range(4):
        here = group_rows(outer_first(core, tree, 4))
        used = [found[:, 2 * tree + h : 2 * tree + h + 1] for h in range(2)]
        fill_rows(rows_ref, tree, col_ref[here, :], used, 8)
    left = pack_ref[0:1024, 0:features]
    for source in range(4):
        src = outer_first(core, source, 4)
        here = slice(source * 256, source * 256 + 256)
        block_ref[:, here] = blocks(
            left, col_ref[...], pack_ref[here, 0:features],
            lambda at: rows_ref[src, pl.ds(tree_leaf(core, at), 1), :],
        )
    pot_ref[...] = mm(block_ref[...], pack_ref[0:1024, features:])


def side_kernel(
    pack_ref, side_ref, mask_ref, col_ref, start_ref, pot_ref, rows_ref, block_ref, *, total
):
    _, core, _, _, _ = place(total)
    features = pack_ref.shape[1] - pot_ref.shape[1]
    found = mask_ref[8:16, :]
    for tree in range(4):
        here = group_rows(outer_first(1 - core, tree, 4))
        used = [found[:, 2 * tree + h : 2 * tree + h + 1] for h in range(2)]
        fill_rows(rows_ref, tree, side_ref[here, 0:features], used, 8)
    for source in range(4):
        src = outer_first(1 - core, source, 4)
        here = slice(source * 256, source * 256 + 256)
        first = 3 - source
        block_ref[first * 256 :, here] = blocks(
            pack_ref[first * 256 : 1024, 0:features], col_ref[first * 256 :, :],
            side_ref[here, 0:features],
            lambda at: rows_ref[src, pl.ds(tree_leaf(core, at + 2 * first), 1), :],
        )
    for group in range(4):
        own = slice(group * 256, group * 256 + 256)
        span = slice((3 - group) * 256, 1024)
        pot_ref[own, :] = start_ref[own, :] + mm(block_ref[own, span], side_ref[span, features:])


def back_kernel(pack_ref, rim_ref, col_ref, ret_ref, rows_ref, *, total):
    _, core, _, _, _ = place(total)
    features = pack_ref.shape[1] - ret_ref.shape[1]
    found = rim_ref[512:528, 0:128].astype(jnp.float32)[0:8, :]
    left = rim_ref[0:512, 0:features]
    col = norm_col(left)
    parts = []
    for source in (2, 3):
        used = []
        for half in range(2):
            one = found[:, 2 * source + half : 2 * source + half + 1]
            other = found[:, 2 * (3 - source) + half : 2 * (3 - source) + half + 1]
            used.append(jnp.where(core == 0, one, other))
        here = slice(source * 256, source * 256 + 256)
        fill_rows(rows_ref, source, col_ref[here, :], used, 8)
        rows = 512 if source == 2 else 256
        parts.append(
            blocks(
                left[0:rows], col[0:rows], pack_ref[here, 0:features],
                lambda at: rows_ref[source, pl.ds(tree_leaf(1 - core, at), 1), :],
            )
        )
    both = jnp.concatenate([parts[0][0:256], parts[1]], axis=1)
    ret_ref[0:256, :] = mm(both, pack_ref[512:1024, features:]).astype(jnp.bfloat16)
    ret_ref[256:512, :] = mm(parts[0][256:512], pack_ref[512:768, features:]).astype(jnp.bfloat16)


def rim_kernel(
    pack_ref, rim_ref, mask_ref, col_ref, start_ref, pot_ref, rows_ref, block_ref, *, total
):
    _, core, _, _, _ = place(total)
    features = pack_ref.shape[1] - pot_ref.shape[1]
    found = mask_ref[16:24, :]
    for source in range(2):
        used = []
        for half in range(2):
            zero = found[:, 2 * source + half : 2 * source + half + 1]
            one = found[:, 2 * (3 - source) + half : 2 * (3 - source) + half + 1]
            used.append(jnp.where(core == 0, one, zero))
        here = slice(source * 256, source * 256 + 256)
        fill_rows(rows_ref, source, rim_ref[here, 0:features], used, 8)
        stop = 1024 - source * 256
        block_ref[0:stop, here] = blocks(
            pack_ref[0:stop, 0:features], col_ref[0:stop, :], rim_ref[here, 0:features],
            lambda at: rows_ref[source, pl.ds(tree_leaf(core, at), 1), :],
        )
    pot_ref[0:768, :] = start_ref[0:768, :] + mm(block_ref[0:768, :], rim_ref[0:512, features:])
    pot_ref[768:, :] = start_ref[768:, :] + mm(block_ref[768:, 0:256], rim_ref[0:256, features:])


def node_part(nodes_ref, ref, mask, core, rows_ref, features):
    own = nodes_ref[group_rows(core), 0:features]
    col = norm_col(own)
    parts = []
    for source in range(2):
        here = slice(source * 256, source * 256 + 256)
        used = [mask[:, 2 * source + h : 2 * source + h + 1] for h in range(2)]
        fill_rows(rows_ref, source, ref[here, 0:features], used, 2)
        parts.append(
            blocks(
                own, col, ref[here, 0:features], lambda at: rows_ref[source, at : at + 1, :]
            )
        )
    return mm(jnp.concatenate(parts, axis=1), ref[0:512, features:])


def upper_part(nodes_ref, ref, used, features):
    own = nodes_ref[512:640, 0:features]
    source = ref[512:640, 0:features]
    row = jnp.where(used > 0.0, norm_row(norm_col(source), 1), NEG)
    power = mm_nt(own, source) * (2.0 * scale_of(features)) + norm_col(own) + row
    return mm(jnp.exp2(power).astype(jnp.bfloat16), ref[512:640, features:])


def outer_node_kernel(
    nodes_ref, side_b_ref, mask_ref, far1_ref, far2_ref, rows_own, rows_ref, *, total
):
    _, core, _, _, _ = place(total)
    features = nodes_ref.shape[1] - far1_ref.shape[1]
    far2_ref[...] = upper_part(nodes_ref, side_b_ref, mask_ref[24:25, :], features)
    far1_ref[...] = node_part(
        nodes_ref, nodes_ref, mask_ref[0:2, :], core, rows_own, features
    ) + node_part(nodes_ref, side_b_ref, mask_ref[8:10, :], core, rows_ref, features)


def merge_kernel(pot_ref, ret_ref, out_ref, *, total):
    _, core, _, _, _ = place(total)
    for group in range(4):
        own = slice(group * 256, group * 256 + 256)
        part = pot_ref[own, :]
        if group < 2:
            part = part + ret_ref[own, :].astype(jnp.float32)
        out_ref[group_rows(outer_first(core, group, 4)), :] = part


def final_kernel(
    nodes_ref, side_a_ref, mask_ref, far1_ref, far2_ref, t, lt, pot_ref, near_ref, basis,
    out_hbm, rows_ref, out_ref, sems, *, total,
):
    _, core, _, _, _ = place(total)
    features = nodes_ref.shape[1] - pot_ref.shape[1]
    leaves, rows, rank = basis.shape
    far2 = far2_ref[...] + upper_part(nodes_ref, side_a_ref, mask_ref[25:26, :], features)
    far1 = far1_ref[...] + node_part(
        nodes_ref, side_a_ref, mask_ref[16:18, :], core, rows_ref, features
    )
    down2 = far2.astype(jnp.bfloat16)
    down1 = (far1 + mm(t[...].reshape(2 * rank, rank), down2)).astype(jnp.bfloat16)
    down0 = []
    for node in range(2):
        own = slice(node * 4 * rank, (node + 1) * 4 * rank)
        transfer = lt[node * 4 : node * 4 + 4].reshape(4 * rank, rank)
        lower = pot_ref[own, :] + mm(transfer, down1[node * rank : (node + 1) * rank])
        down0.append(lower.astype(jnp.bfloat16))
    copies = []
    for node in range(2):
        results = []
        for leaf in range(4):
            at = node * 4 + leaf
            lower = down0[node][leaf * rank : (leaf + 1) * rank]
            own = slice(at * rows, (at + 1) * rows)
            results.append((near_ref[own, :] + mm(basis[at], lower)).astype(jnp.bfloat16))
        for leaf in range(4):
            at = node * 4 + leaf
            out_ref[at * rows : (at + 1) * rows, :] = results[leaf]
        done = pl.ds(node * 4 * rows, 4 * rows)
        copy = pltpu.make_async_copy(out_ref.at[done], out_hbm.at[done], sems.at[node])
        copy.start()
        copies.append(copy)
    for copy in copies:
        copy.wait()


def call(kernel, outs, args, spaces, scratch=(), us=1.0, name=None, out_space=VMEM, after=(), early=()):
    kinds = {"v": VMEM, "h": HBM, "a": pl.ANY}
    n, skip = len(args), len(after) + len(early)

    def body(*refs):
        kernel(*refs[:n], *refs[n + skip :])

    args = list(args) + list(after) + list(early)
    spaces = spaces + "a" * len(after) + "v" * len(early)
    args = [
        pltpu.with_memory_space_constraint(a, HBM) if k == "h" else a for a, k in zip(args, spaces)
    ]
    return pl.pallas_call(
        body,
        out_shape=outs,
        in_specs=[pl.BlockSpec(memory_space=kinds[k]) for k in spaces],
        out_specs=[pl.BlockSpec(memory_space=out_space)] * len(outs),
        scratch_shapes=list(scratch),
        compiler_params=pltpu.CompilerParams(vmem_limit_bytes=LIMIT),
        cost_estimate=pl.CostEstimate(flops=int(us * 1.15e9), bytes_accessed=0, transcendentals=0),
        name=name,
    )(*args)


def like(array, space=None):
    return (space or VMEM)(array.shape, array.dtype)


def per_device(
    points, weights, leaf_basis, leaf_transfer, node_transfer, leaf_skeleton, node_skeleton,
    upper_skeleton, leaf_far, leaf_count, node_far, node_count, upper_far, upper_count,
):
    leaves, rows, rank = leaf_basis.shape
    features = points.shape[1]
    cols = weights.shape[1]
    total = lax.axis_size("leaf")
    width = features + cols
    bf16, f32 = jnp.bfloat16, jnp.float32
    across = [(d, d ^ 1) for d in range(total)]
    outward = [(d, (d + 1) % total if d % 2 else (d - 1) % total) for d in range(total)]
    shape = jax.ShapeDtypeStruct
    sems = pltpu.SemaphoreType.DMA
    bind = functools.partial
    rows_scratch = pltpu.VMEM((leaves // 2, leaves, 256), f32)
    node_rows = pltpu.VMEM((2, 2, 256), f32)
    pot_shape = shape((leaves * rank, cols), f32)

    pack, rim, mask, us_v = call(
        bind(front_kernel, total=total),
        [
            shape((leaves * rank + 3 * rank, width), bf16),
            shape((4 * rank + 16, width), bf16),
            shape((24, 128), f32),
            shape(upper_skeleton.shape, upper_skeleton.dtype),
        ],
        [points, weights, leaf_basis, leaf_transfer, node_transfer, leaf_skeleton, node_skeleton,
         leaf_far, leaf_count, upper_skeleton],
        "hhhhhhhhhh",
        [like(points), like(weights), like(leaf_basis), like(leaf_transfer), like(node_transfer),
         like(leaf_skeleton), like(node_skeleton), like(leaf_far), like(leaf_count, SMEM),
         sems((13,))],
        name="front", us=2.5,
    )
    rim_in = lax.ppermute(rim, "leaf", outward)
    side = lax.ppermute(pack, "leaf", across)
    pot, col = call(
        bind(own_kernel, total=total), [pot_shape, shape((leaves * rank, 128), f32)],
        [pack, mask], "vv", [rows_scratch, pltpu.VMEM((1024, 1024), bf16)],
        name="own", us=1.7,
    )
    (nodes,) = call(
        bind(upper_kernel, total=total),
        [shape((5 * rank, width), bf16)],
        [pack, side, us_v], "vvv",
        [pltpu.VMEM((4 * rank, rank), bf16)],
        name="upper", us=0.3, after=[col],
    )
    nodes_b = lax.ppermute(nodes, "leaf", outward)
    upper_lists = jnp.transpose(upper_far)
    near, node_mask = call(
        bind(near_kernel, rows=rows, total=total),
        [shape((leaves * rows, cols), f32), shape((32, 128), f32)],
        [points, weights, upper_lists, node_far, node_count, upper_count], "vvhhhh",
        [like(upper_lists), like(node_far), like(node_count, SMEM), like(upper_count, SMEM), sems((4,))],
        name="near", us=1.7, after=[nodes],
    )
    (ret,) = call(
        bind(back_kernel, total=total), [shape((4 * rank, cols), bf16)], [pack, rim_in, col],
        "vvv", [rows_scratch], name="back", us=1.3, after=[node_mask],
    )
    ret_in = lax.ppermute(ret, "leaf", outward)
    (pot,) = call(
        bind(side_kernel, total=total), [pot_shape], [pack, side, mask, col, pot], "vvvvv",
        [rows_scratch, pltpu.VMEM((1024, 1024), bf16)], name="side", us=0.1, after=[ret],
    )
    (pot,) = call(
        bind(rim_kernel, total=total), [pot_shape], [pack, rim_in, mask, col, pot], "vvvvv",
        [rows_scratch, pltpu.VMEM((1024, 512), bf16)], name="rim", us=0.1, early=[leaf_basis, leaf_transfer, node_transfer],
    )
    nodes_b, pot = lax.optimization_barrier((nodes_b, pot))
    nodes_a = lax.ppermute(nodes_b, "leaf", across)
    far1, far2 = call(
        bind(outer_node_kernel, total=total),
        [shape((2 * rank, cols), f32), shape((rank, cols), f32)],
        [nodes, nodes_b, node_mask], "vvv", [node_rows, node_rows],
        name="outer_node", us=0.1, after=[pot],
    )
    (pot,) = call(
        bind(merge_kernel, total=total), [pot_shape], [pot, ret_in], "vv", name="merge", us=5.0,
        after=[far2],
    )
    (out,) = call(
        bind(final_kernel, total=total),
        [shape((leaves * rows, cols), bf16)],
        [nodes, nodes_a, node_mask, far1, far2, node_transfer, leaf_transfer, pot, near,
         leaf_basis],
        "vvvvvvvvvv",
        [node_rows, pltpu.VMEM((leaves * rows, cols), bf16), sems((2,))],
        name="final", us=1.9, out_space=HBM,
    )
    return out


def solution(mesh):
    placed = (
        P("leaf", None),
        P("leaf", "cols"),
        P("leaf", None, None),
        P("leaf", None, None),
        P("leaf", None, None),
        P("leaf", None),
        P("leaf", None),
        P(),
        P("leaf", None),
        P("leaf"),
        P("leaf", None),
        P("leaf"),
        P(),
        P(),
    )
    return jax.shard_map(
        per_device, mesh=mesh, in_specs=placed, out_specs=P("leaf", "cols"), check_vma=False
    )
```

```python
import functools
import math

import jax
import jax.numpy as jnp
from jax import lax
from jax.experimental import pallas as pl
from jax.experimental.pallas import tpu as pltpu
from jax.sharding import PartitionSpec as P

NEG = -1e38
VMEM = pltpu.VMEM
SMEM = pltpu.SMEM
HBM = pltpu.HBM
LIMIT = 12 * 1024 * 1024


def mm(a, b):
    return jnp.dot(a, b, preferred_element_type=jnp.float32)


def mm_nt(a, b):
    return lax.dot_general(a, b, (((1,), (1,)), ((), ())), preferred_element_type=jnp.float32)


def mm_tn(a, b):
    return lax.dot_general(a, b, (((0,), (0,)), ((), ())), preferred_element_type=jnp.float32)


def scale_of(features):
    return math.log2(math.e) / math.sqrt(8.0 * features)


def norm_col(pts):
    rows, features = pts.shape
    wide = pts.astype(jnp.float32)
    total = jnp.sum(wide * wide, axis=1, keepdims=True)
    return jnp.broadcast_to(scale_of(features) * (features - total), (rows, 128))


def norm_row(col, targets):
    return jnp.transpose(col)[0:targets]


def twice(col):
    return jnp.concatenate([col, col], axis=1)


def hits(far, counts, first):
    rows, slots = far.shape
    ids = lax.broadcasted_iota(jnp.int32, (rows, 128), 1) + first
    found = jnp.zeros((rows, 128), jnp.float32)
    for k in range(slots):
        same = (far[:, k : k + 1] == ids) & (counts > k)
        found = jnp.where(same, 1.0, found)
    return found


def count_column(count_ref, rows):
    spot = lax.broadcasted_iota(jnp.int32, (rows, 128), 0)
    column = jnp.zeros((rows, 128), jnp.int32)
    for t in range(rows):
        column = jnp.where(spot == t, count_ref[t], column)
    return column


def one_hot_rows(index_columns, at, choices):
    spots = lax.broadcasted_iota(jnp.int32, (index_columns.shape[0], choices), 1)
    same = index_columns[:, at : at + 1] == spots
    return jnp.where(same, 1.0, 0.0).astype(jnp.bfloat16)


def place(total):
    me = lax.axis_index("leaf")
    core = lax.rem(me, 2)
    chips = total // 2
    chip = me // 2
    step = 2 * core - 1
    side_b = lax.rem(chip + step + chips, chips)
    side_a = lax.rem(chip - step + chips, chips)
    return me, core, chip, side_a, side_b


def outer_first(core, group, groups):
    return group + core * (groups - 1 - 2 * group)


def fetch(pairs, sems):
    copies = [pltpu.make_async_copy(s, d, sems.at[i]) for i, (s, d) in enumerate(pairs)]
    for copy in copies:
        copy.start()
    return copies


def group_rows(at):
    return pl.ds(pl.multiple_of(at * 256, 256), 256)


def fill_rows(rows_ref, at, source, used_columns, targets):
    col = norm_col(source) if source.shape[1] != 128 else source
    for half in range(2):
        term = norm_row(col[half * 128 : half * 128 + 128], targets)
        lanes = slice(half * 128, half * 128 + 128)
        rows_ref[at, :, lanes] = jnp.where(used_columns[half] > 0.0, term, NEG)


def blocks(left, col, right, row_of):
    features = left.shape[1]
    inner = mm_nt(left, right)
    parts = []
    for at in range(left.shape[0] // 128):
        own = slice(at * 128, at * 128 + 128)
        power = inner[own] * (2.0 * scale_of(features)) + twice(col[own]) + row_of(at)
        parts.append(jnp.exp2(power).astype(jnp.bfloat16))
    return jnp.concatenate(parts, axis=0) if len(parts) > 1 else parts[0]


def tree_leaf(core, at):
    return outer_first(core, at // 2, 4) * 2 + at % 2


def front_kernel(
    points_hbm, weights_hbm, basis_hbm, lt_hbm, t_hbm, ls_hbm, ns_hbm, far_hbm, count_hbm, us_hbm,
    pack_ref, rim_ref, mask_ref, us,
    points, weights, basis, lt, t, ls, ns, far, count, sems, *, total,
):
    me, core, _, _, _ = place(total)
    leaves, rows, rank = basis.shape
    nodes = t.shape[0]
    features = points.shape[1]
    cols = weights.shape[1]
    small = [(ls_hbm, ls), (ns_hbm, ns), (far_hbm, far), (count_hbm, count), (us_hbm, us)]
    pairs = small + [(lt_hbm, lt), (t_hbm, t)]
    ahead = len(pairs)
    part = leaves // 2
    for half in range(2):
        own = pl.ds(half * part * rows, part * rows)
        some = pl.ds(half * part, part)
        pairs += [
            (points_hbm.at[own], points.at[own]),
            (weights_hbm.at[own], weights.at[own]),
            (basis_hbm.at[some], basis.at[some]),
        ]
    copies = fetch(pairs, sems)
    for copy in copies[: len(small)]:
        copy.wait()
    counts = count_column(count, leaves)
    for at, first in enumerate((me, me + 1 - 2 * core, lax.rem(me + 2 * core - 1 + total, total))):
        found = hits(far[...], counts, first * leaves)
        mask_ref[at * 8 : at * 8 + 8, :] = found
    rim_ref[512:528, :] = jnp.zeros((16, rim_ref.shape[1]), jnp.bfloat16)
    rim_ref[512:528, 0:128] = jnp.concatenate(
        [found, jnp.zeros((8, 128), jnp.float32)], axis=0
    ).astype(jnp.bfloat16)
    leaf_columns = jnp.transpose(ls[...])
    node_columns = jnp.transpose(jnp.concatenate([ns[...]] * 4, axis=0))
    groups = leaves // 2
    picked, charges = [], []
    base = leaves * rank
    for leaf in range(leaves):
        if leaf % part == 0:
            first = ahead + 3 * (leaf // part)
            for copy in copies[first : first + 3]:
                copy.wait()
        own = slice(leaf * rows, (leaf + 1) * rows)
        skel = mm(one_hot_rows(leaf_columns, leaf, rows), points[own, :]).astype(jnp.bfloat16)
        charge = mm_tn(basis[leaf], weights[own, :]).astype(jnp.bfloat16)
        start = outer_first(core, leaf // 2, groups) * 256 + (leaf % 2) * rank
        here = pl.ds(pl.multiple_of(start, 128), rank)
        pack_ref[here, 0:features] = skel
        pack_ref[here, features:] = charge
        picked.append(skel)
        charges.append(charge)
    for copy in copies[len(small) : ahead]:
        copy.wait()
    for node in range(nodes):
        own = slice(base + node * rank, base + (node + 1) * rank)
        kids = jnp.concatenate(picked[node * 4 : node * 4 + 4], axis=0)
        rows_hot = one_hot_rows(node_columns, node, 4 * rank)
        pack_ref[own, 0:features] = mm(rows_hot, kids).astype(jnp.bfloat16)
        transfer = lt[node * 4 : node * 4 + 4].reshape(4 * rank, rank)
        charge = mm_tn(transfer, jnp.concatenate(charges[node * 4 : node * 4 + 4], axis=0))
        pack_ref[own, features:] = charge.astype(jnp.bfloat16)
        last = slice(base + 2 * rank, base + 3 * rank)
        pack_ref[last, node * rank : (node + 1) * rank] = t[node]
    pack_ref[base + 2 * rank :, 2 * rank :] = jnp.zeros((rank, rank), jnp.bfloat16)
    rim_ref[0:512, :] = pack_ref[0:512, :]


def upper_points(points, index):
    columns = jnp.transpose(jnp.broadcast_to(index, (8, index.shape[1])))
    return mm(one_hot_rows(columns, 0, 512), points).astype(jnp.bfloat16)


def node_points(ref, start, count):
    stop = start + count
    return jnp.concatenate([ref[start:stop, :], ref[512 + start : 512 + stop, :]], axis=1)


def upper_kernel(own_ref, other_ref, us_ref, out_ref, points_ref, transfers, *, total):
    _, core, chip, _, _ = place(total)
    base = own_ref.shape[0] - 384
    mine = pl.multiple_of(core * 256, 256)
    theirs = pl.multiple_of((1 - core) * 256, 256)
    for start, ref in ((mine, own_ref), (theirs, other_ref)):
        for chunk in range(3):
            lanes = slice(chunk * 128, chunk * 128 + 128)
            out_ref[pl.ds(chunk * 512 + start, 256), :] = ref[base : base + 256, lanes]
        transfers[pl.ds(start, 128), :] = ref[base + 256 : base + 384, 0:128]
        transfers[pl.ds(start + 128, 128), :] = ref[base + 256 : base + 384, 128:256]
    charge = mm_tn(transfers[...], out_ref[1024:1536, :])
    out_ref[1536:1664, :] = charge.astype(jnp.bfloat16)
    points_ref[...] = upper_points(node_points(out_ref, 0, 512), us_ref[pl.ds(chip, 1), :])


def near_kernel(
    points, weights, ufar_hbm, nfar_hbm, ncount_hbm, ucount_hbm, out_ref, mask_ref,
    ufar, nfar, ncount, ucount, sems, *, rows, total,
):
    _, _, chip, side_a, side_b = place(total)
    copies = fetch(
        [(ufar_hbm, ufar), (nfar_hbm, nfar), (ncount_hbm, ncount), (ucount_hbm, ucount)], sems
    )
    features = points.shape[1]
    same = lax.broadcasted_iota(jnp.int32, (rows, rows), 0) == lax.broadcasted_iota(
        jnp.int32, (rows, rows), 1
    )
    for leaf in range(points.shape[0] // rows):
        own = slice(leaf * rows, (leaf + 1) * rows)
        pts = points[own, :]
        col = norm_col(pts)
        row = jnp.concatenate([norm_row(col[0:128], 1), norm_row(col[128:256], 1)], axis=1)
        power = mm_nt(pts, pts) * (2.0 * scale_of(features)) + twice(col) + row
        tile = jnp.exp2(jnp.where(same, NEG, power)).astype(jnp.bfloat16)
        out_ref[own, :] = mm(tile, weights[own, :])
    for copy in copies:
        copy.wait()
    ncounts = count_column(ncount, 2)
    for at, ident in enumerate((chip, side_b, side_a)):
        mask_ref[at * 8 : at * 8 + 2, :] = hits(nfar[...], ncounts, ident * 4)
    lists = ufar[...]
    live = ucount[chip]
    mine = lax.broadcasted_iota(jnp.int32, lists.shape, 1) == chip
    mine = mine & (lax.broadcasted_iota(jnp.int32, lists.shape, 0) < live)
    for at, ident in enumerate((side_b, side_a)):
        hit = jnp.where(mine & (lists == ident), 1.0, 0.0)
        used = jnp.max(jnp.max(hit, axis=0, keepdims=True), axis=1, keepdims=True)
        mask_ref[24 + at : 25 + at, :] = jnp.broadcast_to(used, (1, 128))


def own_kernel(pack_ref, mask_ref, pot_ref, col_ref, rows_ref, block_ref, *, total):
    _, core, _, _, _ = place(total)
    features = pack_ref.shape[1] - pot_ref.shape[1]
    found = mask_ref[0:8, :]
    col_ref[...] = norm_col(pack_ref[0:1024, 0:features])
    for tree in range(4):
        here = group_rows(outer_first(core, tree, 4))
        used = [found[:, 2 * tree + h : 2 * tree + h + 1] for h in range(2)]
        fill_rows(rows_ref, tree, col_ref[here, :], used, 8)
    left = pack_ref[0:1024, 0:features]
    for source in range(4):
        src = outer_first(core, source, 4)
        here = slice(source * 256, source * 256 + 256)
        block_ref[:, here] = blocks(
            left, col_ref[...], pack_ref[here, 0:features],
            lambda at: rows_ref[src, pl.ds(tree_leaf(core, at), 1), :],
        )
    pot_ref[...] = mm(block_ref[...], pack_ref[0:1024, features:])


def side_work(core, pack_ref, side_ref, mask_ref, col_ref, start_ref, pot_ref, rows_ref, block_ref):
    features = pack_ref.shape[1] - pot_ref.shape[1]
    found = mask_ref[8:16, :]
    for tree in range(4):
        here = group_rows(outer_first(1 - core, tree, 4))
        used = [found[:, 2 * tree + h : 2 * tree + h + 1] for h in range(2)]
        fill_rows(rows_ref, tree, side_ref[here, 0:features], used, 8)
    for source in range(4):
        src = outer_first(1 - core, source, 4)
        here = slice(source * 256, source * 256 + 256)
        first = 3 - source
        block_ref[first * 256 :, here] = blocks(
            pack_ref[first * 256 : 1024, 0:features], col_ref[first * 256 :, :],
            side_ref[here, 0:features],
            lambda at: rows_ref[src, pl.ds(tree_leaf(core, at + 2 * first), 1), :],
        )
    for group in range(4):
        own = slice(group * 256, group * 256 + 256)
        span = slice((3 - group) * 256, 1024)
        pot_ref[own, :] = start_ref[own, :] + mm(block_ref[own, span], side_ref[span, features:])


def back_kernel(pack_ref, rim_ref, col_ref, ret_ref, rows_ref, *, total):
    _, core, _, _, _ = place(total)
    features = pack_ref.shape[1] - ret_ref.shape[1]
    found = rim_ref[512:528, 0:128].astype(jnp.float32)[0:8, :]
    left = rim_ref[0:512, 0:features]
    col = norm_col(left)
    parts = []
    for source in (2, 3):
        used = []
        for half in range(2):
            one = found[:, 2 * source + half : 2 * source + half + 1]
            other = found[:, 2 * (3 - source) + half : 2 * (3 - source) + half + 1]
            used.append(jnp.where(core == 0, one, other))
        here = slice(source * 256, source * 256 + 256)
        fill_rows(rows_ref, source, col_ref[here, :], used, 8)
        rows = 512 if source == 2 else 256
        parts.append(
            blocks(
                left[0:rows], col[0:rows], pack_ref[here, 0:features],
                lambda at: rows_ref[source, pl.ds(tree_leaf(1 - core, at), 1), :],
            )
        )
    both = jnp.concatenate([parts[0][0:256], parts[1]], axis=1)
    ret_ref[0:256, :] = mm(both, pack_ref[512:1024, features:]).astype(jnp.bfloat16)
    ret_ref[256:512, :] = mm(parts[0][256:512], pack_ref[512:768, features:]).astype(jnp.bfloat16)


def rim_work(core, pack_ref, rim_ref, mask_ref, col_ref, start_ref, pot_ref, rows_ref, block_ref):
    features = pack_ref.shape[1] - pot_ref.shape[1]
    found = mask_ref[16:24, :]
    for source in range(2):
        used = []
        for half in range(2):
            zero = found[:, 2 * source + half : 2 * source + half + 1]
            one = found[:, 2 * (3 - source) + half : 2 * (3 - source) + half + 1]
            used.append(jnp.where(core == 0, one, zero))
        here = slice(source * 256, source * 256 + 256)
        fill_rows(rows_ref, source, rim_ref[here, 0:features], used, 8)
        stop = 1024 - source * 256
        block_ref[0:stop, here] = blocks(
            pack_ref[0:stop, 0:features], col_ref[0:stop, :], rim_ref[here, 0:features],
            lambda at: rows_ref[source, pl.ds(tree_leaf(core, at), 1), :],
        )
    pot_ref[0:768, :] = start_ref[0:768, :] + mm(block_ref[0:768, 0:512], rim_ref[0:512, features:])
    pot_ref[768:, :] = start_ref[768:, :] + mm(block_ref[768:, 0:256], rim_ref[0:256, features:])


def early_kernel(
    work, pack_ref, other_ref, mask_ref, col_ref, start_ref, pot_ref, rows_ref, block_ref, *, total
):
    _, core, _, _, _ = place(total)

    @pl.when(core == 1)
    def _():
        work(core, pack_ref, other_ref, mask_ref, col_ref, start_ref, pot_ref, rows_ref, block_ref)

    @pl.when(core == 0)
    def _():
        pot_ref[...] = start_ref[...]


def late_kernel(
    pack_ref, side_ref, rim_ref, mask_ref, col_ref, start_ref, pot_ref, rows_ref, block_ref, *, total
):
    _, core, _, _, _ = place(total)
    rest = (mask_ref, col_ref)

    @pl.when(core == 0)
    def _():
        side_work(core, pack_ref, side_ref, *rest, start_ref, pot_ref, rows_ref, block_ref)
        rim_work(core, pack_ref, rim_ref, *rest, pot_ref, pot_ref, rows_ref, block_ref)

    @pl.when(core == 1)
    def _():
        pot_ref[...] = start_ref[...]


def node_part(own, ref, mask, rows_ref):
    col = norm_col(own)
    parts = []
    for source in range(2):
        pts = node_points(ref, source * 256, 256)
        used = [mask[:, 2 * source + h : 2 * source + h + 1] for h in range(2)]
        fill_rows(rows_ref, source, pts, used, 2)
        parts.append(blocks(own, col, pts, lambda at: rows_ref[source, at : at + 1, :]))
    return mm(jnp.concatenate(parts, axis=1), ref[1024:1536, :])


def own_nodes(ref, core):
    start = pl.multiple_of(core * 256, 256)
    both = [ref[pl.ds(start, 256), :], ref[pl.ds(start + 512, 256), :]]
    return jnp.concatenate(both, axis=1)


def upper_part(own, ref, index, used):
    source = upper_points(node_points(ref, 0, 512), index)
    row = jnp.where(used > 0.0, norm_row(norm_col(source), 1), NEG)
    power = mm_nt(own, source) * (2.0 * scale_of(own.shape[1])) + norm_col(own) + row
    return mm(jnp.exp2(power).astype(jnp.bfloat16), ref[1536:1664, :])


def outer_node_kernel(
    nodes_ref, upper_ref, side_b_ref, us_ref, mask_ref, far1_ref, far2_ref, rows_own, rows_ref,
    *, total,
):
    _, core, _, _, side_b = place(total)
    index = us_ref[pl.ds(side_b, 1), :]
    far2_ref[...] = upper_part(upper_ref[...], side_b_ref, index, mask_ref[24:25, :])
    own = own_nodes(nodes_ref, core)
    far1_ref[...] = node_part(own, nodes_ref, mask_ref[0:2, :], rows_own) + node_part(
        own, side_b_ref, mask_ref[8:10, :], rows_ref
    )


def merge_kernel(pot_ref, ret_ref, out_ref, *, total):
    _, core, _, _, _ = place(total)
    for group in range(4):
        own = slice(group * 256, group * 256 + 256)
        part = pot_ref[own, :]
        if group < 2:
            part = part + ret_ref[own, :].astype(jnp.float32)
        out_ref[group_rows(outer_first(core, group, 4)), :] = part


def final_kernel(
    nodes_ref, upper_ref, side_a_ref, us_ref, mask_ref, far1_ref, far2_ref, t, lt, pot_ref,
    near_ref, basis, out_hbm, rows_ref, out_ref, sems, *, total,
):
    _, core, _, side_a, _ = place(total)
    leaves, rows, rank = basis.shape
    index = us_ref[pl.ds(side_a, 1), :]
    far2 = far2_ref[...] + upper_part(upper_ref[...], side_a_ref, index, mask_ref[25:26, :])
    far1 = far1_ref[...] + node_part(
        own_nodes(nodes_ref, core), side_a_ref, mask_ref[16:18, :], rows_ref
    )
    down2 = far2.astype(jnp.bfloat16)
    down1 = (far1 + mm(t[...].reshape(2 * rank, rank), down2)).astype(jnp.bfloat16)
    down0 = []
    for node in range(2):
        own = slice(node * 4 * rank, (node + 1) * 4 * rank)
        transfer = lt[node * 4 : node * 4 + 4].reshape(4 * rank, rank)
        lower = pot_ref[own, :] + mm(transfer, down1[node * rank : (node + 1) * rank])
        down0.append(lower.astype(jnp.bfloat16))
    copies = []
    for node in range(2):
        results = []
        for leaf in range(4):
            at = node * 4 + leaf
            lower = down0[node][leaf * rank : (leaf + 1) * rank]
            own = slice(at * rows, (at + 1) * rows)
            results.append((near_ref[own, :] + mm(basis[at], lower)).astype(jnp.bfloat16))
        for leaf in range(4):
            at = node * 4 + leaf
            out_ref[at * rows : (at + 1) * rows, :] = results[leaf]
            if leaf % 2 == 1:
                done = pl.ds((at - 1) * rows, 2 * rows)
                copy = pltpu.make_async_copy(out_ref.at[done], out_hbm.at[done], sems.at[at // 2])
                copy.start()
                copies.append(copy)
    for copy in copies:
        copy.wait()


def call(kernel, outs, args, spaces, scratch=(), us=1.0, name=None, out_space=VMEM, after=(), early=()):
    kinds = {"v": VMEM, "h": HBM, "a": pl.ANY}
    n, skip = len(args), len(after) + len(early)

    def body(*refs):
        kernel(*refs[:n], *refs[n + skip :])

    args = list(args) + list(after) + list(early)
    spaces = spaces + "a" * len(after) + "v" * len(early)
    args = [
        pltpu.with_memory_space_constraint(a, HBM) if k == "h" else a for a, k in zip(args, spaces)
    ]
    return pl.pallas_call(
        body,
        out_shape=outs,
        in_specs=[pl.BlockSpec(memory_space=kinds[k]) for k in spaces],
        out_specs=[pl.BlockSpec(memory_space=out_space)] * len(outs),
        scratch_shapes=list(scratch),
        compiler_params=pltpu.CompilerParams(vmem_limit_bytes=LIMIT),
        cost_estimate=pl.CostEstimate(flops=int(us * 1.15e9), bytes_accessed=0, transcendentals=0),
        name=name,
    )(*args)


def like(array, space=None):
    return (space or VMEM)(array.shape, array.dtype)


def per_device(
    points, weights, leaf_basis, leaf_transfer, node_transfer, leaf_skeleton, node_skeleton,
    upper_skeleton, leaf_far, leaf_count, node_far, node_count, upper_far, upper_count,
):
    leaves, rows, rank = leaf_basis.shape
    features = points.shape[1]
    cols = weights.shape[1]
    total = lax.axis_size("leaf")
    width = features + cols
    bf16, f32 = jnp.bfloat16, jnp.float32
    across = [(d, d ^ 1) for d in range(total)]
    outward = [(d, (d + 1) % total if d % 2 else (d - 1) % total) for d in range(total)]
    shape = jax.ShapeDtypeStruct
    sems = pltpu.SemaphoreType.DMA
    bind = functools.partial
    rows_scratch = pltpu.VMEM((leaves // 2, leaves, 256), f32)
    node_rows = pltpu.VMEM((2, 2, 256), f32)
    pot_shape = shape((leaves * rank, cols), f32)

    pack, rim, mask, us_v = call(
        bind(front_kernel, total=total),
        [
            shape((leaves * rank + 3 * rank, width), bf16),
            shape((4 * rank + 16, width), bf16),
            shape((24, 128), f32),
            shape(upper_skeleton.shape, upper_skeleton.dtype),
        ],
        [points, weights, leaf_basis, leaf_transfer, node_transfer, leaf_skeleton, node_skeleton,
         leaf_far, leaf_count, upper_skeleton],
        "hhhhhhhhhh",
        [like(points), like(weights), like(leaf_basis), like(leaf_transfer), like(node_transfer),
         like(leaf_skeleton), like(node_skeleton), like(leaf_far), like(leaf_count, SMEM),
         sems((13,))],
        name="front", us=2.5,
    )
    rim_in = lax.ppermute(rim, "leaf", outward)
    side = lax.ppermute(pack, "leaf", across)
    nodes, upper = call(
        bind(upper_kernel, total=total),
        [shape((13 * rank, cols), bf16), shape((rank, features), bf16)],
        [pack, side, us_v], "vvv",
        [pltpu.VMEM((4 * rank, rank), bf16)],
        name="upper", us=0.3,
    )
    nodes_b = lax.ppermute(nodes, "leaf", outward)
    pot, col = call(
        bind(own_kernel, total=total), [pot_shape, shape((leaves * rank, 128), f32)],
        [pack, mask], "vv", [rows_scratch, pltpu.VMEM((1024, 1024), bf16)],
        name="own", us=1.7, after=[nodes],
    )
    upper_lists = jnp.transpose(upper_far)
    near, node_mask = call(
        bind(near_kernel, rows=rows, total=total),
        [shape((leaves * rows, cols), f32), shape((32, 128), f32)],
        [points, weights, upper_lists, node_far, node_count, upper_count], "vvhhhh",
        [like(upper_lists), like(node_far), like(node_count, SMEM), like(upper_count, SMEM), sems((4,))],
        name="near", us=1.7, after=[col],
    )
    far_scratch = [rows_scratch, pltpu.VMEM((1024, 1024), bf16)]
    (pot,) = call(
        bind(early_kernel, side_work, total=total), [pot_shape], [pack, side, mask, col, pot],
        "vvvvv", far_scratch, name="side", us=1.3, after=[node_mask],
    )
    (ret,) = call(
        bind(back_kernel, total=total), [shape((4 * rank, cols), bf16)], [pack, rim_in, col],
        "vvv", [rows_scratch], name="back", us=1.3, after=[pot],
    )
    ret_in = lax.ppermute(ret, "leaf", outward)
    (pot,) = call(
        bind(early_kernel, rim_work, total=total), [pot_shape], [pack, rim_in, mask, col, pot],
        "vvvvv", far_scratch, name="rim", us=0.1, after=[ret],
        early=[leaf_basis, leaf_transfer, node_transfer],
    )
    nodes_b, pot = lax.optimization_barrier((nodes_b, pot))
    nodes_a = lax.ppermute(nodes_b, "leaf", across)
    (pot,) = call(
        bind(late_kernel, total=total), [pot_shape], [pack, side, rim_in, mask, col, pot],
        "vvvvvv", far_scratch, name="late", us=0.1,
    )
    far1, far2 = call(
        bind(outer_node_kernel, total=total),
        [shape((2 * rank, cols), f32), shape((rank, cols), f32)],
        [nodes, upper, nodes_b, us_v, node_mask], "vvvvv", [node_rows, node_rows],
        name="outer_node", us=0.1, after=[pot],
    )
    (pot,) = call(
        bind(merge_kernel, total=total), [pot_shape], [pot, ret_in], "vv", name="merge", us=5.0,
        after=[far2],
    )
    (out,) = call(
        bind(final_kernel, total=total),
        [shape((leaves * rows, cols), bf16)],
        [nodes, upper, nodes_a, us_v, node_mask, far1, far2, node_transfer, leaf_transfer, pot,
         near, leaf_basis],
        "vvvvvvvvvvvv",
        [node_rows, pltpu.VMEM((leaves * rows, cols), bf16), sems((4,))],
        name="final", us=1.9, out_space=HBM,
    )
    return out


def solution(mesh):
    placed = (
        P("leaf", None),
        P("leaf", "cols"),
        P("leaf", None, None),
        P("leaf", None, None),
        P("leaf", None, None),
        P("leaf", None),
        P("leaf", None),
        P(),
        P("leaf", None),
        P("leaf"),
        P("leaf", None),
        P("leaf"),
        P(),
        P(),
    )
    return jax.shard_map(
        per_device, mesh=mesh, in_specs=placed, out_specs=P("leaf", "cols"), check_vma=False
    )
```

```python
import functools
import math

import jax
import jax.numpy as jnp
from jax import lax
from jax.experimental import pallas as pl
from jax.experimental.pallas import tpu as pltpu
from jax.sharding import PartitionSpec as P

NEG = -1e38
VMEM = pltpu.VMEM
SMEM = pltpu.SMEM
HBM = pltpu.HBM
LIMIT = 12 * 1024 * 1024


def mm(a, b):
    return jnp.dot(a, b, preferred_element_type=jnp.float32)


def mm_nt(a, b):
    return lax.dot_general(a, b, (((1,), (1,)), ((), ())), preferred_element_type=jnp.float32)


def mm_tn(a, b):
    return lax.dot_general(a, b, (((0,), (0,)), ((), ())), preferred_element_type=jnp.float32)


def scale_of(features):
    return math.log2(math.e) / math.sqrt(8.0 * features)


def norm_col(pts):
    rows, features = pts.shape
    wide = pts.astype(jnp.float32)
    total = jnp.sum(wide * wide, axis=1, keepdims=True)
    return jnp.broadcast_to(scale_of(features) * (features - total), (rows, 128))


def norm_row(col, targets):
    return jnp.transpose(col)[0:targets]


def twice(col):
    return jnp.concatenate([col, col], axis=1)


def hits(far, counts, first):
    rows, slots = far.shape
    ids = lax.broadcasted_iota(jnp.int32, (rows, 128), 1) + first
    found = jnp.zeros((rows, 128), jnp.float32)
    for k in range(slots):
        same = (far[:, k : k + 1] == ids) & (counts > k)
        found = jnp.where(same, 1.0, found)
    return found


def count_column(count_ref, rows):
    spot = lax.broadcasted_iota(jnp.int32, (rows, 128), 0)
    column = jnp.zeros((rows, 128), jnp.int32)
    for t in range(rows):
        column = jnp.where(spot == t, count_ref[t], column)
    return column


def one_hot_rows(index_columns, at, choices):
    spots = lax.broadcasted_iota(jnp.int32, (index_columns.shape[0], choices), 1)
    same = index_columns[:, at : at + 1] == spots
    return jnp.where(same, 1.0, 0.0).astype(jnp.bfloat16)


def place(total):
    me = lax.axis_index("leaf")
    core = lax.rem(me, 2)
    chips = total // 2
    chip = me // 2
    step = 2 * core - 1
    side_b = lax.rem(chip + step + chips, chips)
    side_a = lax.rem(chip - step + chips, chips)
    return me, core, chip, side_a, side_b


def outer_first(core, group, groups):
    return group + core * (groups - 1 - 2 * group)


def fetch(pairs, sems):
    copies = [pltpu.make_async_copy(s, d, sems.at[i]) for i, (s, d) in enumerate(pairs)]
    for copy in copies:
        copy.start()
    return copies


def group_rows(at):
    return pl.ds(pl.multiple_of(at * 256, 256), 256)


def fill_rows(rows_ref, at, source, used_columns, targets):
    col = norm_col(source) if source.shape[1] != 128 else source
    for half in range(2):
        term = norm_row(col[half * 128 : half * 128 + 128], targets)
        lanes = slice(half * 128, half * 128 + 128)
        rows_ref[at, :, lanes] = jnp.where(used_columns[half] > 0.0, term, NEG)


def blocks(left, col, right, row_of):
    features = left.shape[1]
    inner = mm_nt(left, right)
    parts = []
    for at in range(left.shape[0] // 128):
        own = slice(at * 128, at * 128 + 128)
        power = inner[own] * (2.0 * scale_of(features)) + twice(col[own]) + row_of(at)
        parts.append(jnp.exp2(power).astype(jnp.bfloat16))
    return jnp.concatenate(parts, axis=0) if len(parts) > 1 else parts[0]


def tree_leaf(core, at):
    return outer_first(core, at // 2, 4) * 2 + at % 2


def front_kernel(
    points_hbm, weights_hbm, basis_hbm, lt_hbm, t_hbm, ls_hbm, ns_hbm, far_hbm, count_hbm, us_hbm,
    pack_ref, rim_ref, mask_ref, us,
    points, weights, basis, lt, t, ls, ns, far, count, sems, *, total,
):
    me, core, _, _, _ = place(total)
    leaves, rows, rank = basis.shape
    nodes = t.shape[0]
    features = points.shape[1]
    cols = weights.shape[1]
    small = [(ls_hbm, ls), (ns_hbm, ns), (far_hbm, far), (count_hbm, count), (us_hbm, us)]
    pairs = list(small)
    ahead = len(pairs)
    part = leaves // 2
    for half in range(2):
        own = pl.ds(half * part * rows, part * rows)
        some = pl.ds(half * part, part)
        pairs += [
            (points_hbm.at[own], points.at[own]),
            (weights_hbm.at[own], weights.at[own]),
            (basis_hbm.at[some], basis.at[some]),
        ]
    pairs += [(lt_hbm, lt), (t_hbm, t)]
    copies = fetch(pairs, sems)
    for copy in copies[: len(small)]:
        copy.wait()
    counts = count_column(count, leaves)
    for at, first in enumerate((me, me + 1 - 2 * core, lax.rem(me + 2 * core - 1 + total, total))):
        found = hits(far[...], counts, first * leaves)
        mask_ref[at * 8 : at * 8 + 8, :] = found
    rim_ref[512:528, :] = jnp.zeros((16, rim_ref.shape[1]), jnp.bfloat16)
    rim_ref[512:528, 0:128] = jnp.concatenate(
        [found, jnp.zeros((8, 128), jnp.float32)], axis=0
    ).astype(jnp.bfloat16)
    leaf_columns = jnp.transpose(ls[...])
    node_columns = jnp.transpose(jnp.concatenate([ns[...]] * 4, axis=0))
    groups = leaves // 2
    picked, charges = [], []
    base = leaves * rank
    for leaf in range(leaves):
        if leaf % part == 0:
            first = ahead + 3 * (leaf // part)
            for copy in copies[first : first + 3]:
                copy.wait()
        own = slice(leaf * rows, (leaf + 1) * rows)
        skel = mm(one_hot_rows(leaf_columns, leaf, rows), points[own, :]).astype(jnp.bfloat16)
        charge = mm_tn(basis[leaf], weights[own, :]).astype(jnp.bfloat16)
        start = outer_first(core, leaf // 2, groups) * 256 + (leaf % 2) * rank
        here = pl.ds(pl.multiple_of(start, 128), rank)
        pack_ref[here, 0:features] = skel
        pack_ref[here, features:] = charge
        picked.append(skel)
        charges.append(charge)
    for copy in copies[ahead + 6 :]:
        copy.wait()
    for node in range(nodes):
        own = slice(base + node * rank, base + (node + 1) * rank)
        kids = jnp.concatenate(picked[node * 4 : node * 4 + 4], axis=0)
        rows_hot = one_hot_rows(node_columns, node, 4 * rank)
        pack_ref[own, 0:features] = mm(rows_hot, kids).astype(jnp.bfloat16)
        transfer = lt[node * 4 : node * 4 + 4].reshape(4 * rank, rank)
        charge = mm_tn(transfer, jnp.concatenate(charges[node * 4 : node * 4 + 4], axis=0))
        pack_ref[own, features:] = charge.astype(jnp.bfloat16)
        last = slice(base + 2 * rank, base + 3 * rank)
        pack_ref[last, node * rank : (node + 1) * rank] = t[node]
    pack_ref[base + 2 * rank :, 2 * rank :] = jnp.zeros((rank, rank), jnp.bfloat16)
    rim_ref[0:512, :] = pack_ref[0:512, :]


def upper_hot(index):
    columns = jnp.transpose(jnp.broadcast_to(index, (8, index.shape[1])))
    return one_hot_rows(columns, 0, 512)


def node_points(ref, start, count):
    stop = start + count
    return jnp.concatenate([ref[start:stop, :], ref[512 + start : 512 + stop, :]], axis=1)


def upper_kernel(own_ref, other_ref, us_ref, out_ref, points_ref, transfers, *, total):
    _, core, chip, _, _ = place(total)
    base = own_ref.shape[0] - 384
    mine = pl.multiple_of(core * 256, 256)
    theirs = pl.multiple_of((1 - core) * 256, 256)
    for start, ref in ((mine, own_ref), (theirs, other_ref)):
        for chunk in range(3):
            lanes = slice(chunk * 128, chunk * 128 + 128)
            out_ref[pl.ds(chunk * 512 + start, 256), :] = ref[base : base + 256, lanes]
        transfers[pl.ds(start, 128), :] = ref[base + 256 : base + 384, 0:128]
        transfers[pl.ds(start + 128, 128), :] = ref[base + 256 : base + 384, 128:256]
    charge = mm_tn(transfers[...], out_ref[1024:1536, :])
    out_ref[1536:1664, :] = charge.astype(jnp.bfloat16)
    hot = upper_hot(us_ref[pl.ds(chip, 1), :])
    points_ref[...] = mm(hot, node_points(out_ref, 0, 512)).astype(jnp.bfloat16)


def near_kernel(
    points, weights, ufar_hbm, nfar_hbm, ncount_hbm, ucount_hbm, out_ref, mask_ref,
    ufar, nfar, ncount, ucount, sems, *, rows, total,
):
    _, _, chip, side_a, side_b = place(total)
    copies = fetch(
        [(ufar_hbm, ufar), (nfar_hbm, nfar), (ncount_hbm, ncount), (ucount_hbm, ucount)], sems
    )
    features = points.shape[1]
    same = lax.broadcasted_iota(jnp.int32, (rows, rows), 0) == lax.broadcasted_iota(
        jnp.int32, (rows, rows), 1
    )
    for leaf in range(points.shape[0] // rows):
        own = slice(leaf * rows, (leaf + 1) * rows)
        pts = points[own, :]
        col = norm_col(pts)
        row = jnp.concatenate([norm_row(col[0:128], 1), norm_row(col[128:256], 1)], axis=1)
        power = mm_nt(pts, pts) * (2.0 * scale_of(features)) + twice(col) + row
        tile = jnp.exp2(jnp.where(same, NEG, power)).astype(jnp.bfloat16)
        out_ref[own, :] = mm(tile, weights[own, :])
    for copy in copies:
        copy.wait()
    ncounts = count_column(ncount, 2)
    for at, ident in enumerate((chip, side_b, side_a)):
        mask_ref[at * 8 : at * 8 + 2, :] = hits(nfar[...], ncounts, ident * 4)
    lists = ufar[...]
    live = ucount[chip]
    mine = lax.broadcasted_iota(jnp.int32, lists.shape, 1) == chip
    mine = mine & (lax.broadcasted_iota(jnp.int32, lists.shape, 0) < live)
    for at, ident in enumerate((side_b, side_a)):
        hit = jnp.where(mine & (lists == ident), 1.0, 0.0)
        used = jnp.max(jnp.max(hit, axis=0, keepdims=True), axis=1, keepdims=True)
        mask_ref[24 + at : 25 + at, :] = jnp.broadcast_to(used, (1, 128))


def own_kernel(pack_ref, mask_ref, pot_ref, col_ref, rows_ref, block_ref, *, total):
    _, core, _, _, _ = place(total)
    features = pack_ref.shape[1] - pot_ref.shape[1]
    found = mask_ref[0:8, :]
    col_ref[...] = norm_col(pack_ref[0:1024, 0:features])
    for tree in range(4):
        here = group_rows(outer_first(core, tree, 4))
        used = [found[:, 2 * tree + h : 2 * tree + h + 1] for h in range(2)]
        fill_rows(rows_ref, tree, col_ref[here, :], used, 8)
    left = pack_ref[0:1024, 0:features]
    for source in range(4):
        src = outer_first(core, source, 4)
        here = slice(source * 256, source * 256 + 256)
        block_ref[:, here] = blocks(
            left, col_ref[...], pack_ref[here, 0:features],
            lambda at: rows_ref[src, pl.ds(tree_leaf(core, at), 1), :],
        )
    pot_ref[...] = mm(block_ref[...], pack_ref[0:1024, features:])


def side_work(core, pack_ref, side_ref, mask_ref, col_ref, start_ref, pot_ref, rows_ref, block_ref):
    features = pack_ref.shape[1] - pot_ref.shape[1]
    found = mask_ref[8:16, :]
    for tree in range(4):
        here = group_rows(outer_first(1 - core, tree, 4))
        used = [found[:, 2 * tree + h : 2 * tree + h + 1] for h in range(2)]
        fill_rows(rows_ref, tree, side_ref[here, 0:features], used, 8)
    for source in range(4):
        src = outer_first(1 - core, source, 4)
        here = slice(source * 256, source * 256 + 256)
        first = 3 - source
        block_ref[first * 256 :, here] = blocks(
            pack_ref[first * 256 : 1024, 0:features], col_ref[first * 256 :, :],
            side_ref[here, 0:features],
            lambda at: rows_ref[src, pl.ds(tree_leaf(core, at + 2 * first), 1), :],
        )
    for group in range(4):
        own = slice(group * 256, group * 256 + 256)
        span = slice((3 - group) * 256, 1024)
        pot_ref[own, :] = start_ref[own, :] + mm(block_ref[own, span], side_ref[span, features:])


def back_kernel(pack_ref, rim_ref, col_ref, ret_ref, rows_ref, *, total):
    _, core, _, _, _ = place(total)
    features = pack_ref.shape[1] - ret_ref.shape[1]
    found = rim_ref[512:528, 0:128].astype(jnp.float32)[0:8, :]
    left = rim_ref[0:512, 0:features]
    col = norm_col(left)
    parts = []
    for source in (2, 3):
        used = []
        for half in range(2):
            one = found[:, 2 * source + half : 2 * source + half + 1]
            other = found[:, 2 * (3 - source) + half : 2 * (3 - source) + half + 1]
            used.append(jnp.where(core == 0, one, other))
        here = slice(source * 256, source * 256 + 256)
        fill_rows(rows_ref, source, col_ref[here, :], used, 8)
        rows = 512 if source == 2 else 256
        parts.append(
            blocks(
                left[0:rows], col[0:rows], pack_ref[here, 0:features],
                lambda at: rows_ref[source, pl.ds(tree_leaf(1 - core, at), 1), :],
            )
        )
    both = jnp.concatenate([parts[0][0:256], parts[1]], axis=1)
    ret_ref[0:256, :] = mm(both, pack_ref[512:1024, features:]).astype(jnp.bfloat16)
    ret_ref[256:512, :] = mm(parts[0][256:512], pack_ref[512:768, features:]).astype(jnp.bfloat16)


def rim_work(core, pack_ref, rim_ref, mask_ref, col_ref, start_ref, pot_ref, rows_ref, block_ref):
    features = pack_ref.shape[1] - pot_ref.shape[1]
    found = mask_ref[16:24, :]
    for source in range(2):
        used = []
        for half in range(2):
            zero = found[:, 2 * source + half : 2 * source + half + 1]
            one = found[:, 2 * (3 - source) + half : 2 * (3 - source) + half + 1]
            used.append(jnp.where(core == 0, one, zero))
        here = slice(source * 256, source * 256 + 256)
        fill_rows(rows_ref, source, rim_ref[here, 0:features], used, 8)
        stop = 1024 - source * 256
        block_ref[0:stop, here] = blocks(
            pack_ref[0:stop, 0:features], col_ref[0:stop, :], rim_ref[here, 0:features],
            lambda at: rows_ref[source, pl.ds(tree_leaf(core, at), 1), :],
        )
    pot_ref[0:768, :] = start_ref[0:768, :] + mm(block_ref[0:768, 0:512], rim_ref[0:512, features:])
    pot_ref[768:, :] = start_ref[768:, :] + mm(block_ref[768:, 0:256], rim_ref[0:256, features:])


def early_kernel(
    work, pack_ref, other_ref, mask_ref, col_ref, start_ref, pot_ref, rows_ref, block_ref, *, total
):
    _, core, _, _, _ = place(total)

    @pl.when(core == 1)
    def _():
        work(core, pack_ref, other_ref, mask_ref, col_ref, start_ref, pot_ref, rows_ref, block_ref)

    @pl.when(core == 0)
    def _():
        pot_ref[...] = start_ref[...]


def late_kernel(
    pack_ref, side_ref, rim_ref, mask_ref, col_ref, start_ref, pot_ref, rows_ref, block_ref, *, total
):
    _, core, _, _, _ = place(total)
    rest = (mask_ref, col_ref)

    @pl.when(core == 0)
    def _():
        side_work(core, pack_ref, side_ref, *rest, start_ref, pot_ref, rows_ref, block_ref)
        rim_work(core, pack_ref, rim_ref, *rest, pot_ref, pot_ref, rows_ref, block_ref)

    @pl.when(core == 1)
    def _():
        pot_ref[...] = start_ref[...]


def node_part(own, col, ref, mask):
    parts = []
    for source in range(2):
        pts = node_points(ref, source * 256, 256)
        norms = norm_col(pts)
        rows = []
        for half in range(2):
            j = 2 * source + half
            term = norm_row(norms[half * 128 : half * 128 + 128], 2)
            rows.append(jnp.where(mask[:, j : j + 1] > 0.0, term, NEG))
        row = jnp.concatenate(rows, axis=1)
        parts.append(blocks(own, col, pts, lambda at: row[at : at + 1]))
    return mm(jnp.concatenate(parts, axis=1), ref[1024:1536, :])


def own_nodes(ref, core):
    start = pl.multiple_of(core * 256, 256)
    both = [ref[pl.ds(start, 256), :], ref[pl.ds(start + 512, 256), :]]
    return jnp.concatenate(both, axis=1)


def upper_part(own, col, ref, hot, used):
    source = mm(hot, node_points(ref, 0, 512)).astype(jnp.bfloat16)
    row = jnp.where(used > 0.0, norm_row(norm_col(source), 1), NEG)
    power = mm_nt(own, source) * (2.0 * scale_of(own.shape[1])) + col + row
    return mm(jnp.exp2(power).astype(jnp.bfloat16), ref[1536:1664, :])


def outer_node_kernel(
    nodes_ref, upper_ref, side_b_ref, us_ref, mask_ref, far1_ref, far2_ref, own_ref, col_ref,
    hot_ref, *, total,
):
    _, core, _, side_a, side_b = place(total)
    own = own_nodes(nodes_ref, core)
    col = norm_col(own)
    upper_col = norm_col(upper_ref[...])
    own_ref[...] = own
    col_ref[0:256, :] = col
    col_ref[256:384, :] = upper_col
    hot_ref[...] = upper_hot(us_ref[pl.ds(side_a, 1), :])
    hot = upper_hot(us_ref[pl.ds(side_b, 1), :])
    far2_ref[...] = upper_part(upper_ref[...], upper_col, side_b_ref, hot, mask_ref[24:25, :])
    far1_ref[...] = node_part(own, col, nodes_ref, mask_ref[0:2, :]) + node_part(
        own, col, side_b_ref, mask_ref[8:10, :]
    )


def merge_kernel(pot_ref, ret_ref, out_ref, *, total):
    _, core, _, _, _ = place(total)
    for group in range(4):
        own = slice(group * 256, group * 256 + 256)
        part = pot_ref[own, :]
        if group < 2:
            part = part + ret_ref[own, :].astype(jnp.float32)
        out_ref[group_rows(outer_first(core, group, 4)), :] = part


def final_kernel(
    own_ref, upper_ref, col_ref, hot_ref, side_a_ref, mask_ref, far1_ref, far2_ref, t, lt, pot_ref,
    near_ref, basis, out_hbm, out_ref, sems,
):
    leaves, rows, rank = basis.shape
    far2 = far2_ref[...] + upper_part(
        upper_ref[...], col_ref[256:384, :], side_a_ref, hot_ref[...], mask_ref[25:26, :]
    )
    far1 = far1_ref[...] + node_part(
        own_ref[...], col_ref[0:256, :], side_a_ref, mask_ref[16:18, :]
    )
    down2 = far2.astype(jnp.bfloat16)
    down1 = (far1 + mm(t[...].reshape(2 * rank, rank), down2)).astype(jnp.bfloat16)
    down0 = []
    for node in range(2):
        own = slice(node * 4 * rank, (node + 1) * 4 * rank)
        transfer = lt[node * 4 : node * 4 + 4].reshape(4 * rank, rank)
        lower = pot_ref[own, :] + mm(transfer, down1[node * rank : (node + 1) * rank])
        down0.append(lower.astype(jnp.bfloat16))
    copies = []
    for node in range(2):
        results = []
        for leaf in range(4):
            at = node * 4 + leaf
            lower = down0[node][leaf * rank : (leaf + 1) * rank]
            own = slice(at * rows, (at + 1) * rows)
            results.append((near_ref[own, :] + mm(basis[at], lower)).astype(jnp.bfloat16))
        for leaf in range(4):
            at = node * 4 + leaf
            out_ref[at * rows : (at + 1) * rows, :] = results[leaf]
            if leaf % 2 == 1:
                done = pl.ds((at - 1) * rows, 2 * rows)
                copy = pltpu.make_async_copy(out_ref.at[done], out_hbm.at[done], sems.at[at // 2])
                copy.start()
                copies.append(copy)
    for copy in copies:
        copy.wait()


def call(kernel, outs, args, spaces, scratch=(), us=1.0, name=None, out_space=VMEM, after=(), early=()):
    kinds = {"v": VMEM, "h": HBM, "a": pl.ANY}
    n, skip = len(args), len(after) + len(early)

    def body(*refs):
        kernel(*refs[:n], *refs[n + skip :])

    args = list(args) + list(after) + list(early)
    spaces = spaces + "a" * len(after) + "v" * len(early)
    args = [
        pltpu.with_memory_space_constraint(a, HBM) if k == "h" else a for a, k in zip(args, spaces)
    ]
    return pl.pallas_call(
        body,
        out_shape=outs,
        in_specs=[pl.BlockSpec(memory_space=kinds[k]) for k in spaces],
        out_specs=[pl.BlockSpec(memory_space=out_space)] * len(outs),
        scratch_shapes=list(scratch),
        compiler_params=pltpu.CompilerParams(vmem_limit_bytes=LIMIT),
        cost_estimate=pl.CostEstimate(flops=int(us * 1.15e9), bytes_accessed=0, transcendentals=0),
        name=name,
    )(*args)


def like(array, space=None):
    return (space or VMEM)(array.shape, array.dtype)


def per_device(
    points, weights, leaf_basis, leaf_transfer, node_transfer, leaf_skeleton, node_skeleton,
    upper_skeleton, leaf_far, leaf_count, node_far, node_count, upper_far, upper_count,
):
    leaves, rows, rank = leaf_basis.shape
    features = points.shape[1]
    cols = weights.shape[1]
    total = lax.axis_size("leaf")
    width = features + cols
    bf16, f32 = jnp.bfloat16, jnp.float32
    across = [(d, d ^ 1) for d in range(total)]
    outward = [(d, (d + 1) % total if d % 2 else (d - 1) % total) for d in range(total)]
    shape = jax.ShapeDtypeStruct
    sems = pltpu.SemaphoreType.DMA
    bind = functools.partial
    rows_scratch = pltpu.VMEM((leaves // 2, leaves, 256), f32)
    pot_shape = shape((leaves * rank, cols), f32)

    pack, rim, mask, us_v = call(
        bind(front_kernel, total=total),
        [
            shape((leaves * rank + 3 * rank, width), bf16),
            shape((4 * rank + 16, width), bf16),
            shape((24, 128), f32),
            shape(upper_skeleton.shape, upper_skeleton.dtype),
        ],
        [points, weights, leaf_basis, leaf_transfer, node_transfer, leaf_skeleton, node_skeleton,
         leaf_far, leaf_count, upper_skeleton],
        "hhhhhhhhhh",
        [like(points), like(weights), like(leaf_basis), like(leaf_transfer), like(node_transfer),
         like(leaf_skeleton), like(node_skeleton), like(leaf_far), like(leaf_count, SMEM),
         sems((13,))],
        name="front", us=2.5,
    )
    rim_in = lax.ppermute(rim, "leaf", outward)
    side = lax.ppermute(pack, "leaf", across)
    nodes, upper = call(
        bind(upper_kernel, total=total),
        [shape((13 * rank, cols), bf16), shape((rank, features), bf16)],
        [pack, side, us_v], "vvv",
        [pltpu.VMEM((4 * rank, rank), bf16)],
        name="upper", us=0.3,
    )
    nodes_b = lax.ppermute(nodes, "leaf", outward)
    pot, col = call(
        bind(own_kernel, total=total), [pot_shape, shape((leaves * rank, 128), f32)],
        [pack, mask], "vv", [rows_scratch, pltpu.VMEM((1024, 1024), bf16)],
        name="own", us=1.7, after=[nodes],
    )
    upper_lists = jnp.transpose(upper_far)
    near, node_mask = call(
        bind(near_kernel, rows=rows, total=total),
        [shape((leaves * rows, cols), f32), shape((32, 128), f32)],
        [points, weights, upper_lists, node_far, node_count, upper_count], "vvhhhh",
        [like(upper_lists), like(node_far), like(node_count, SMEM), like(upper_count, SMEM), sems((4,))],
        name="near", us=1.7, after=[col],
    )
    far_scratch = [rows_scratch, pltpu.VMEM((1024, 1024), bf16)]
    (pot,) = call(
        bind(early_kernel, side_work, total=total), [pot_shape], [pack, side, mask, col, pot],
        "vvvvv", far_scratch, name="side", us=1.3, after=[node_mask],
    )
    (ret,) = call(
        bind(back_kernel, total=total), [shape((4 * rank, cols), bf16)], [pack, rim_in, col],
        "vvv", [rows_scratch], name="back", us=1.3, after=[pot],
    )
    ret_in = lax.ppermute(ret, "leaf", outward)
    (pot,) = call(
        bind(early_kernel, rim_work, total=total), [pot_shape], [pack, rim_in, mask, col, pot],
        "vvvvv", far_scratch, name="rim", us=0.1, after=[ret],
        early=[leaf_basis, leaf_transfer, node_transfer],
    )
    nodes_b, pot = lax.optimization_barrier((nodes_b, pot))
    nodes_a = lax.ppermute(nodes_b, "leaf", across)
    (pot,) = call(
        bind(late_kernel, total=total), [pot_shape], [pack, side, rim_in, mask, col, pot],
        "vvvvvv", far_scratch, name="late", us=0.1,
    )
    far1, far2, own_points, node_col, hot = call(
        bind(outer_node_kernel, total=total),
        [
            shape((2 * rank, cols), f32), shape((rank, cols), f32),
            shape((2 * rank, features), bf16), shape((3 * rank, 128), f32),
            shape((rank, 4 * rank), bf16),
        ],
        [nodes, upper, nodes_b, us_v, node_mask], "vvvvv",
        name="outer_node", us=0.1, after=[pot],
    )
    (pot,) = call(
        bind(merge_kernel, total=total), [pot_shape], [pot, ret_in], "vv", name="merge", us=5.0,
        after=[far2],
    )
    (out,) = call(
        final_kernel,
        [shape((leaves * rows, cols), bf16)],
        [own_points, upper, node_col, hot, nodes_a, node_mask, far1, far2, node_transfer,
         leaf_transfer, pot, near, leaf_basis],
        "vvvvvvvvvvvvv",
        [pltpu.VMEM((leaves * rows, cols), bf16), sems((4,))],
        name="final", us=1.9, out_space=HBM,
    )
    return out


def solution(mesh):
    placed = (
        P("leaf", None),
        P("leaf", "cols"),
        P("leaf", None, None),
        P("leaf", None, None),
        P("leaf", None, None),
        P("leaf", None),
        P("leaf", None),
        P(),
        P("leaf", None),
        P("leaf"),
        P("leaf", None),
        P("leaf"),
        P(),
        P(),
    )
    return jax.shard_map(
        per_device, mesh=mesh, in_specs=placed, out_specs=P("leaf", "cols"), check_vma=False
    )
```

```python
import functools
import math

import jax
import jax.numpy as jnp
from jax import lax
from jax.experimental import pallas as pl
from jax.experimental.pallas import tpu as pltpu
from jax.sharding import PartitionSpec as P

NEG = -1e38
VMEM = pltpu.VMEM
SMEM = pltpu.SMEM
HBM = pltpu.HBM
LIMIT = 12 * 1024 * 1024


def mm(a, b):
    return jnp.dot(a, b, preferred_element_type=jnp.float32)


def mm_nt(a, b):
    return lax.dot_general(a, b, (((1,), (1,)), ((), ())), preferred_element_type=jnp.float32)


def mm_tn(a, b):
    return lax.dot_general(a, b, (((0,), (0,)), ((), ())), preferred_element_type=jnp.float32)


def scale_of(features):
    return math.log2(math.e) / math.sqrt(8.0 * features)


def norm_col(pts):
    rows, features = pts.shape
    wide = pts.astype(jnp.float32)
    total = jnp.sum(wide * wide, axis=1, keepdims=True)
    return jnp.broadcast_to(scale_of(features) * (features - total), (rows, 128))


def norm_row(col, targets):
    return jnp.transpose(col)[0:targets]


def twice(col):
    return jnp.concatenate([col, col], axis=1)


def hits(far, counts, first):
    rows, slots = far.shape
    ids = lax.broadcasted_iota(jnp.int32, (rows, 128), 1) + first
    found = jnp.zeros((rows, 128), jnp.float32)
    for k in range(slots):
        same = (far[:, k : k + 1] == ids) & (counts > k)
        found = jnp.where(same, 1.0, found)
    return found


def count_column(count_ref, rows):
    spot = lax.broadcasted_iota(jnp.int32, (rows, 128), 0)
    column = jnp.zeros((rows, 128), jnp.int32)
    for t in range(rows):
        column = jnp.where(spot == t, count_ref[t], column)
    return column


def one_hot_rows(index_columns, at, choices):
    spots = lax.broadcasted_iota(jnp.int32, (index_columns.shape[0], choices), 1)
    same = index_columns[:, at : at + 1] == spots
    return jnp.where(same, 1.0, 0.0).astype(jnp.bfloat16)


def place(total):
    me = lax.axis_index("leaf")
    core = lax.rem(me, 2)
    chips = total // 2
    chip = me // 2
    step = 2 * core - 1
    side_b = lax.rem(chip + step + chips, chips)
    side_a = lax.rem(chip - step + chips, chips)
    return me, core, chip, side_a, side_b


def outer_first(core, group, groups):
    return group + core * (groups - 1 - 2 * group)


def fetch(pairs, sems):
    copies = [pltpu.make_async_copy(s, d, sems.at[i]) for i, (s, d) in enumerate(pairs)]
    for copy in copies:
        copy.start()
    return copies


def group_rows(at):
    return pl.ds(pl.multiple_of(at * 256, 256), 256)


def fill_rows(rows_ref, at, source, used_columns, targets):
    col = norm_col(source) if source.shape[1] != 128 else source
    for half in range(2):
        term = norm_row(col[half * 128 : half * 128 + 128], targets)
        lanes = slice(half * 128, half * 128 + 128)
        rows_ref[at, :, lanes] = jnp.where(used_columns[half] > 0.0, term, NEG)


def blocks(left, col, right, row_of):
    features = left.shape[1]
    inner = mm_nt(left, right)
    parts = []
    for at in range(left.shape[0] // 128):
        own = slice(at * 128, at * 128 + 128)
        power = inner[own] * (2.0 * scale_of(features)) + twice(col[own]) + row_of(at)
        parts.append(jnp.exp2(power).astype(jnp.bfloat16))
    return jnp.concatenate(parts, axis=0) if len(parts) > 1 else parts[0]


def tree_leaf(core, at):
    return outer_first(core, at // 2, 4) * 2 + at % 2


def front_kernel(
    points_hbm, weights_hbm, basis_hbm, lt_hbm, t_hbm, ls_hbm, ns_hbm, far_hbm, count_hbm, us_hbm,
    pack_ref, rim_ref, mask_ref, us,
    points, weights, basis, lt, t, ls, ns, far, count, sems, *, total,
):
    me, core, _, _, _ = place(total)
    leaves, rows, rank = basis.shape
    nodes = t.shape[0]
    features = points.shape[1]
    cols = weights.shape[1]
    small = [(ls_hbm, ls), (ns_hbm, ns), (far_hbm, far), (count_hbm, count), (us_hbm, us)]
    pairs = list(small)
    ahead = len(pairs)
    part = leaves // 2
    for half in range(2):
        own = pl.ds(half * part * rows, part * rows)
        some = pl.ds(half * part, part)
        pairs += [
            (points_hbm.at[own], points.at[own]),
            (weights_hbm.at[own], weights.at[own]),
            (basis_hbm.at[some], basis.at[some]),
        ]
    pairs += [(lt_hbm, lt), (t_hbm, t)]
    copies = fetch(pairs, sems)
    for copy in copies[: len(small)]:
        copy.wait()
    counts = count_column(count, leaves)
    for at, first in enumerate((me, me + 1 - 2 * core, lax.rem(me + 2 * core - 1 + total, total))):
        found = hits(far[...], counts, first * leaves)
        mask_ref[at * 8 : at * 8 + 8, :] = found
    rim_ref[512:528, :] = jnp.zeros((16, rim_ref.shape[1]), jnp.bfloat16)
    rim_ref[512:528, 0:128] = jnp.concatenate(
        [found, jnp.zeros((8, 128), jnp.float32)], axis=0
    ).astype(jnp.bfloat16)
    leaf_columns = jnp.transpose(ls[...])
    node_columns = jnp.transpose(jnp.concatenate([ns[...]] * 4, axis=0))
    groups = leaves // 2
    picked, charges = [], []
    base = leaves * rank
    for leaf in range(leaves):
        if leaf % part == 0:
            first = ahead + 3 * (leaf // part)
            for copy in copies[first : first + 3]:
                copy.wait()
        own = slice(leaf * rows, (leaf + 1) * rows)
        skel = mm(one_hot_rows(leaf_columns, leaf, rows), points[own, :]).astype(jnp.bfloat16)
        charge = mm_tn(basis[leaf], weights[own, :]).astype(jnp.bfloat16)
        start = outer_first(core, leaf // 2, groups) * 256 + (leaf % 2) * rank
        here = pl.ds(pl.multiple_of(start, 128), rank)
        pack_ref[here, 0:features] = skel
        pack_ref[here, features:] = charge
        picked.append(skel)
        charges.append(charge)
    for copy in copies[ahead + 6 :]:
        copy.wait()
    for node in range(nodes):
        own = slice(base + node * rank, base + (node + 1) * rank)
        kids = jnp.concatenate(picked[node * 4 : node * 4 + 4], axis=0)
        rows_hot = one_hot_rows(node_columns, node, 4 * rank)
        pack_ref[own, 0:features] = mm(rows_hot, kids).astype(jnp.bfloat16)
        transfer = lt[node * 4 : node * 4 + 4].reshape(4 * rank, rank)
        charge = mm_tn(transfer, jnp.concatenate(charges[node * 4 : node * 4 + 4], axis=0))
        pack_ref[own, features:] = charge.astype(jnp.bfloat16)
        last = slice(base + 2 * rank, base + 3 * rank)
        pack_ref[last, node * rank : (node + 1) * rank] = t[node]
    pack_ref[base + 2 * rank :, 2 * rank :] = jnp.zeros((rank, rank), jnp.bfloat16)
    rim_ref[0:512, :] = pack_ref[0:512, :]


def upper_hot(index):
    columns = jnp.transpose(jnp.broadcast_to(index, (8, index.shape[1])))
    return one_hot_rows(columns, 0, 512)


def node_points(ref, start, count):
    stop = start + count
    return jnp.concatenate([ref[start:stop, :], ref[512 + start : 512 + stop, :]], axis=1)


def upper_kernel(own_ref, other_ref, us_ref, out_ref, points_ref, transfers, *, total):
    _, core, chip, _, _ = place(total)
    base = own_ref.shape[0] - 384
    mine = pl.multiple_of(core * 256, 256)
    theirs = pl.multiple_of((1 - core) * 256, 256)
    for start, ref in ((mine, own_ref), (theirs, other_ref)):
        for chunk in range(3):
            lanes = slice(chunk * 128, chunk * 128 + 128)
            out_ref[pl.ds(chunk * 512 + start, 256), :] = ref[base : base + 256, lanes]
        transfers[pl.ds(start, 128), :] = ref[base + 256 : base + 384, 0:128]
        transfers[pl.ds(start + 128, 128), :] = ref[base + 256 : base + 384, 128:256]
    charge = mm_tn(transfers[...], out_ref[1024:1536, :])
    out_ref[1536:1664, :] = charge.astype(jnp.bfloat16)
    hot = upper_hot(us_ref[pl.ds(chip, 1), :])
    points_ref[...] = mm(hot, node_points(out_ref, 0, 512)).astype(jnp.bfloat16)


def near_work(points, weights, out_ref, rows):
    features = points.shape[1]
    same = lax.broadcasted_iota(jnp.int32, (rows, rows), 0) == lax.broadcasted_iota(
        jnp.int32, (rows, rows), 1
    )
    for leaf in range(points.shape[0] // rows):
        own = slice(leaf * rows, (leaf + 1) * rows)
        pts = points[own, :]
        col = norm_col(pts)
        row = jnp.concatenate([norm_row(col[0:128], 1), norm_row(col[128:256], 1)], axis=1)
        power = mm_nt(pts, pts) * (2.0 * scale_of(features)) + twice(col) + row
        tile = jnp.exp2(jnp.where(same, NEG, power)).astype(jnp.bfloat16)
        out_ref[own, :] = mm(tile, weights[own, :])


def near_kernel(
    points, weights, ufar_hbm, nfar_hbm, ncount_hbm, ucount_hbm, out_ref, mask_ref,
    ufar, nfar, ncount, ucount, sems, *, rows, total,
):
    _, core, chip, side_a, side_b = place(total)
    copies = fetch(
        [(ufar_hbm, ufar), (nfar_hbm, nfar), (ncount_hbm, ncount), (ucount_hbm, ucount)], sems
    )

    @pl.when(core >= 0)
    def _():
        near_work(points, weights, out_ref, rows)

    for copy in copies:
        copy.wait()
    ncounts = count_column(ncount, 2)
    for at, ident in enumerate((chip, side_b, side_a)):
        mask_ref[at * 8 : at * 8 + 2, :] = hits(nfar[...], ncounts, ident * 4)
    lists = ufar[...]
    live = ucount[chip]
    mine = lax.broadcasted_iota(jnp.int32, lists.shape, 1) == chip
    mine = mine & (lax.broadcasted_iota(jnp.int32, lists.shape, 0) < live)
    for at, ident in enumerate((side_b, side_a)):
        hit = jnp.where(mine & (lists == ident), 1.0, 0.0)
        used = jnp.max(jnp.max(hit, axis=0, keepdims=True), axis=1, keepdims=True)
        mask_ref[24 + at : 25 + at, :] = jnp.broadcast_to(used, (1, 128))


def own_kernel(pack_ref, mask_ref, pot_ref, col_ref, rows_ref, block_ref, *, total):
    _, core, _, _, _ = place(total)
    features = pack_ref.shape[1] - pot_ref.shape[1]
    found = mask_ref[0:8, :]
    col_ref[...] = norm_col(pack_ref[0:1024, 0:features])
    for tree in range(4):
        here = group_rows(outer_first(core, tree, 4))
        used = [found[:, 2 * tree + h : 2 * tree + h + 1] for h in range(2)]
        fill_rows(rows_ref, tree, col_ref[here, :], used, 8)
    left = pack_ref[0:1024, 0:features]
    for source in range(4):
        src = outer_first(core, source, 4)
        here = slice(source * 256, source * 256 + 256)
        block_ref[:, here] = blocks(
            left, col_ref[...], pack_ref[here, 0:features],
            lambda at: rows_ref[src, pl.ds(tree_leaf(core, at), 1), :],
        )
    pot_ref[...] = mm(block_ref[...], pack_ref[0:1024, features:])


def side_work(core, pack_ref, side_ref, mask_ref, col_ref, start_ref, pot_ref, rows_ref, block_ref):
    features = pack_ref.shape[1] - pot_ref.shape[1]
    found = mask_ref[8:16, :]
    for tree in range(4):
        here = group_rows(outer_first(1 - core, tree, 4))
        used = [found[:, 2 * tree + h : 2 * tree + h + 1] for h in range(2)]
        fill_rows(rows_ref, tree, side_ref[here, 0:features], used, 8)
    for source in range(4):
        src = outer_first(1 - core, source, 4)
        here = slice(source * 256, source * 256 + 256)
        first = 3 - source
        block_ref[first * 256 :, here] = blocks(
            pack_ref[first * 256 : 1024, 0:features], col_ref[first * 256 :, :],
            side_ref[here, 0:features],
            lambda at: rows_ref[src, pl.ds(tree_leaf(core, at + 2 * first), 1), :],
        )
    for group in range(4):
        own = slice(group * 256, group * 256 + 256)
        span = slice((3 - group) * 256, 1024)
        pot_ref[own, :] = start_ref[own, :] + mm(block_ref[own, span], side_ref[span, features:])


def back_kernel(pack_ref, rim_ref, col_ref, ret_ref, rows_ref, *, total):
    _, core, _, _, _ = place(total)
    features = pack_ref.shape[1] - ret_ref.shape[1]
    found = rim_ref[512:528, 0:128].astype(jnp.float32)[0:8, :]
    left = rim_ref[0:512, 0:features]
    col = norm_col(left)
    parts = []
    for source in (2, 3):
        used = []
        for half in range(2):
            one = found[:, 2 * source + half : 2 * source + half + 1]
            other = found[:, 2 * (3 - source) + half : 2 * (3 - source) + half + 1]
            used.append(jnp.where(core == 0, one, other))
        here = slice(source * 256, source * 256 + 256)
        fill_rows(rows_ref, source, col_ref[here, :], used, 8)
        rows = 512 if source == 2 else 256
        parts.append(
            blocks(
                left[0:rows], col[0:rows], pack_ref[here, 0:features],
                lambda at: rows_ref[source, pl.ds(tree_leaf(1 - core, at), 1), :],
            )
        )
    both = jnp.concatenate([parts[0][0:256], parts[1]], axis=1)
    ret_ref[0:256, :] = mm(both, pack_ref[512:1024, features:]).astype(jnp.bfloat16)
    ret_ref[256:512, :] = mm(parts[0][256:512], pack_ref[512:768, features:]).astype(jnp.bfloat16)


def rim_work(core, pack_ref, rim_ref, mask_ref, col_ref, start_ref, pot_ref, rows_ref, block_ref):
    features = pack_ref.shape[1] - pot_ref.shape[1]
    found = mask_ref[16:24, :]
    for source in range(2):
        used = []
        for half in range(2):
            zero = found[:, 2 * source + half : 2 * source + half + 1]
            one = found[:, 2 * (3 - source) + half : 2 * (3 - source) + half + 1]
            used.append(jnp.where(core == 0, one, zero))
        here = slice(source * 256, source * 256 + 256)
        fill_rows(rows_ref, source, rim_ref[here, 0:features], used, 8)
        stop = 1024 - source * 256
        block_ref[0:stop, here] = blocks(
            pack_ref[0:stop, 0:features], col_ref[0:stop, :], rim_ref[here, 0:features],
            lambda at: rows_ref[source, pl.ds(tree_leaf(core, at), 1), :],
        )
    pot_ref[0:768, :] = start_ref[0:768, :] + mm(block_ref[0:768, 0:512], rim_ref[0:512, features:])
    pot_ref[768:, :] = start_ref[768:, :] + mm(block_ref[768:, 0:256], rim_ref[0:256, features:])


def early_kernel(
    work, pack_ref, other_ref, mask_ref, col_ref, start_ref, pot_ref, rows_ref, block_ref, *, total
):
    _, core, _, _, _ = place(total)

    @pl.when(core == 1)
    def _():
        work(core, pack_ref, other_ref, mask_ref, col_ref, start_ref, pot_ref, rows_ref, block_ref)

    @pl.when(core == 0)
    def _():
        pot_ref[...] = start_ref[...]


def late_kernel(
    pack_ref, side_ref, rim_ref, mask_ref, col_ref, start_ref, pot_ref, rows_ref, block_ref, *, total
):
    _, core, _, _, _ = place(total)
    rest = (mask_ref, col_ref)

    @pl.when(core == 0)
    def _():
        side_work(core, pack_ref, side_ref, *rest, start_ref, pot_ref, rows_ref, block_ref)
        rim_work(core, pack_ref, rim_ref, *rest, pot_ref, pot_ref, rows_ref, block_ref)

    @pl.when(core == 1)
    def _():
        pot_ref[...] = start_ref[...]


def node_part(own, col, ref, mask):
    parts = []
    for source in range(2):
        pts = node_points(ref, source * 256, 256)
        norms = norm_col(pts)
        rows = []
        for half in range(2):
            j = 2 * source + half
            term = norm_row(norms[half * 128 : half * 128 + 128], 2)
            rows.append(jnp.where(mask[:, j : j + 1] > 0.0, term, NEG))
        row = jnp.concatenate(rows, axis=1)
        parts.append(blocks(own, col, pts, lambda at: row[at : at + 1]))
    return mm(jnp.concatenate(parts, axis=1), ref[1024:1536, :])


def own_nodes(ref, core):
    start = pl.multiple_of(core * 256, 256)
    both = [ref[pl.ds(start, 256), :], ref[pl.ds(start + 512, 256), :]]
    return jnp.concatenate(both, axis=1)


def upper_part(own, col, ref, hot, used):
    source = mm(hot, node_points(ref, 0, 512)).astype(jnp.bfloat16)
    row = jnp.where(used > 0.0, norm_row(norm_col(source), 1), NEG)
    power = mm_nt(own, source) * (2.0 * scale_of(own.shape[1])) + col + row
    return mm(jnp.exp2(power).astype(jnp.bfloat16), ref[1536:1664, :])


def outer_node_kernel(
    nodes_ref, upper_ref, side_b_ref, us_ref, mask_ref, far1_ref, far2_ref, own_ref, col_ref,
    hot_ref, *, total,
):
    _, core, _, side_a, side_b = place(total)
    own = own_nodes(nodes_ref, core)
    col = norm_col(own)
    upper_col = norm_col(upper_ref[...])
    own_ref[...] = own
    col_ref[0:256, :] = col
    col_ref[256:384, :] = upper_col
    hot_ref[...] = upper_hot(us_ref[pl.ds(side_a, 1), :])
    hot = upper_hot(us_ref[pl.ds(side_b, 1), :])
    far2_ref[...] = upper_part(upper_ref[...], upper_col, side_b_ref, hot, mask_ref[24:25, :])
    far1_ref[...] = node_part(own, col, nodes_ref, mask_ref[0:2, :]) + node_part(
        own, col, side_b_ref, mask_ref[8:10, :]
    )


def merge_kernel(pot_ref, ret_ref, out_ref, *, total):
    _, core, _, _, _ = place(total)
    for group in range(4):
        own = slice(group * 256, group * 256 + 256)
        part = pot_ref[own, :]
        if group < 2:
            part = part + ret_ref[own, :].astype(jnp.float32)
        out_ref[group_rows(outer_first(core, group, 4)), :] = part


def final_kernel(
    own_ref, upper_ref, col_ref, hot_ref, side_a_ref, mask_ref, far1_ref, far2_ref, t, lt, pot_ref,
    near_ref, basis, out_hbm, out_ref, sems,
):
    leaves, rows, rank = basis.shape
    far2 = far2_ref[...] + upper_part(
        upper_ref[...], col_ref[256:384, :], side_a_ref, hot_ref[...], mask_ref[25:26, :]
    )
    far1 = far1_ref[...] + node_part(
        own_ref[...], col_ref[0:256, :], side_a_ref, mask_ref[16:18, :]
    )
    down2 = far2.astype(jnp.bfloat16)
    down1 = (far1 + mm(t[...].reshape(2 * rank, rank), down2)).astype(jnp.bfloat16)
    down0 = []
    for node in range(2):
        own = slice(node * 4 * rank, (node + 1) * 4 * rank)
        transfer = lt[node * 4 : node * 4 + 4].reshape(4 * rank, rank)
        lower = pot_ref[own, :] + mm(transfer, down1[node * rank : (node + 1) * rank])
        down0.append(lower.astype(jnp.bfloat16))
    copies = []
    for node in range(2):
        results = []
        for leaf in range(4):
            at = node * 4 + leaf
            lower = down0[node][leaf * rank : (leaf + 1) * rank]
            own = slice(at * rows, (at + 1) * rows)
            results.append((near_ref[own, :] + mm(basis[at], lower)).astype(jnp.bfloat16))
        for leaf in range(4):
            at = node * 4 + leaf
            out_ref[at * rows : (at + 1) * rows, :] = results[leaf]
            if leaf % 2 == 1:
                done = pl.ds((at - 1) * rows, 2 * rows)
                copy = pltpu.make_async_copy(out_ref.at[done], out_hbm.at[done], sems.at[at // 2])
                copy.start()
                copies.append(copy)
    for copy in copies:
        copy.wait()


def call(kernel, outs, args, spaces, scratch=(), us=1.0, name=None, out_space=VMEM, after=(), early=()):
    kinds = {"v": VMEM, "h": HBM, "a": pl.ANY}
    n, skip = len(args), len(after) + len(early)

    def body(*refs):
        kernel(*refs[:n], *refs[n + skip :])

    args = list(args) + list(after) + list(early)
    spaces = spaces + "a" * len(after) + "v" * len(early)
    args = [
        pltpu.with_memory_space_constraint(a, HBM) if k == "h" else a for a, k in zip(args, spaces)
    ]
    return pl.pallas_call(
        body,
        out_shape=outs,
        in_specs=[pl.BlockSpec(memory_space=kinds[k]) for k in spaces],
        out_specs=[pl.BlockSpec(memory_space=out_space)] * len(outs),
        scratch_shapes=list(scratch),
        compiler_params=pltpu.CompilerParams(vmem_limit_bytes=LIMIT),
        cost_estimate=pl.CostEstimate(flops=int(us * 1.15e9), bytes_accessed=0, transcendentals=0),
        name=name,
    )(*args)


def like(array, space=None):
    return (space or VMEM)(array.shape, array.dtype)


def per_device(
    points, weights, leaf_basis, leaf_transfer, node_transfer, leaf_skeleton, node_skeleton,
    upper_skeleton, leaf_far, leaf_count, node_far, node_count, upper_far, upper_count,
):
    leaves, rows, rank = leaf_basis.shape
    features = points.shape[1]
    cols = weights.shape[1]
    total = lax.axis_size("leaf")
    width = features + cols
    bf16, f32 = jnp.bfloat16, jnp.float32
    across = [(d, d ^ 1) for d in range(total)]
    outward = [(d, (d + 1) % total if d % 2 else (d - 1) % total) for d in range(total)]
    shape = jax.ShapeDtypeStruct
    sems = pltpu.SemaphoreType.DMA
    bind = functools.partial
    rows_scratch = pltpu.VMEM((leaves // 2, leaves, 256), f32)
    pot_shape = shape((leaves * rank, cols), f32)

    pack, rim, mask, us_v = call(
        bind(front_kernel, total=total),
        [
            shape((leaves * rank + 3 * rank, width), bf16),
            shape((4 * rank + 16, width), bf16),
            shape((24, 128), f32),
            shape(upper_skeleton.shape, upper_skeleton.dtype),
        ],
        [points, weights, leaf_basis, leaf_transfer, node_transfer, leaf_skeleton, node_skeleton,
         leaf_far, leaf_count, upper_skeleton],
        "hhhhhhhhhh",
        [like(points), like(weights), like(leaf_basis), like(leaf_transfer), like(node_transfer),
         like(leaf_skeleton), like(node_skeleton), like(leaf_far), like(leaf_count, SMEM),
         sems((13,))],
        name="front", us=2.5,
    )
    rim_in = lax.ppermute(rim, "leaf", outward)
    side = lax.ppermute(pack, "leaf", across)
    nodes, upper = call(
        bind(upper_kernel, total=total),
        [shape((13 * rank, cols), bf16), shape((rank, features), bf16)],
        [pack, side, us_v], "vvv",
        [pltpu.VMEM((4 * rank, rank), bf16)],
        name="upper", us=0.3,
    )
    nodes_b = lax.ppermute(nodes, "leaf", outward)
    pot, col = call(
        bind(own_kernel, total=total), [pot_shape, shape((leaves * rank, 128), f32)],
        [pack, mask], "vv", [rows_scratch, pltpu.VMEM((1024, 1024), bf16)],
        name="own", us=1.7, after=[nodes],
    )
    upper_lists = jnp.transpose(upper_far)
    near, node_mask = call(
        bind(near_kernel, rows=rows, total=total),
        [shape((leaves * rows, cols), f32), shape((32, 128), f32)],
        [points, weights, upper_lists, node_far, node_count, upper_count], "vvhhhh",
        [like(upper_lists), like(node_far), like(node_count, SMEM), like(upper_count, SMEM), sems((4,))],
        name="near", us=1.7, after=[col],
    )
    far_scratch = [rows_scratch, pltpu.VMEM((1024, 1024), bf16)]
    (pot,) = call(
        bind(early_kernel, side_work, total=total), [pot_shape], [pack, side, mask, col, pot],
        "vvvvv", far_scratch, name="side", us=1.3, after=[node_mask],
    )
    (ret,) = call(
        bind(back_kernel, total=total), [shape((4 * rank, cols), bf16)], [pack, rim_in, col],
        "vvv", [rows_scratch], name="back", us=1.3, after=[pot],
    )
    ret_in = lax.ppermute(ret, "leaf", outward)
    (pot,) = call(
        bind(early_kernel, rim_work, total=total), [pot_shape], [pack, rim_in, mask, col, pot],
        "vvvvv", far_scratch, name="rim", us=0.1, after=[ret],
        early=[leaf_basis, leaf_transfer, node_transfer],
    )
    nodes_b, pot = lax.optimization_barrier((nodes_b, pot))
    nodes_a = lax.ppermute(nodes_b, "leaf", across)
    (pot,) = call(
        bind(late_kernel, total=total), [pot_shape], [pack, side, rim_in, mask, col, pot],
        "vvvvvv", far_scratch, name="late", us=0.1,
    )
    far1, far2, own_points, node_col, hot = call(
        bind(outer_node_kernel, total=total),
        [
            shape((2 * rank, cols), f32), shape((rank, cols), f32),
            shape((2 * rank, features), bf16), shape((3 * rank, 128), f32),
            shape((rank, 4 * rank), bf16),
        ],
        [nodes, upper, nodes_b, us_v, node_mask], "vvvvv",
        name="outer_node", us=0.1, after=[pot],
    )
    (pot,) = call(
        bind(merge_kernel, total=total), [pot_shape], [pot, ret_in], "vv", name="merge", us=5.0,
        after=[far2],
    )
    (out,) = call(
        final_kernel,
        [shape((leaves * rows, cols), bf16)],
        [own_points, upper, node_col, hot, nodes_a, node_mask, far1, far2, node_transfer,
         leaf_transfer, pot, near, leaf_basis],
        "vvvvvvvvvvvvv",
        [pltpu.VMEM((leaves * rows, cols), bf16), sems((4,))],
        name="final", us=1.9, out_space=HBM,
    )
    return out


def solution(mesh):
    placed = (
        P("leaf", None),
        P("leaf", "cols"),
        P("leaf", None, None),
        P("leaf", None, None),
        P("leaf", None, None),
        P("leaf", None),
        P("leaf", None),
        P(),
        P("leaf", None),
        P("leaf"),
        P("leaf", None),
        P("leaf"),
        P(),
        P(),
    )
    return jax.shard_map(
        per_device, mesh=mesh, in_specs=placed, out_specs=P("leaf", "cols"), check_vma=False
    )
```

```python
import functools
import math

import jax
import jax.numpy as jnp
from jax import lax
from jax.experimental import pallas as pl
from jax.experimental.pallas import tpu as pltpu
from jax.sharding import PartitionSpec as P

NEG = -1e38
VMEM = pltpu.VMEM
SMEM = pltpu.SMEM
HBM = pltpu.HBM
LIMIT = 12 * 1024 * 1024


def mm(a, b):
    return jnp.dot(a, b, preferred_element_type=jnp.float32)


def mm_nt(a, b):
    return lax.dot_general(a, b, (((1,), (1,)), ((), ())), preferred_element_type=jnp.float32)


def mm_tn(a, b):
    return lax.dot_general(a, b, (((0,), (0,)), ((), ())), preferred_element_type=jnp.float32)


def scale_of(features):
    return math.log2(math.e) / math.sqrt(8.0 * features)


def norm_col(pts):
    rows, features = pts.shape
    wide = pts.astype(jnp.float32)
    total = jnp.sum(wide * wide, axis=1, keepdims=True)
    return jnp.broadcast_to(scale_of(features) * (features - total), (rows, 128))


def norm_row(col, targets):
    return jnp.transpose(col)[0:targets]


def twice(col):
    return jnp.concatenate([col, col], axis=1)


def hits(far, counts, first):
    rows, slots = far.shape
    ids = lax.broadcasted_iota(jnp.int32, (rows, 128), 1) + first
    found = jnp.zeros((rows, 128), jnp.float32)
    for k in range(slots):
        same = (far[:, k : k + 1] == ids) & (counts > k)
        found = jnp.where(same, 1.0, found)
    return found


def count_column(count_ref, rows):
    spot = lax.broadcasted_iota(jnp.int32, (rows, 128), 0)
    column = jnp.zeros((rows, 128), jnp.int32)
    for t in range(rows):
        column = jnp.where(spot == t, count_ref[t], column)
    return column


def one_hot_rows(index_columns, at, choices):
    spots = lax.broadcasted_iota(jnp.int32, (index_columns.shape[0], choices), 1)
    same = index_columns[:, at : at + 1] == spots
    return jnp.where(same, 1.0, 0.0).astype(jnp.bfloat16)


def place(total):
    me = lax.axis_index("leaf")
    core = lax.rem(me, 2)
    chips = total // 2
    chip = me // 2
    step = 2 * core - 1
    side_b = lax.rem(chip + step + chips, chips)
    side_a = lax.rem(chip - step + chips, chips)
    return me, core, chip, side_a, side_b


def outer_first(core, group, groups):
    return group + core * (groups - 1 - 2 * group)


def fetch(pairs, sems):
    copies = [pltpu.make_async_copy(s, d, sems.at[i]) for i, (s, d) in enumerate(pairs)]
    for copy in copies:
        copy.start()
    return copies


def group_rows(at):
    return pl.ds(pl.multiple_of(at * 256, 256), 256)


def fill_rows(rows_ref, at, source, used_columns, targets):
    col = norm_col(source) if source.shape[1] != 128 else source
    for half in range(2):
        term = norm_row(col[half * 128 : half * 128 + 128], targets)
        lanes = slice(half * 128, half * 128 + 128)
        rows_ref[at, :, lanes] = jnp.where(used_columns[half] > 0.0, term, NEG)


def blocks(left, col, right, row_of):
    features = left.shape[1]
    inner = mm_nt(left, right)
    parts = []
    for at in range(left.shape[0] // 128):
        own = slice(at * 128, at * 128 + 128)
        power = inner[own] * (2.0 * scale_of(features)) + twice(col[own]) + row_of(at)
        parts.append(jnp.exp2(power).astype(jnp.bfloat16))
    return jnp.concatenate(parts, axis=0) if len(parts) > 1 else parts[0]


def tree_leaf(core, at):
    return outer_first(core, at // 2, 4) * 2 + at % 2


def front_kernel(
    points_hbm, weights_hbm, basis_hbm, lt_hbm, t_hbm, ls_hbm, ns_hbm, far_hbm, count_hbm, us_hbm,
    pack_ref, rim_ref, mask_ref, us,
    points, weights, basis, lt, t, ls, ns, far, count, sems, *, total,
):
    me, core, _, _, _ = place(total)
    leaves, rows, rank = basis.shape
    nodes = t.shape[0]
    features = points.shape[1]
    cols = weights.shape[1]
    small = [(ls_hbm, ls), (ns_hbm, ns), (far_hbm, far), (count_hbm, count), (us_hbm, us)]
    pairs = list(small)
    ahead = len(pairs)
    part = leaves // 2
    for half in range(2):
        own = pl.ds(half * part * rows, part * rows)
        some = pl.ds(half * part, part)
        pairs += [
            (points_hbm.at[own], points.at[own]),
            (weights_hbm.at[own], weights.at[own]),
            (basis_hbm.at[some], basis.at[some]),
        ]
    pairs += [(lt_hbm, lt), (t_hbm, t)]
    copies = fetch(pairs, sems)
    for copy in copies[: len(small)]:
        copy.wait()
    counts = count_column(count, leaves)
    for at, first in enumerate((me, me + 1 - 2 * core, lax.rem(me + 2 * core - 1 + total, total))):
        found = hits(far[...], counts, first * leaves)
        mask_ref[at * 8 : at * 8 + 8, :] = found
    rim_ref[512:528, :] = jnp.zeros((16, rim_ref.shape[1]), jnp.bfloat16)
    rim_ref[512:528, 0:128] = jnp.concatenate(
        [found, jnp.zeros((8, 128), jnp.float32)], axis=0
    ).astype(jnp.bfloat16)
    leaf_columns = jnp.transpose(ls[...])
    node_columns = jnp.transpose(jnp.concatenate([ns[...]] * 4, axis=0))
    groups = leaves // 2
    picked, charges = [], []
    base = leaves * rank
    for leaf in range(leaves):
        if leaf % part == 0:
            first = ahead + 3 * (leaf // part)
            for copy in copies[first : first + 3]:
                copy.wait()
        own = slice(leaf * rows, (leaf + 1) * rows)
        skel = mm(one_hot_rows(leaf_columns, leaf, rows), points[own, :]).astype(jnp.bfloat16)
        charge = mm_tn(basis[leaf], weights[own, :]).astype(jnp.bfloat16)
        start = outer_first(core, leaf // 2, groups) * 256 + (leaf % 2) * rank
        here = pl.ds(pl.multiple_of(start, 128), rank)
        pack_ref[here, 0:features] = skel
        pack_ref[here, features:] = charge
        picked.append(skel)
        charges.append(charge)
    for copy in copies[ahead + 6 :]:
        copy.wait()
    for node in range(nodes):
        own = slice(base + node * rank, base + (node + 1) * rank)
        kids = jnp.concatenate(picked[node * 4 : node * 4 + 4], axis=0)
        rows_hot = one_hot_rows(node_columns, node, 4 * rank)
        pack_ref[own, 0:features] = mm(rows_hot, kids).astype(jnp.bfloat16)
        transfer = lt[node * 4 : node * 4 + 4].reshape(4 * rank, rank)
        charge = mm_tn(transfer, jnp.concatenate(charges[node * 4 : node * 4 + 4], axis=0))
        pack_ref[own, features:] = charge.astype(jnp.bfloat16)
        last = slice(base + 2 * rank, base + 3 * rank)
        pack_ref[last, node * rank : (node + 1) * rank] = t[node]
    pack_ref[base + 2 * rank :, 2 * rank :] = jnp.zeros((rank, rank), jnp.bfloat16)
    rim_ref[0:512, :] = pack_ref[0:512, :]


def upper_hot(index):
    columns = jnp.transpose(jnp.broadcast_to(index, (8, index.shape[1])))
    return one_hot_rows(columns, 0, 512)


def node_points(ref, start, count):
    stop = start + count
    return jnp.concatenate([ref[start:stop, :], ref[512 + start : 512 + stop, :]], axis=1)


def upper_kernel(own_ref, other_ref, us_ref, out_ref, points_ref, transfers, *, total):
    _, core, chip, _, _ = place(total)
    base = own_ref.shape[0] - 384
    mine = pl.multiple_of(core * 256, 256)
    theirs = pl.multiple_of((1 - core) * 256, 256)
    for start, ref in ((mine, own_ref), (theirs, other_ref)):
        for chunk in range(3):
            lanes = slice(chunk * 128, chunk * 128 + 128)
            out_ref[pl.ds(chunk * 512 + start, 256), :] = ref[base : base + 256, lanes]
        transfers[pl.ds(start, 128), :] = ref[base + 256 : base + 384, 0:128]
        transfers[pl.ds(start + 128, 128), :] = ref[base + 256 : base + 384, 128:256]
    charge = mm_tn(transfers[...], out_ref[1024:1536, :])
    out_ref[1536:1664, :] = charge.astype(jnp.bfloat16)
    hot = upper_hot(us_ref[pl.ds(chip, 1), :])
    points_ref[...] = mm(hot, node_points(out_ref, 0, 512)).astype(jnp.bfloat16)


def near_work(points, weights, out_ref, rows):
    features = points.shape[1]
    same = lax.broadcasted_iota(jnp.int32, (rows, rows), 0) == lax.broadcasted_iota(
        jnp.int32, (rows, rows), 1
    )
    for leaf in range(points.shape[0] // rows):
        own = slice(leaf * rows, (leaf + 1) * rows)
        pts = points[own, :]
        col = norm_col(pts)
        row = jnp.concatenate([norm_row(col[0:128], 1), norm_row(col[128:256], 1)], axis=1)
        power = mm_nt(pts, pts) * (2.0 * scale_of(features)) + twice(col) + row
        tile = jnp.exp2(jnp.where(same, NEG, power)).astype(jnp.bfloat16)
        out_ref[own, :] = mm(tile, weights[own, :])


def near_kernel(
    points, weights, ufar_hbm, nfar_hbm, ncount_hbm, ucount_hbm, out_ref, mask_ref,
    ufar, nfar, ncount, ucount, sems, *, rows, total,
):
    _, core, chip, side_a, side_b = place(total)
    copies = fetch(
        [(ufar_hbm, ufar), (nfar_hbm, nfar), (ncount_hbm, ncount), (ucount_hbm, ucount)], sems
    )

    @pl.when(core >= 0)
    def _():
        near_work(points, weights, out_ref, rows)

    for copy in copies:
        copy.wait()
    ncounts = count_column(ncount, 2)
    for at, ident in enumerate((chip, side_b, side_a)):
        mask_ref[at * 8 : at * 8 + 2, :] = hits(nfar[...], ncounts, ident * 4)
    lists = ufar[...]
    live = ucount[chip]
    mine = lax.broadcasted_iota(jnp.int32, lists.shape, 1) == chip
    mine = mine & (lax.broadcasted_iota(jnp.int32, lists.shape, 0) < live)
    for at, ident in enumerate((side_b, side_a)):
        hit = jnp.where(mine & (lists == ident), 1.0, 0.0)
        used = jnp.max(jnp.max(hit, axis=0, keepdims=True), axis=1, keepdims=True)
        mask_ref[24 + at : 25 + at, :] = jnp.broadcast_to(used, (1, 128))


def own_kernel(pack_ref, mask_ref, pot_ref, col_ref, rows_ref, block_ref, *, total):
    _, core, _, _, _ = place(total)
    features = pack_ref.shape[1] - pot_ref.shape[1]
    found = mask_ref[0:8, :]
    col_ref[...] = norm_col(pack_ref[0:1024, 0:features])
    for tree in range(4):
        here = group_rows(outer_first(core, tree, 4))
        used = [found[:, 2 * tree + h : 2 * tree + h + 1] for h in range(2)]
        fill_rows(rows_ref, tree, col_ref[here, :], used, 8)
    left = pack_ref[0:1024, 0:features]
    for source in range(4):
        src = outer_first(core, source, 4)
        here = slice(source * 256, source * 256 + 256)
        block_ref[:, here] = blocks(
            left, col_ref[...], pack_ref[here, 0:features],
            lambda at: rows_ref[src, pl.ds(tree_leaf(core, at), 1), :],
        )
    pot_ref[...] = mm(block_ref[...], pack_ref[0:1024, features:])


def side_work(core, pack_ref, side_ref, mask_ref, col_ref, start_ref, pot_ref, rows_ref, block_ref):
    features = pack_ref.shape[1] - pot_ref.shape[1]
    found = mask_ref[8:16, :]
    for tree in range(4):
        here = group_rows(outer_first(1 - core, tree, 4))
        used = [found[:, 2 * tree + h : 2 * tree + h + 1] for h in range(2)]
        fill_rows(rows_ref, tree, side_ref[here, 0:features], used, 8)
    for source in range(4):
        src = outer_first(1 - core, source, 4)
        here = slice(source * 256, source * 256 + 256)
        first = 3 - source
        block_ref[first * 256 :, here] = blocks(
            pack_ref[first * 256 : 1024, 0:features], col_ref[first * 256 :, :],
            side_ref[here, 0:features],
            lambda at: rows_ref[src, pl.ds(tree_leaf(core, at + 2 * first), 1), :],
        )
    for group in range(4):
        own = slice(group * 256, group * 256 + 256)
        span = slice((3 - group) * 256, 1024)
        pot_ref[own, :] = start_ref[own, :] + mm(block_ref[own, span], side_ref[span, features:])


def back_kernel(pack_ref, rim_ref, col_ref, ret_ref, rows_ref, *, total):
    _, core, _, _, _ = place(total)
    features = pack_ref.shape[1] - ret_ref.shape[1]
    found = rim_ref[512:528, 0:128].astype(jnp.float32)[0:8, :]
    left = rim_ref[0:512, 0:features]
    col = norm_col(left)
    parts = []
    for source in (2, 3):
        used = []
        for half in range(2):
            one = found[:, 2 * source + half : 2 * source + half + 1]
            other = found[:, 2 * (3 - source) + half : 2 * (3 - source) + half + 1]
            used.append(jnp.where(core == 0, one, other))
        here = slice(source * 256, source * 256 + 256)
        fill_rows(rows_ref, source, col_ref[here, :], used, 8)
        rows = 512 if source == 2 else 256
        parts.append(
            blocks(
                left[0:rows], col[0:rows], pack_ref[here, 0:features],
                lambda at: rows_ref[source, pl.ds(tree_leaf(1 - core, at), 1), :],
            )
        )
    both = jnp.concatenate([parts[0][0:256], parts[1]], axis=1)
    ret_ref[0:256, :] = mm(both, pack_ref[512:1024, features:]).astype(jnp.bfloat16)
    ret_ref[256:512, :] = mm(parts[0][256:512], pack_ref[512:768, features:]).astype(jnp.bfloat16)


def rim_work(core, pack_ref, rim_ref, mask_ref, col_ref, start_ref, pot_ref, rows_ref, block_ref):
    features = pack_ref.shape[1] - pot_ref.shape[1]
    found = mask_ref[16:24, :]
    for source in range(2):
        used = []
        for half in range(2):
            zero = found[:, 2 * source + half : 2 * source + half + 1]
            one = found[:, 2 * (3 - source) + half : 2 * (3 - source) + half + 1]
            used.append(jnp.where(core == 0, one, zero))
        here = slice(source * 256, source * 256 + 256)
        fill_rows(rows_ref, source, rim_ref[here, 0:features], used, 8)
        stop = 1024 - source * 256
        block_ref[0:stop, here] = blocks(
            pack_ref[0:stop, 0:features], col_ref[0:stop, :], rim_ref[here, 0:features],
            lambda at: rows_ref[source, pl.ds(tree_leaf(core, at), 1), :],
        )
    pot_ref[0:768, :] = start_ref[0:768, :] + mm(block_ref[0:768, 0:512], rim_ref[0:512, features:])
    pot_ref[768:, :] = start_ref[768:, :] + mm(block_ref[768:, 0:256], rim_ref[0:256, features:])


def early_kernel(
    work, pack_ref, other_ref, mask_ref, col_ref, start_ref, pot_ref, rows_ref, block_ref, *, total
):
    _, core, _, _, _ = place(total)

    @pl.when(core == 1)
    def _():
        work(core, pack_ref, other_ref, mask_ref, col_ref, start_ref, pot_ref, rows_ref, block_ref)

    @pl.when(core == 0)
    def _():
        pot_ref[...] = start_ref[...]


def late_kernel(
    pack_ref, side_ref, rim_ref, mask_ref, col_ref, start_ref, pot_ref, rows_ref, block_ref, *, total
):
    _, core, _, _, _ = place(total)
    rest = (mask_ref, col_ref)

    @pl.when(core == 0)
    def _():
        side_work(core, pack_ref, side_ref, *rest, start_ref, pot_ref, rows_ref, block_ref)
        rim_work(core, pack_ref, rim_ref, *rest, pot_ref, pot_ref, rows_ref, block_ref)

    @pl.when(core == 1)
    def _():
        pot_ref[...] = start_ref[...]


def node_part(own, col, ref, mask):
    parts = []
    for source in range(2):
        pts = node_points(ref, source * 256, 256)
        norms = norm_col(pts)
        rows = []
        for half in range(2):
            j = 2 * source + half
            term = norm_row(norms[half * 128 : half * 128 + 128], 2)
            rows.append(jnp.where(mask[:, j : j + 1] > 0.0, term, NEG))
        row = jnp.concatenate(rows, axis=1)
        parts.append(blocks(own, col, pts, lambda at: row[at : at + 1]))
    return mm(jnp.concatenate(parts, axis=1), ref[1024:1536, :])


def own_nodes(ref, core):
    start = pl.multiple_of(core * 256, 256)
    both = [ref[pl.ds(start, 256), :], ref[pl.ds(start + 512, 256), :]]
    return jnp.concatenate(both, axis=1)


def upper_part(own, col, ref, hot, used):
    source = mm(hot, node_points(ref, 0, 512)).astype(jnp.bfloat16)
    row = jnp.where(used > 0.0, norm_row(norm_col(source), 1), NEG)
    power = mm_nt(own, source) * (2.0 * scale_of(own.shape[1])) + col + row
    return mm(jnp.exp2(power).astype(jnp.bfloat16), ref[1536:1664, :])


def chip_node_kernel(nodes_ref, mask_ref, far1_ref, *, total):
    _, core, _, _, _ = place(total)
    own = own_nodes(nodes_ref, core)
    far1_ref[...] = node_part(own, norm_col(own), nodes_ref, mask_ref[0:2, :])


def outer_node_kernel(
    nodes_ref, upper_ref, side_b_ref, us_ref, mask_ref, start_ref, far1_ref, far2_ref, own_ref, col_ref,
    hot_ref, *, total,
):
    _, core, _, side_a, side_b = place(total)
    own = own_nodes(nodes_ref, core)
    col = norm_col(own)
    upper_col = norm_col(upper_ref[...])
    own_ref[...] = own
    col_ref[0:256, :] = col
    col_ref[256:384, :] = upper_col
    hot_ref[...] = upper_hot(us_ref[pl.ds(side_a, 1), :])
    hot = upper_hot(us_ref[pl.ds(side_b, 1), :])
    far2_ref[...] = upper_part(upper_ref[...], upper_col, side_b_ref, hot, mask_ref[24:25, :])
    far1_ref[...] = start_ref[...] + node_part(
        own, col, side_b_ref, mask_ref[8:10, :]
    )


def merge_kernel(pot_ref, ret_ref, out_ref, *, total):
    _, core, _, _, _ = place(total)
    for group in range(4):
        own = slice(group * 256, group * 256 + 256)
        part = pot_ref[own, :]
        if group < 2:
            part = part + ret_ref[own, :].astype(jnp.float32)
        out_ref[group_rows(outer_first(core, group, 4)), :] = part


def final_kernel(
    own_ref, upper_ref, col_ref, hot_ref, side_a_ref, mask_ref, far1_ref, far2_ref, t, lt, pot_ref,
    near_ref, basis, out_hbm, out_ref, sems,
):
    leaves, rows, rank = basis.shape
    far2 = far2_ref[...] + upper_part(
        upper_ref[...], col_ref[256:384, :], side_a_ref, hot_ref[...], mask_ref[25:26, :]
    )
    far1 = far1_ref[...] + node_part(
        own_ref[...], col_ref[0:256, :], side_a_ref, mask_ref[16:18, :]
    )
    down2 = far2.astype(jnp.bfloat16)
    down1 = (far1 + mm(t[...].reshape(2 * rank, rank), down2)).astype(jnp.bfloat16)
    down0 = []
    for node in range(2):
        own = slice(node * 4 * rank, (node + 1) * 4 * rank)
        transfer = lt[node * 4 : node * 4 + 4].reshape(4 * rank, rank)
        lower = pot_ref[own, :] + mm(transfer, down1[node * rank : (node + 1) * rank])
        down0.append(lower.astype(jnp.bfloat16))
    copies = []
    for node in range(2):
        results = []
        for leaf in range(4):
            at = node * 4 + leaf
            lower = down0[node][leaf * rank : (leaf + 1) * rank]
            own = slice(at * rows, (at + 1) * rows)
            results.append((near_ref[own, :] + mm(basis[at], lower)).astype(jnp.bfloat16))
        for leaf in range(4):
            at = node * 4 + leaf
            out_ref[at * rows : (at + 1) * rows, :] = results[leaf]
            if leaf % 2 == 1:
                done = pl.ds((at - 1) * rows, 2 * rows)
                copy = pltpu.make_async_copy(out_ref.at[done], out_hbm.at[done], sems.at[at // 2])
                copy.start()
                copies.append(copy)
    for copy in copies:
        copy.wait()


def call(kernel, outs, args, spaces, scratch=(), us=1.0, name=None, out_space=VMEM, after=(), early=()):
    kinds = {"v": VMEM, "h": HBM, "a": pl.ANY}
    n, skip = len(args), len(after) + len(early)

    def body(*refs):
        kernel(*refs[:n], *refs[n + skip :])

    args = list(args) + list(after) + list(early)
    spaces = spaces + "a" * len(after) + "v" * len(early)
    args = [
        pltpu.with_memory_space_constraint(a, HBM) if k == "h" else a for a, k in zip(args, spaces)
    ]
    return pl.pallas_call(
        body,
        out_shape=outs,
        in_specs=[pl.BlockSpec(memory_space=kinds[k]) for k in spaces],
        out_specs=[pl.BlockSpec(memory_space=out_space)] * len(outs),
        scratch_shapes=list(scratch),
        compiler_params=pltpu.CompilerParams(vmem_limit_bytes=LIMIT),
        cost_estimate=pl.CostEstimate(flops=int(us * 1.15e9), bytes_accessed=0, transcendentals=0),
        name=name,
    )(*args)


def like(array, space=None):
    return (space or VMEM)(array.shape, array.dtype)


def per_device(
    points, weights, leaf_basis, leaf_transfer, node_transfer, leaf_skeleton, node_skeleton,
    upper_skeleton, leaf_far, leaf_count, node_far, node_count, upper_far, upper_count,
):
    leaves, rows, rank = leaf_basis.shape
    features = points.shape[1]
    cols = weights.shape[1]
    total = lax.axis_size("leaf")
    width = features + cols
    bf16, f32 = jnp.bfloat16, jnp.float32
    across = [(d, d ^ 1) for d in range(total)]
    outward = [(d, (d + 1) % total if d % 2 else (d - 1) % total) for d in range(total)]
    shape = jax.ShapeDtypeStruct
    sems = pltpu.SemaphoreType.DMA
    bind = functools.partial
    rows_scratch = pltpu.VMEM((leaves // 2, leaves, 256), f32)
    pot_shape = shape((leaves * rank, cols), f32)

    pack, rim, mask, us_v = call(
        bind(front_kernel, total=total),
        [
            shape((leaves * rank + 3 * rank, width), bf16),
            shape((4 * rank + 16, width), bf16),
            shape((24, 128), f32),
            shape(upper_skeleton.shape, upper_skeleton.dtype),
        ],
        [points, weights, leaf_basis, leaf_transfer, node_transfer, leaf_skeleton, node_skeleton,
         leaf_far, leaf_count, upper_skeleton],
        "hhhhhhhhhh",
        [like(points), like(weights), like(leaf_basis), like(leaf_transfer), like(node_transfer),
         like(leaf_skeleton), like(node_skeleton), like(leaf_far), like(leaf_count, SMEM),
         sems((13,))],
        name="front", us=2.5,
    )
    rim_in = lax.ppermute(rim, "leaf", outward)
    side = lax.ppermute(pack, "leaf", across)
    nodes, upper = call(
        bind(upper_kernel, total=total),
        [shape((13 * rank, cols), bf16), shape((rank, features), bf16)],
        [pack, side, us_v], "vvv",
        [pltpu.VMEM((4 * rank, rank), bf16)],
        name="upper", us=0.3,
    )
    nodes_b = lax.ppermute(nodes, "leaf", outward)
    pot, col = call(
        bind(own_kernel, total=total), [pot_shape, shape((leaves * rank, 128), f32)],
        [pack, mask], "vv", [rows_scratch, pltpu.VMEM((1024, 1024), bf16)],
        name="own", us=1.7, after=[nodes],
    )
    upper_lists = jnp.transpose(upper_far)
    near, node_mask = call(
        bind(near_kernel, rows=rows, total=total),
        [shape((leaves * rows, cols), f32), shape((32, 128), f32)],
        [points, weights, upper_lists, node_far, node_count, upper_count], "vvhhhh",
        [like(upper_lists), like(node_far), like(node_count, SMEM), like(upper_count, SMEM), sems((4,))],
        name="near", us=1.7, after=[col],
    )
    (far1,) = call(
        bind(chip_node_kernel, total=total), [shape((2 * rank, cols), f32)], [nodes, node_mask],
        "vv", name="chip_node", us=0.5,
    )
    far_scratch = [rows_scratch, pltpu.VMEM((1024, 1024), bf16)]
    (pot,) = call(
        bind(early_kernel, side_work, total=total), [pot_shape], [pack, side, mask, col, pot],
        "vvvvv", far_scratch, name="side", us=1.3, after=[far1],
    )
    (ret,) = call(
        bind(back_kernel, total=total), [shape((4 * rank, cols), bf16)], [pack, rim_in, col],
        "vvv", [rows_scratch], name="back", us=1.3, after=[pot],
    )
    ret_in = lax.ppermute(ret, "leaf", outward)
    (pot,) = call(
        bind(early_kernel, rim_work, total=total), [pot_shape], [pack, rim_in, mask, col, pot],
        "vvvvv", far_scratch, name="rim", us=0.1, after=[ret],
        early=[leaf_basis, leaf_transfer, node_transfer],
    )
    nodes_b, pot = lax.optimization_barrier((nodes_b, pot))
    nodes_a = lax.ppermute(nodes_b, "leaf", across)
    (pot,) = call(
        bind(late_kernel, total=total), [pot_shape], [pack, side, rim_in, mask, col, pot],
        "vvvvvv", far_scratch, name="late", us=0.1,
    )
    far1, far2, own_points, node_col, hot = call(
        bind(outer_node_kernel, total=total),
        [
            shape((2 * rank, cols), f32), shape((rank, cols), f32),
            shape((2 * rank, features), bf16), shape((3 * rank, 128), f32),
            shape((rank, 4 * rank), bf16),
        ],
        [nodes, upper, nodes_b, us_v, node_mask, far1], "vvvvvv",
        name="outer_node", us=0.1, after=[pot],
    )
    (pot,) = call(
        bind(merge_kernel, total=total), [pot_shape], [pot, ret_in], "vv", name="merge", us=5.0,
        after=[far2],
    )
    (out,) = call(
        final_kernel,
        [shape((leaves * rows, cols), bf16)],
        [own_points, upper, node_col, hot, nodes_a, node_mask, far1, far2, node_transfer,
         leaf_transfer, pot, near, leaf_basis],
        "vvvvvvvvvvvvv",
        [pltpu.VMEM((leaves * rows, cols), bf16), sems((4,))],
        name="final", us=1.9, out_space=HBM,
    )
    return out


def solution(mesh):
    placed = (
        P("leaf", None),
        P("leaf", "cols"),
        P("leaf", None, None),
        P("leaf", None, None),
        P("leaf", None, None),
        P("leaf", None),
        P("leaf", None),
        P(),
        P("leaf", None),
        P("leaf"),
        P("leaf", None),
        P("leaf"),
        P(),
        P(),
    )
    return jax.shard_map(
        per_device, mesh=mesh, in_specs=placed, out_specs=P("leaf", "cols"), check_vma=False
    )
```
